256 devices in a mesh: img: 128 (over y, z, x_lo, core), band: 2 (over x_hi).
Axes of the slice: x: 4 (x_hi: 2, x_lo: 2; x = x_hi * 2 + x_lo), y: 4, z: 8, core: 2. Of those that a mesh axis runs over, the one named last changes fastest.
Arguments:
- latents: bfloat16 [512, 256, 384], P('img', 'band'), may hold values from -6 to 6
- pos_row: int32 [512, 256], P('img', 'band'), may hold values from 0 to 15, as said below
- pos_col: int32 [512, 256], P('img', 'band'), may hold values from 0 to 15, as said below
- timesteps: int32 [512], P('img'), may hold values from 0 to 999
- labels: int32 [512], P('img'), may hold values from 0 to 1000
- t_w1: bfloat16 [256, 384], replicated, may hold values from -0.375 to 0.375
- t_w2: bfloat16 [384, 384], replicated, may hold values from -0.3125 to 0.3125
- label_table: bfloat16 [1001, 384], replicated, may hold values from -6 to 6
- mod_w: bfloat16 [384, 2304], replicated, may hold values from -0.3125 to 0.3125
- qkv_w: bfloat16 [384, 1152], replicated, may hold values from -0.3125 to 0.3125
- q_gain: float32 [64], replicated, may hold values from 0.5 to 1.5
- k_gain: float32 [64], replicated, may hold values from 0.5 to 1.5
- proj_w: bfloat16 [384, 384], replicated, may hold values from -1.25 to 1.25
- gate_up_w: bfloat16 [384, 2048], replicated, may hold values from -0.3125 to 0.3125
- down_w: bfloat16 [1024, 384], replicated, may hold values from -0.1875 to 0.1875
- out_grad: bfloat16 [512, 256, 384], P('img', 'band'), may hold values from -6 to 6
Outputs:
- block_out: bfloat16 [512, 256, 384], P('img', 'band')
- latents_grad: float32 [512, 256, 384], P('img', 'band')
- t_w1_grad: float32 [256, 384], replicated
- t_w2_grad: float32 [384, 384], replicated
- label_table_grad: float32 [1001, 384], replicated
- mod_w_grad: float32 [384, 2304], replicated
- qkv_w_grad: float32 [384, 1152], replicated
- q_gain_grad: float32 [64], replicated
- k_gain_grad: float32 [64], replicated
- proj_w_grad: float32 [384, 384], replicated
- gate_up_w_grad: float32 [384, 2048], replicated
- down_w_grad: float32 [1024, 384], replicated
The draws below stay inside these ranges and needn't reach their ends.
Inputs may be any that keep to these rules, and one draw needn't show every extreme that they name: The 256 patches of each image hold the cells of its 16 x 16 grid once each, in an order drawn for each image; pos_row is a cell's row. pos_col is the column of the same cell.
All inputs are finite; a program needn't handle non-finite values.
Results may differ from the reference program's by a relative error of at most 0.014.
Values may be sent and summed in bfloat16 or wider, within the bound.
No kernel may reach another device: no remote copies, remote signals or barrier semaphores. Data moves between devices by JAX's collectives and lax.ppermute only.
A program may use at most 128 MiB of HBM per device.

```python
import math
import jax
import jax.numpy as jnp
from jax import lax

D = 384
HEADS = 6
HD = 64
FF = 1024
CLASSES = 1001
FREQ = 256
GRID = 16
PATCHES = 256
IMAGES = 512


def cell_order(key):
    keys = jax.random.split(jax.random.fold_in(key, 11), IMAGES)
    return jax.vmap(lambda k: jax.random.permutation(k, GRID * GRID))(keys).astype(jnp.int32)


def draw_pos_row(key, part):
    return cell_order(key) // GRID


def draw_pos_col(key, part):
    return cell_order(key) % GRID


def plant(result, key, smallest, largest):
    shape = result.shape
    index_at = [jax.random.randint(jax.random.fold_in(key, axis), (), 0, shape[axis]) for axis in range(len(shape))]
    result = result.at[tuple(index_at)].set(smallest)
    longest = shape.index(max(shape))
    index_at[longest] = (index_at[longest] + 1) % shape[longest]
    return result.at[tuple(index_at)].set(largest)


def block_scale(stream_key, extent, shards, least, high):
    def one(axis_at, parts):
        draws = jax.random.uniform(jax.random.fold_in(jax.random.fold_in(stream_key, 6), axis_at), (parts,), jnp.float32, least / len(shards), high / len(shards))
        return jnp.repeat(jnp.exp(draws), extent[axis_at] // parts).reshape((-1,) + (1,) * (len(extent) - axis_at - 1))

    factor_of = one(*shards[0])
    for cut in shards[1:]:
        factor_of = factor_of * one(*cut)
    return factor_of


def gaussian(stream_key, shape, scale, reach, cuts=(), held_as=jnp.bfloat16):
    factor_of = block_scale(stream_key, shape, cuts, -0.22, 0.18) if cuts else 1.0
    array = jax.random.normal(stream_key, shape, jnp.float32) * scale * factor_of
    return jnp.minimum(jnp.maximum(array, -reach), reach).astype(held_as)


def setup_inputs(seed: int = 0) -> dict:
    key_of = jax.random.split(jax.random.key(seed), 17)
    latents = gaussian(key_of[0], (IMAGES, PATCHES, D), 1.0, 6.0, ((0, 128), (1, 2)))
    pos_row = draw_pos_row(jax.random.fold_in(key_of[16], 71), 0)
    pos_col = draw_pos_col(jax.random.fold_in(key_of[16], 71), 0)
    timesteps = plant(jax.random.randint(key_of[3], (IMAGES,), 0, 1000), jax.random.fold_in(key_of[3], 1), 0, 999).astype(jnp.int32)
    labels = plant(jax.random.randint(key_of[4], (IMAGES,), 0, CLASSES), jax.random.fold_in(key_of[4], 1), 0, CLASSES - 1).astype(jnp.int32)
    t_w1 = gaussian(key_of[5], (FREQ, D), FREQ ** -0.5, 0.375)
    t_w2 = gaussian(key_of[6], (D, D), D ** -0.5, 0.3125)
    label_table = gaussian(key_of[7], (CLASSES, D), 1.0, 6.0)
    mod_w = gaussian(key_of[8], (D, 6 * D), D ** -0.5, 0.3125)
    qkv_w = gaussian(key_of[9], (D, 3 * D), D ** -0.5, 0.3125)
    q_gain = jnp.clip(1.0 + 0.1 * jax.random.normal(key_of[10], (HD,), jnp.float32), 0.5, 1.5)
    k_gain = jnp.clip(1.0 + 0.1 * jax.random.normal(key_of[11], (HD,), jnp.float32), 0.5, 1.5)
    proj_w = gaussian(key_of[12], (D, D), (D // 16) ** -0.5, 1.25)
    gate_up_w = gaussian(key_of[13], (D, 2 * FF), D ** -0.5, 0.3125)
    down_w = gaussian(key_of[14], (FF, D), FF ** -0.5, 0.1875)
    out_grad = gaussian(key_of[15], (IMAGES, PATCHES, D), 1.0, 6.0, ((0, 128), (1, 2)))
    return dict(latents=latents, pos_row=pos_row, pos_col=pos_col, timesteps=timesteps, labels=labels, t_w1=t_w1, t_w2=t_w2, label_table=label_table, mod_w=mod_w, qkv_w=qkv_w, q_gain=q_gain, k_gain=k_gain, proj_w=proj_w, gate_up_w=gate_up_w, down_w=down_w, out_grad=out_grad)


@jax.custom_vjp
def low(v):
    return lax.optimization_barrier(v.astype(jnp.bfloat16)).astype(jnp.float32)

@jax.custom_vjp
def low_back(v):
    return v

def low_keep(v):
    return (low(v), None)

def low_pass(kept, grad):
    return (grad,)

def back_keep(v):
    return (v, None)

def back_low(kept, grad):
    return (low(grad),)
low.defvjp(low_keep, low_pass)
low_back.defvjp(back_keep, back_low)

def rms(v):
    return v * lax.rsqrt(lax.optimization_barrier(jnp.mean(v * v, axis=-1, keepdims=True)) + 1e-06)

def freq_embed(tsteps):
    half = FREQ // 2
    freqs = jnp.exp(-math.log(10000.0) * jnp.arange(half, dtype=jnp.float32) / half)
    angle = tsteps.astype(jnp.float32)[:, None] * freqs[None, :]
    return jnp.concatenate([jnp.cos(angle), jnp.sin(angle)], axis=-1)

def rope_tables(prow, pcol):
    quarter = HD // 4
    rates = 10000.0 ** (-jnp.arange(quarter, dtype=jnp.float32) / quarter)
    angle = jnp.stack([prow.astype(jnp.float32)[..., None] * rates, pcol.astype(jnp.float32)[..., None] * rates], axis=-2)
    return (jnp.cos(angle)[:, :, None, :, None, :], jnp.sin(angle)[:, :, None, :, None, :])

def rope(v, cosine, sine):
    shaped = v.reshape(v.shape[:3] + (2, 2, v.shape[-1] // 4))
    first = shaped[..., 0:1, :]
    second = shaped[..., 1:2, :]
    turned = jnp.concatenate([first * cosine - second * sine, second * cosine + first * sine], axis=-2)
    return turned.reshape(v.shape)

def forward(latents, prow, pcol, tsteps, labs, params):
    high = lax.Precision.HIGHEST
    tw1, tw2, table, modw, qkvw, qgain, kgain, projw, guw, downw = params
    group = latents.shape[0]
    hidden_t = jax.nn.silu(jnp.dot(freq_embed(tsteps), tw1, precision=high))
    cond = jnp.dot(hidden_t, tw2, precision=high) + table[labs]
    mod = jnp.dot(jax.nn.silu(cond), modw, precision=high)
    shift1, scale1, gate1, shift2, scale2, gate2 = [mod[:, None, j * D:(j + 1) * D] for j in range(6)]
    h1 = low(rms(latents) * (1.0 + scale1) + shift1)
    qkv = low_back(jnp.einsum('ipd,de->ipe', h1, qkvw, precision=high))
    cosine, sine = rope_tables(prow, pcol)
    shape4 = (group, PATCHES, HEADS, HD)
    query = low(rope(rms(qkv[..., :D].reshape(shape4)) * qgain, cosine, sine))
    key = low(rope(rms(qkv[..., D:2 * D].reshape(shape4)) * kgain, cosine, sine))
    value = low(qkv[..., 2 * D:].reshape(shape4))
    scores = low_back(jnp.einsum('iphd,iqhd->ihpq', query, key, precision=high) * HD ** (-0.5))
    probs = low(jax.nn.softmax(scores, axis=-1))
    attended = low(low_back(jnp.einsum('ihpq,iqhd->iphd', probs, value, precision=high))).reshape(group, PATCHES, D)
    branch = low_back(jnp.einsum('ipd,de->ipe', attended, projw, precision=high))
    mid = latents + gate1 * branch
    h2 = low(rms(mid) * (1.0 + scale2) + shift2)
    gate_up = low_back(jnp.einsum('ipd,de->ipe', h2, guw, precision=high))
    hid = low(jax.nn.silu(gate_up[..., :FF]) * gate_up[..., FF:])
    mlp = low_back(jnp.einsum('ipf,fd->ipd', hid, downw, precision=high))
    return mid + gate2 * mlp

def reference(latents, pos_row, pos_col, timesteps, labels, t_w1, t_w2, label_table, mod_w, qkv_w, q_gain, k_gain, proj_w, gate_up_w, down_w, out_grad):
    params = tuple((w.astype(jnp.float32) for w in (t_w1, t_w2, label_table, mod_w, qkv_w, q_gain, k_gain, proj_w, gate_up_w, down_w)))
    group = math.gcd(IMAGES, max(1, 4096 // PATCHES))
    count = IMAGES // group

    def split(a):
        return a.reshape((count, group) + a.shape[1:])

    def step(total, items):
        xs, prow, pcol, tsteps, labs, cot = items

        def apply(x_in, p_in):
            return forward(x_in, prow, pcol, tsteps, labs, p_in)
        outs, pull = jax.vjp(apply, xs.astype(jnp.float32), params)
        d_in, d_params = pull(cot.astype(jnp.float32))
        total = jax.tree.map(lambda a, b: a + b, total, d_params)
        return (total, (outs.astype(jnp.bfloat16), d_in))
    zeros = tuple((jnp.zeros_like(p) for p in params))
    items = (split(latents), split(pos_row), split(pos_col), split(timesteps), split(labels), split(out_grad))
    total, (outs, d_in) = lax.scan(step, zeros, items)
    return (outs.reshape(IMAGES, PATCHES, D), d_in.reshape(IMAGES, PATCHES, D), total[0], total[1], total[2], total[3], total[4], total[5], total[6], total[7], total[8], total[9])
```

```python
import itertools
import math

import jax
import jax.numpy as jnp
from jax import lax
from jax.sharding import PartitionSpec as P

AXES = ("img", "band")
SIZES = {"y": 4, "z": 8, "x": 4, "c": 2}
f32 = jnp.float32
bf16 = jnp.bfloat16


def flat(y, z, x, c):
    return ((((y * 8 + z) * 2 + x % 2) * 2 + c) * 2) + x // 2


def groups(axes):
    rest = [a for a in "yzxc" if a not in axes]
    out = []
    for fixed in itertools.product(*[range(SIZES[a]) for a in rest]):
        place = dict(zip(rest, fixed))
        row = []
        for moving in itertools.product(*[range(SIZES[a]) for a in axes]):
            row.append(flat(**{**place, **dict(zip(axes, moving))}))
        out.append(row)
    return out


def exchange(v, axes):
    return lax.all_to_all(v, AXES, 0, 0, tiled=True, axis_index_groups=groups(axes))


def scatter_sum(v, axes):
    return jnp.sum(exchange(v, axes).astype(f32), axis=0).astype(bf16)


def gather(v, axes):
    n = math.prod(SIZES[a] for a in axes)
    return exchange(jnp.broadcast_to(v[None], (n,) + v.shape), axes)


def rms(v):
    return v * lax.rsqrt(jnp.mean(v * v, axis=-1, keepdims=True) + 1e-06)


def freq_embed(tsteps, width):
    half = width // 2
    freqs = jnp.exp(-math.log(10000.0) * jnp.arange(half, dtype=jnp.float32) / half)
    angle = tsteps.astype(jnp.float32)[:, None] * freqs[None, :]
    return jnp.concatenate([jnp.cos(angle), jnp.sin(angle)], axis=-1)


def rope_tables(prow, pcol, head):
    quarter = head // 4
    rates = 10000.0 ** (-jnp.arange(quarter, dtype=jnp.float32) / quarter)
    angle = jnp.stack(
        [prow.astype(jnp.float32)[..., None] * rates, pcol.astype(jnp.float32)[..., None] * rates],
        axis=-2,
    )
    return (jnp.cos(angle)[:, :, None, :, None, :], jnp.sin(angle)[:, :, None, :, None, :])


def rope(v, cosine, sine):
    shaped = v.reshape(v.shape[:3] + (2, 2, v.shape[-1] // 4))
    first = shaped[..., 0:1, :]
    second = shaped[..., 1:2, :]
    turned = jnp.concatenate(
        [first * cosine - second * sine, second * cosine + first * sine], axis=-2
    )
    return turned.reshape(v.shape)


def condition(tw1, tw2, table, modw, tsteps, labs):
    high = lax.Precision.HIGHEST
    hidden_t = jax.nn.silu(jnp.dot(freq_embed(tsteps, tw1.shape[0]), tw1, precision=high))
    onehot = (labs[:, None] == jnp.arange(table.shape[0], dtype=jnp.int32)[None, :]).astype(
        jnp.float32
    )
    cond = jnp.dot(hidden_t, tw2, precision=high) + jnp.dot(onehot, table, precision=high)
    return jnp.dot(jax.nn.silu(cond), modw, precision=high)


def modulate(v, shift, scale):
    return rms(v) * (1.0 + scale) + shift


def swiglu(gate_part, up_part):
    return jax.nn.silu(gate_part) * up_part


def block(base, prow, pcol, mod, qkv_w, q_gain, k_gain, proj_w, gate_up_w, down_w, cotan):
    images, rows, width = base.shape
    head = q_gain.shape[0]
    heads = width // head
    hidden_units = down_w.shape[0]
    scale = head ** (-0.5)
    shift1, scale1, gate1, shift2, scale2, gate2 = [
        mod[:, None, j * width : (j + 1) * width] for j in range(6)
    ]
    h1_full, h1_pull = jax.vjp(modulate, base, shift1, scale1)
    h1 = h1_full.astype(bf16)
    qkv = jnp.einsum("ipd,de->ipe", h1, qkv_w, preferred_element_type=f32)
    cosine, sine = rope_tables(prow, pcol, head)
    shape4 = (images, rows, heads, head)

    def qk_post(q_raw, k_raw, q_g, k_g):
        return (rope(rms(q_raw) * q_g, cosine, sine), rope(rms(k_raw) * k_g, cosine, sine))

    (query_f, key_f), qk_pull = jax.vjp(
        qk_post,
        qkv[..., :width].reshape(shape4),
        qkv[..., width : 2 * width].reshape(shape4),
        q_gain,
        k_gain,
    )
    query = query_f.astype(bf16)
    key = key_f.astype(bf16)
    value = qkv[..., 2 * width :].astype(bf16).reshape(shape4)
    scores = jnp.einsum("iphd,iqhd->ihpq", query, key, preferred_element_type=f32) * scale
    top = jnp.max(scores, axis=-1, keepdims=True)
    lse = top + jnp.log(jnp.sum(jnp.exp(scores - top), axis=-1, keepdims=True))
    soft = jnp.exp(scores - lse)
    attended = (
        jnp.einsum("ihpq,iqhd->iphd", soft.astype(bf16), value, preferred_element_type=f32)
        .astype(bf16)
        .reshape(images, rows, width)
    )
    branch = jnp.einsum("ipd,de->ipe", attended, proj_w, preferred_element_type=f32)
    mid = base + gate1 * branch
    h2_full, h2_pull = jax.vjp(modulate, mid, shift2, scale2)
    h2 = h2_full.astype(bf16)
    gate_up = jnp.einsum("ipd,de->ipe", h2, gate_up_w, preferred_element_type=f32)
    hid_full, hid_pull = jax.vjp(swiglu, gate_up[..., :hidden_units], gate_up[..., hidden_units:])
    hid = hid_full.astype(bf16)
    mlp = jnp.einsum("ipf,fd->ipd", hid, down_w, preferred_element_type=f32)
    block_out = (mid + gate2 * mlp).astype(bf16)
    d_gate2 = jnp.sum(cotan * mlp, axis=1, keepdims=True)
    d_mlp = (gate2 * cotan).astype(bf16)
    down_grad = jnp.einsum("ipf,ipd->fd", hid, d_mlp, preferred_element_type=f32)
    d_hid = jnp.einsum("ipd,fd->ipf", d_mlp, down_w, preferred_element_type=f32)
    d_gate_part, d_up_part = hid_pull(d_hid)
    d_gate_up = jnp.concatenate([d_gate_part, d_up_part], axis=-1).astype(bf16)
    gate_up_grad = jnp.einsum("ipd,ipe->de", h2, d_gate_up, preferred_element_type=f32)
    d_h2 = jnp.einsum("ipe,de->ipd", d_gate_up, gate_up_w, preferred_element_type=f32)
    d_mid_norm, d_shift2, d_scale2 = h2_pull(d_h2)
    d_mid = cotan + d_mid_norm
    d_gate1 = jnp.sum(d_mid * branch, axis=1, keepdims=True)
    d_branch = (gate1 * d_mid).astype(bf16)
    proj_grad = jnp.einsum("ipd,ipe->de", attended, d_branch, preferred_element_type=f32)
    d_att = (
        jnp.einsum("ipe,de->ipd", d_branch, proj_w, preferred_element_type=f32)
        .astype(bf16)
        .reshape(shape4)
    )
    d_probs = jnp.einsum("iphd,iqhd->ihpq", d_att, value, preferred_element_type=f32)
    delta = jnp.sum(soft * d_probs, axis=-1, keepdims=True)
    d_scores = (soft * (d_probs - delta)).astype(bf16)
    d_query = jnp.einsum("ihpq,iqhd->iphd", d_scores, key, preferred_element_type=f32) * scale
    d_key = jnp.einsum("ihpq,iphd->iqhd", d_scores, query, preferred_element_type=f32) * scale
    d_value = jnp.einsum("ihpq,iphd->iqhd", soft.astype(bf16), d_att, preferred_element_type=f32)
    d_q_raw, d_k_raw, q_gain_grad, k_gain_grad = qk_pull((d_query, d_key))
    d_qkv = jnp.concatenate(
        [a.reshape(images, rows, width) for a in (d_q_raw, d_k_raw, d_value)], axis=-1
    ).astype(bf16)
    qkv_grad = jnp.einsum("ipd,ipe->de", h1, d_qkv, preferred_element_type=f32)
    d_h1 = jnp.einsum("ipe,de->ipd", d_qkv, qkv_w, preferred_element_type=f32)
    d_base, d_shift1, d_scale1 = h1_pull(d_h1)
    latents_grad = d_mid + d_base
    d_mod = jnp.concatenate([d_shift1, d_scale1, d_gate1, d_shift2, d_scale2, d_gate2], axis=-1)[
        :, 0, :
    ]
    return (
        block_out,
        latents_grad,
        d_mod,
        qkv_grad,
        q_gain_grad,
        k_gain_grad,
        proj_grad,
        gate_up_grad,
        down_grad,
    )


def to_rows(w):
    r, c = w.shape
    return w.reshape(r, c // 128, 128).transpose(1, 0, 2).reshape(-1, 128).astype(bf16)


def from_rows(v, r, c):
    return v.reshape(c // 128, r, 128).transpose(1, 0, 2).reshape(r, c).astype(f32)


PAIR = [(i * 2 + b, i * 2 + 1 - b) for i in range(128) for b in range(2)]


def swap(v):
    return lax.ppermute(v, AXES, PAIR)


def body(
    latents,
    pos_row,
    pos_col,
    timesteps,
    labels,
    t_w1,
    t_w2,
    label_table,
    mod_w,
    qkv_w,
    q_gain,
    k_gain,
    proj_w,
    gate_up_w,
    down_w,
    out_grad,
):
    width = latents.shape[-1]
    band = lax.axis_index("band")
    mine = 2 * band
    other = 2 - mine

    def whole(v):
        kept = lax.dynamic_slice_in_dim(v, mine, 2, 0)
        return jnp.concatenate([kept, swap(lax.dynamic_slice_in_dim(v, other, 2, 0))], axis=1)

    def back(v, kept_type):
        half = v.shape[1] // 2
        got = swap(v[:, half:].astype(bf16)).astype(kept_type)
        out = jnp.zeros((4, half, width), kept_type)
        out = lax.dynamic_update_slice_in_dim(out, v[:, :half], mine, 0)
        return lax.dynamic_update_slice_in_dim(out, got, other, 0)

    base = whole(latents).astype(f32)
    pos = whole(jnp.stack([pos_row, pos_col], axis=-1))
    cotan = whole(out_grad).astype(f32)
    tsteps = lax.dynamic_slice_in_dim(timesteps, mine, 2, 0)
    labs = lax.dynamic_slice_in_dim(labels, mine, 2, 0)
    weights = tuple(w.astype(f32) for w in (t_w1, t_w2, label_table, mod_w))
    mod = condition(*weights, tsteps, labs)
    (
        block_out,
        latents_grad,
        d_mod,
        qkv_grad,
        q_gain_grad,
        k_gain_grad,
        proj_grad,
        gate_up_grad,
        down_grad,
    ) = block(
        base, pos[..., 0], pos[..., 1], mod, qkv_w, q_gain, k_gain, proj_w, gate_up_w, down_w, cotan
    )
    gains = jnp.concatenate([q_gain_grad, k_gain_grad])[None].astype(bf16)
    parts = [to_rows(qkv_grad), to_rows(proj_grad), to_rows(gate_up_grad), to_rows(down_grad), gains]
    used = sum(p.shape[0] for p in parts)
    total = 14336
    parts.append(jnp.zeros((total - used, 128), bf16))
    grads = jnp.concatenate(parts)
    grads = scatter_sum(grads.reshape(2, total // 2, 128), "c")
    grads = scatter_sum(grads.reshape(16, total // 32, 128), "xy")
    grads = scatter_sum(grads.reshape(8, total // 256, 128), "z")
    codes = jnp.concatenate([tsteps // 32, tsteps % 32, labs // 32, labs % 32]).astype(bf16)
    codes = jnp.pad(codes[None], ((0, 3), (0, 120)))
    packed = jnp.concatenate([grads, d_mod.astype(bf16).reshape(36, 128), codes])
    packed = gather(packed, "z")
    packed = gather(packed, "xy")
    packed = gather(packed, "c").reshape(256, 96, 128)
    summed = packed[:, :56].reshape(total, 128)
    d_mod_all = packed[:, 56:92].reshape(512, 6 * width).astype(f32)
    codes = packed[:, 92, :8].astype(jnp.int32).reshape(256, 4, 2)
    tsteps_all = (codes[:, 0] * 32 + codes[:, 1]).reshape(512)
    labs_all = (codes[:, 2] * 32 + codes[:, 3]).reshape(512)
    _, cond_pull = jax.vjp(
        lambda a, b, c, d: condition(a, b, c, d, tsteps_all, labs_all), *weights
    )
    tw1_grad, tw2_grad, table_grad, modw_grad = cond_pull(d_mod_all)
    at = 0
    sums = []
    for w in (qkv_w, proj_w, gate_up_w, down_w):
        n = w.size // 128
        sums.append(from_rows(summed[at : at + n], *w.shape))
        at += n
    qkv_sum, proj_sum, gu_sum, down_sum = sums
    gain_sum = summed[at].astype(f32)
    return (
        back(block_out, bf16),
        back(latents_grad, f32),
        tw1_grad,
        tw2_grad,
        table_grad,
        modw_grad,
        qkv_sum,
        gain_sum[:64],
        gain_sum[64:],
        proj_sum,
        gu_sum,
        down_sum,
    )


def solution(mesh):
    split = P("img", "band", None)
    return jax.shard_map(
        body,
        mesh=mesh,
        in_specs=(split, P("img", "band"), P("img", "band"), P("img"), P("img"))
        + (P(),) * 10
        + (split,),
        out_specs=(split, split) + (P(),) * 10,
        check_vma=False,
    )
```

```python
import itertools
import math

import jax
import jax.numpy as jnp
from jax import lax
from jax.experimental import pallas as pl
from jax.experimental.pallas import tpu as pltpu
from jax.sharding import PartitionSpec as P

AXES = ("img", "band")
SIZES = {"y": 4, "z": 8, "x": 4, "c": 2}
f32 = jnp.float32
bf16 = jnp.bfloat16
EPS = 1e-06
MIB = 1024 * 1024


def dot(a, b):
    return jnp.dot(a, b, preferred_element_type=f32)


def dot_nt(a, b):
    return lax.dot_general(a, b, (((1,), (1,)), ((), ())), preferred_element_type=f32)


def dot_tn(a, b):
    return lax.dot_general(a, b, (((0,), (0,)), ((), ())), preferred_element_type=f32)


def inv_rms(v):
    return lax.rsqrt(jnp.mean(v * v, axis=-1, keepdims=True) + EPS)


def lane_iota(shape):
    return lax.broadcasted_iota(jnp.int32, shape, len(shape) - 1)


def head_mean(v):
    r = lax.broadcasted_iota(jnp.int32, (128, 128), 0) < 64
    c = lax.broadcasted_iota(jnp.int32, (128, 128), 1) < 64
    same = jnp.where(r == c, 1.0 / 64, 0.0).astype(bf16)
    hi = v.astype(bf16)
    lo = (v - hi.astype(f32)).astype(bf16)
    return dot(hi, same) + dot(lo, same)


def partner(v):
    first = (lane_iota((1, 128)) % 32) < 16
    return jnp.where(first, pltpu.roll(v, 112, 1), pltpu.roll(v, 16, 1))


def head_masks():
    low = (lane_iota((1, 128)) < 64).astype(f32)
    return low.astype(bf16), (1.0 - low).astype(bf16)


def both(a_ref, b_ref):
    return jnp.concatenate([a_ref[0], b_ref[0]], axis=0).astype(f32)


def pairs(width=384):
    return [slice(j, j + 128) for j in range(0, width, 128)]


def forward_kernel(
    at_ref, kept_ref, got_ref, mod_ref, w_ref, gain_ref, cos_ref, sin_ref, q_ref, k_ref, v_ref, att_ref
):
    x = both(kept_ref, got_ref)
    h1 = (x * inv_rms(x) * (1.0 + mod_ref[0, 1:2]) + mod_ref[0, 0:1]).astype(bf16)
    z = dot(h1, w_ref[...])
    cosine, sine = cos_ref[0], sin_ref[0]
    masks = head_masks()
    for p in pairs():
        turned = []
        for part in range(2):
            zp = z[:, part * 384 + p.start : part * 384 + p.stop]
            n = zp * lax.rsqrt(head_mean(zp * zp) + EPS) * gain_ref[part : part + 1]
            turned.append(n * cosine + partner(n) * sine)
        q = (turned[0].astype(bf16).astype(f32) * 0.125).astype(bf16)
        k = turned[1].astype(bf16)
        v = z[:, 768 + p.start : 768 + p.stop].astype(bf16)
        q_ref[0, :, p], k_ref[0, :, p], v_ref[0, :, p] = q, k, v
        out = None
        for m in masks:
            e = jnp.exp(dot_nt(q * m, k))
            probs = (e * (1.0 / jnp.sum(e, axis=-1, keepdims=True))).astype(bf16)
            part_out = dot(probs, v * m)
            out = part_out if out is None else out + part_out
        att_ref[0, :, p] = out.astype(bf16)


def mlp_kernel(
    at_ref,
    kept_ref,
    got_ref,
    dkept_ref,
    dgot_ref,
    att_ref,
    mod_ref,
    proj_ref,
    wg_ref,
    wu_ref,
    wd_ref,
    keep_ref,
    send_ref,
    out_ref,
    outsend_ref,
    dmid_ref,
    sums_ref,
    branch_s,
    mid_s,
    h2_s,
    h2t_s,
    dmlp_s,
    mlp_s,
    dh2_s,
    units_s,
):
    j = pl.program_id(0)
    images = range(2)

    def rows(i):
        return slice(i * 256, (i + 1) * 256)

    def dy_of(i):
        return jnp.concatenate([dkept_ref[i], dgot_ref[i]], axis=0).astype(f32)

    @pl.when(j == 0)
    def _():
        branch_s[...] = dot(att_ref[...], proj_ref[...])
        for i in images:
            x = jnp.concatenate([kept_ref[i], got_ref[i]], axis=0).astype(f32)
            mid = x + mod_ref[i, 2:3] * branch_s[rows(i)]
            mid_s[rows(i)] = mid
            h2_s[rows(i)] = (mid * inv_rms(mid) * (1.0 + mod_ref[i, 4:5]) + mod_ref[i, 3:4]).astype(
                bf16
            )
            dmlp_s[rows(i)] = (mod_ref[i, 5:6] * dy_of(i)).astype(bf16)
        h2t_s[...] = h2_s[...].T
        mlp_s[...] = jnp.zeros_like(mlp_s)
        dh2_s[...] = jnp.zeros_like(dh2_s)

    h2 = h2_s[...]
    d_mlp = dmlp_s[...]
    g = dot(h2, wg_ref[...])
    u = dot(h2, wu_ref[...])
    d_hid = dot_nt(d_mlp, wd_ref[...])
    sig = 1.0 / (1.0 + jnp.exp(-g))
    act = g * sig
    hid = (act * u).astype(bf16)
    du = (d_hid * act).astype(bf16)
    dg = (d_hid * u * (sig + act * (1.0 - sig))).astype(bf16)
    mlp_s[...] += dot(hid, wd_ref[...])
    dh2_s[...] += dot_nt(dg, wg_ref[...]) + dot_nt(du, wu_ref[...])
    h2t = h2t_s[...]
    for n, d in ((0, dg), (2, du)):
        grad = dot(h2t, d).astype(bf16)
        for b in range(2):
            units_s[(n + b) // 3, pl.ds((n + b) % 3 * 384, 384)] = grad[:, b * 128 : b * 128 + 128]
    down = dot_tn(hid, d_mlp).astype(bf16)
    for b in range(2):
        for c in range(3):
            units_s[1, pl.ds((b + 1) * 384 + c * 128, 128)] = down[
                b * 128 : b * 128 + 128, c * 128 : c * 128 + 128
            ]
    keep_ref[...] = units_s[at_ref[1]]
    send_ref[...] = units_s[1 - at_ref[1]]

    @pl.when(j == 3)
    def _():
        for i in images:
            mid, mlp, dh2, dy = mid_s[rows(i)], mlp_s[rows(i)], dh2_s[rows(i)], dy_of(i)
            out = (mid + mod_ref[i, 5:6] * mlp).astype(bf16)
            out_ref[i] = out[:128]
            outsend_ref[i] = out[128:]
            s = inv_rms(mid)
            n = mid * s
            e2 = dh2 * (1.0 + mod_ref[i, 4:5])
            d_mid = dy + s * (e2 - n * jnp.mean(e2 * n, axis=-1, keepdims=True))
            dmid_ref[rows(i)] = d_mid
            for k, v in enumerate((d_mid * branch_s[rows(i)], dh2, dh2 * n, dy * mlp)):
                total = jnp.sum(v, axis=0, keepdims=True)
                for b, p in enumerate(pairs()):
                    sums_ref[pl.ds(i * 12 + k * 3 + b, 1)] = total[:, p]


def backward_kernel(
    at_ref,
    kept_ref,
    got_ref,
    mod_ref,
    w_ref,
    gain_ref,
    cos_ref,
    sin_ref,
    q_ref,
    k_ref,
    v_ref,
    att_ref,
    dmid_ref,
    proj_ref,
    keep_ref,
    send_ref,
    grad_ref,
    gradsend_ref,
    sums_ref,
    h1_s,
    dqkv_s,
    dbranch_s,
    att_s,
    gain_s,
    units_s,
):
    i = pl.program_id(0)
    here = pl.ds(pl.multiple_of(i * 256, 256), 256)
    x = both(kept_ref, got_ref)
    s1 = inv_rms(x)
    n1 = x * s1
    h1 = (n1 * (1.0 + mod_ref[0, 1:2]) + mod_ref[0, 0:1]).astype(bf16)
    h1_s[here] = h1
    att_s[here] = att_ref[0]
    d_mid = dmid_ref[...]
    d_branch = (mod_ref[0, 2:3] * d_mid).astype(bf16)
    dbranch_s[here] = d_branch
    d_att = dot_nt(d_branch, proj_ref[...]).astype(bf16)
    z = dot(h1, w_ref[:, :768])
    cosine, sine = cos_ref[0], sin_ref[0]
    masks = head_masks()
    gain_sums = [None, None]
    for p in pairs():
        q, k, v, do = q_ref[0, :, p], k_ref[0, :, p], v_ref[0, :, p], d_att[:, p]
        dq = dk = dv = 0.0
        for m in masks:
            qm, km, vm, dom = q * m, k * m, v * m, do * m
            e = jnp.exp(dot_nt(qm, k))
            soft = e * (1.0 / jnp.sum(e, axis=-1, keepdims=True))
            d_probs = dot_nt(dom, v)
            delta = jnp.sum(soft * d_probs, axis=-1, keepdims=True)
            ds = (soft * (d_probs - delta)).astype(bf16)
            dq = dq + dot(ds, km)
            dk = dk + dot_tn(ds, qm)
            dv = dv + dot_tn(soft.astype(bf16), dom)
        for part, d in enumerate((dq * 0.125, dk)):
            zp = z[:, part * 384 + p.start : part * 384 + p.stop]
            r = lax.rsqrt(head_mean(zp * zp) + EPS)
            n = zp * r
            dn = d * cosine - partner(d) * sine
            total = jnp.sum(dn * n, axis=0, keepdims=True)
            gain_sums[part] = total if gain_sums[part] is None else gain_sums[part] + total
            e = dn * gain_ref[part : part + 1]
            dz = r * (e - n * head_mean(e * n))
            dqkv_s[here, part * 384 + p.start : part * 384 + p.stop] = dz.astype(bf16)
        dqkv_s[here, 768 + p.start : 768 + p.stop] = dv.astype(bf16)
    d_h1 = dot_nt(dqkv_s[here], w_ref[...])
    e1 = d_h1 * (1.0 + mod_ref[0, 1:2])
    grad = d_mid + s1 * (e1 - n1 * jnp.mean(e1 * n1, axis=-1, keepdims=True))
    grad_ref[0] = grad[:128]
    gradsend_ref[0] = grad[128:].astype(bf16)
    gains = [g + pltpu.roll(g, 64, 1) for g in gain_sums]
    gains = jnp.where(lane_iota((1, 128)) < 64, gains[0], gains[1])

    def put_sums(at):
        for k, v in enumerate((d_h1, d_h1 * n1)):
            total = jnp.sum(v, axis=0, keepdims=True)
            for b, p in enumerate(pairs()):
                sums_ref[pl.ds(at * 6 + k * 3 + b, 1)] = total[:, p]

    @pl.when(i == 0)
    def _():
        put_sums(0)
        gain_s[...] = jnp.broadcast_to(gains, (8, 128))

    @pl.when(i == 1)
    def _():
        put_sums(1)
        sums_ref[pl.ds(12, 1)] = gain_s[0:1] + gains
        sums_ref[pl.ds(13, 3)] = jnp.zeros((3, 128), f32)
        h1t = h1_s[...].T
        for part in range(3):
            w = dot(h1t, dqkv_s[:, part * 384 : part * 384 + 384]).astype(bf16)
            for b, p in enumerate(pairs()):
                n = part * 3 + b
                units_s[n // 6, pl.ds(n % 6 * 384, 384)] = w[:, p]
        w = dot_tn(att_s[...], dbranch_s[...]).astype(bf16)
        for b, p in enumerate(pairs()):
            units_s[1, pl.ds((3 + b) * 384, 384)] = w[:, p]
        keep_ref[...] = units_s[at_ref[1]]
        send_ref[...] = units_s[1 - at_ref[1]]


def whole_spec(shape):
    return pl.BlockSpec(shape, lambda *_: (0,) * len(shape))


def params(mib):
    return pltpu.CompilerParams(vmem_limit_bytes=mib * MIB)


def shape_of(shape, dtype):
    return jax.ShapeDtypeStruct(shape, dtype)


def image_spec(shape):
    return pl.BlockSpec((1,) + shape, lambda i, at: (i,) + (0,) * len(shape))


KEPT = pl.BlockSpec((1, 128, 384), lambda i, at: (2 * at[0] + i, 0, 0))
KEPT2 = pl.BlockSpec((2, 128, 384), lambda j, at: (at[0], 0, 0))


def cost(flops, nbytes):
    return pl.CostEstimate(flops=flops, bytes_accessed=nbytes, transcendentals=0)


def forward_call(at, latents, got, mod, qkv_w, gains, cosine, sine):
    act = shape_of((2, 256, 384), bf16)
    return pl.pallas_call(
        forward_kernel,
        grid_spec=pltpu.PrefetchScalarGridSpec(
            num_scalar_prefetch=1,
            grid=(2,),
            in_specs=[
                KEPT,
                image_spec((128, 384)),
                image_spec((6, 384)),
                whole_spec((384, 1152)),
                whole_spec((2, 128)),
                image_spec((256, 128)),
                image_spec((256, 128)),
            ],
            out_specs=[image_spec((256, 384))] * 4,
        ),
        out_shape=[act] * 4,
        compiler_params=params(40),
        cost_estimate=cost(3_000_000_000, 4_000_000),
        name="attention_forward",
    )(at, latents, got, mod, qkv_w, gains, cosine, sine)


def mlp_call(at, latents, got, out_grad, dgot, att, mod, proj_w, gate_up_w, down_w):
    return pl.pallas_call(
        mlp_kernel,
        grid_spec=pltpu.PrefetchScalarGridSpec(
            num_scalar_prefetch=1,
            grid=(4,),
            in_specs=[
                KEPT2,
                whole_spec((2, 128, 384)),
                KEPT2,
                whole_spec((2, 128, 384)),
                whole_spec((512, 384)),
                whole_spec((2, 6, 384)),
                whole_spec((384, 384)),
                pl.BlockSpec((384, 256), lambda j, at: (0, j)),
                pl.BlockSpec((384, 256), lambda j, at: (0, j + 4)),
                pl.BlockSpec((256, 384), lambda j, at: (j, 0)),
            ],
            out_specs=[
                pl.BlockSpec((1152, 128), lambda j, at: (j, 0)),
                pl.BlockSpec((1152, 128), lambda j, at: (j, 0)),
                KEPT2,
                whole_spec((2, 128, 384)),
                whole_spec((512, 384)),
                whole_spec((24, 128)),
            ],
            scratch_shapes=[
                pltpu.VMEM((512, 384), f32),
                pltpu.VMEM((512, 384), f32),
                pltpu.VMEM((512, 384), bf16),
                pltpu.VMEM((384, 512), bf16),
                pltpu.VMEM((512, 384), bf16),
                pltpu.VMEM((512, 384), f32),
                pltpu.VMEM((512, 384), f32),
                pltpu.VMEM((2, 1152, 128), bf16),
            ],
        ),
        out_shape=[
            shape_of((4608, 128), bf16),
            shape_of((4608, 128), bf16),
            shape_of((4, 128, 384), bf16),
            shape_of((2, 128, 384), bf16),
            shape_of((512, 384), f32),
            shape_of((24, 128), f32),
        ],
        compiler_params=params(48),
        cost_estimate=cost(6_000_000_000, 8_000_000),
        name="mlp_both_ways",
    )(at, latents, got, out_grad, dgot, att, mod, proj_w, gate_up_w, gate_up_w, down_w)


def backward_call(at, latents, got, mod, qkv_w, gains, cosine, sine, q, k, v, att, d_mid, proj_w):
    return pl.pallas_call(
        backward_kernel,
        grid_spec=pltpu.PrefetchScalarGridSpec(
            num_scalar_prefetch=1,
            grid=(2,),
            in_specs=[
                KEPT,
                image_spec((128, 384)),
                image_spec((6, 384)),
                whole_spec((384, 1152)),
                whole_spec((2, 128)),
                image_spec((256, 128)),
                image_spec((256, 128)),
            ]
            + [image_spec((256, 384))] * 4
            + [pl.BlockSpec((256, 384), lambda i, at: (i, 0)), whole_spec((384, 384))],
            out_specs=[
                whole_spec((2304, 128)),
                whole_spec((2304, 128)),
                KEPT,
                image_spec((128, 384)),
                whole_spec((16, 128)),
            ],
            scratch_shapes=[
                pltpu.VMEM((512, 384), bf16),
                pltpu.VMEM((512, 1152), bf16),
                pltpu.VMEM((512, 384), bf16),
                pltpu.VMEM((512, 384), bf16),
                pltpu.VMEM((8, 128), f32),
                pltpu.VMEM((2, 2304, 128), bf16),
            ],
        ),
        out_shape=[
            shape_of((2304, 128), bf16),
            shape_of((2304, 128), bf16),
            shape_of((4, 128, 384), f32),
            shape_of((2, 128, 384), bf16),
            shape_of((16, 128), f32),
        ],
        compiler_params=params(48),
        cost_estimate=cost(5_000_000_000, 6_000_000),
        name="attention_backward",
    )(at, latents, got, mod, qkv_w, gains, cosine, sine, q, k, v, att, d_mid, proj_w)


def turn_tables(pos):
    lane = jnp.arange(128)
    rates = 10000.0 ** (-(lane % 16).astype(f32) / 16)
    where_row = (lane % 64) < 32
    pos = pos.astype(f32)
    angle = jnp.where(where_row, pos[..., 0:1], pos[..., 1:2]) * rates
    sign = jnp.where(lane % 32 < 16, -1.0, 1.0)
    return jnp.cos(angle), jnp.sin(angle) * sign


def join_kernel(a_ref, a_got_ref, b_ref, b_got_ref, extra_ref, out_ref):
    out_ref[:, :288] = (a_ref[...].astype(f32) + a_got_ref[...].astype(f32)).astype(bf16)
    out_ref[:, 288:432] = (b_ref[...].astype(f32) + b_got_ref[...].astype(f32)).astype(bf16)
    out_ref[:, 432:] = jnp.broadcast_to(extra_ref[...][None], (16, 48, 128))


def join_call(keep1, got1, keep2, got2, extra):
    big, small = (16, 288, 128), (16, 144, 128)
    return pl.pallas_call(
        join_kernel,
        out_shape=shape_of((16, 480, 128), bf16),
        compiler_params=params(32),
        cost_estimate=cost(2_000_000, 6_000_000),
        name="join_messages",
    )(keep1.reshape(big), got1.reshape(big), keep2.reshape(small), got2.reshape(small), extra)


def sum_kernel(a_ref, out_ref, extra_ref):
    total = a_ref[0, :432].astype(f32)
    for n in range(1, 16):
        total = total + a_ref[n, :432].astype(f32)
    out_ref[:432] = total.astype(bf16)
    out_ref[432:] = jnp.zeros((16, 128), bf16)
    extra_ref[...] = a_ref[:, 432:]


def sum_call(a):
    return pl.pallas_call(
        sum_kernel,
        out_shape=[shape_of((448, 128), bf16), shape_of((16, 48, 128), bf16)],
        compiler_params=params(32),
        cost_estimate=cost(2_000_000, 3_000_000),
        name="sum_xy",
    )(a)


def fetch(at_ref, own_ref, got_ref, slots, sems):
    c = at_ref[1]
    copies = [
        pltpu.make_async_copy(own_ref, slots.at[c], sems.at[0]),
        pltpu.make_async_copy(got_ref, slots.at[1 - c], sems.at[1]),
    ]
    for copy in copies:
        copy.start()
    for copy in copies:
        copy.wait()


def condition_kernel(
    at_ref,
    own_ref,
    got_ref,
    tw1_ref,
    tw2_ref,
    modw_ref,
    tw1g_ref,
    tw2g_ref,
    tableg_ref,
    modwg_ref,
    gains_ref,
    slots,
    rows_s,
    dmod_s,
    cond_s,
    emb_s,
    sems,
):
    fetch(at_ref, own_ref, got_ref, slots, sems)
    for h in range(2):
        for n in range(8):
            part = slots[h, pl.ds(n * 768, 768)]
            rows_s[pl.ds(h * 6144 + n * 768, 768)] = part.astype(f32)

    def line(r):
        return rows_s[pl.ds(r, 256, stride=48), :]

    for i in range(2):
        here = slice(i * 256, i * 256 + 256)
        for k in range(6):
            for b in range(3):
                r = 24 + i * 6 + k * 3 + b if k < 2 else i * 12 + (k - 2) * 3 + b
                at = k * 384 + b * 128
                dmod_s[here, at : at + 128] = line(r).astype(bf16)
        for b in range(2):
            emb_s[here, b * 128 : b * 128 + 128] = line(38 + i * 2 + b).astype(bf16)
        for b in range(3):
            cond_s[here, b * 128 : b * 128 + 128] = line(42 + i * 3 + b)
    gains_ref[...] = jnp.sum(line(36), axis=0, keepdims=True)
    codes = line(37)
    labels = jnp.concatenate([codes[:, i : i + 1] * 32.0 + codes[:, i + 2 : i + 3] for i in range(2)])
    cond = cond_s[...]
    sig = 1.0 / (1.0 + jnp.exp(-cond))
    act_t = (cond * sig).astype(bf16).T
    for k in range(6):
        cols = slice(k * 384, k * 384 + 384)
        modwg_ref[:, cols] = dot(act_t, dmod_s[:, cols])
    d_cond = dot_nt(dmod_s[...], modw_ref[...]) * (sig + cond * sig * (1.0 - sig))
    dc = d_cond.astype(bf16)
    labels = labels.astype(jnp.int32)
    for n in range(4):
        hot = jnp.where(lane_iota((512, 256)) + n * 256 == labels, 1.0, 0.0).astype(bf16)
        rows = dot_tn(hot, dc)
        top = min(256, 1001 - n * 256)
        tableg_ref[n * 256 : n * 256 + top] = rows[:top]
    emb = emb_s[...]
    pre = dot(emb, tw1_ref[...])
    sig = 1.0 / (1.0 + jnp.exp(-pre))
    hid = pre * sig
    tw2g_ref[...] = dot_tn(hid.astype(bf16), dc)
    d_pre = (dot_nt(dc, tw2_ref[...]) * (sig + hid * (1.0 - sig))).astype(bf16)
    tw1g_ref[...] = dot_tn(emb, d_pre)


def condition_call(at, own, got, t_w1, t_w2, mod_w):
    anywhere = pl.BlockSpec(memory_space=pl.ANY)
    shapes = [(256, 384), (384, 384), (1001, 384), (384, 2304), (1, 128)]
    return pl.pallas_call(
        condition_kernel,
        grid_spec=pltpu.PrefetchScalarGridSpec(
            num_scalar_prefetch=1,
            grid=(1,),
            in_specs=[anywhere, anywhere]
            + [whole_spec(s) for s in ((256, 384), (384, 384), (384, 2304))],
            out_specs=[whole_spec(s) for s in shapes],
            scratch_shapes=[
                pltpu.VMEM((2, 6144, 128), bf16),
                pltpu.VMEM((12288, 128), f32),
                pltpu.VMEM((512, 2304), bf16),
                pltpu.VMEM((512, 384), f32),
                pltpu.VMEM((512, 256), bf16),
                pltpu.SemaphoreType.DMA((2,)),
            ],
        ),
        out_shape=[shape_of(s, f32) for s in shapes],
        compiler_params=params(56),
        cost_estimate=cost(4_000_000_000, 12_000_000),
        name="condition_gradients",
    )(at, own, got, t_w1, t_w2, mod_w)


def cuts(start, chunk):
    out, at = [], start
    while at < start + 384:
        n = at // chunk
        stop = min((n + 1) * chunk, start + 384)
        out.append((n, at - n * chunk, stop - n * chunk))
        at = stop
    return out


def unpack_kernel(at_ref, own_ref, got_ref, qkv_ref, proj_ref, gu_ref, down_ref, slots, sems):
    t = pl.program_id(0)

    @pl.when(t == 0)
    def _():
        fetch(at_ref, own_ref, got_ref, slots, sems)

    def unit(half, first, u, chunk, base):
        return jnp.concatenate(
            [slots[half, first + n, base + a : base + b] for n, a, b in cuts(u * 384, chunk)]
        ).astype(f32)

    @pl.when(t < 4)
    def _():
        gu_ref[:, :128] = unit(0, 4 * t, 0, 288, 0)
        gu_ref[:, 128:] = unit(0, 4 * t, 1, 288, 0)
        for b, p in enumerate(pairs()):
            block = unit(t // 2, 8 * (t % 2), b, 144, 288)

            @pl.when(t < 3)
            def _():
                qkv_ref[:, p] = block

            @pl.when(t == 3)
            def _():
                proj_ref[:, p] = block

    @pl.when(t >= 4)
    def _():
        gu_ref[:, :128] = unit(0, 4 * (t - 4), 2, 288, 0)
        gu_ref[:, 128:] = unit(1, 4 * (t - 4), 0, 288, 0)

    for odd in range(2):

        @pl.when(t % 2 == odd)
        def _():
            rows = unit(1, 4 * (t // 2), 1 + odd, 288, 0)
            for b, p in enumerate(pairs()):
                down_ref[:, p] = rows[b * 128 : b * 128 + 128]


def unpack_call(at, own, got):
    anywhere = pl.BlockSpec(memory_space=pl.ANY)
    return pl.pallas_call(
        unpack_kernel,
        grid_spec=pltpu.PrefetchScalarGridSpec(
            num_scalar_prefetch=1,
            grid=(8,),
            in_specs=[anywhere, anywhere],
            out_specs=[
                pl.BlockSpec((384, 384), lambda t, at: (0, jnp.minimum(t, 2))),
                whole_spec((384, 384)),
                pl.BlockSpec((384, 256), lambda t, at: (0, t)),
                pl.BlockSpec((128, 384), lambda t, at: (t, 0)),
            ],
            scratch_shapes=[
                pltpu.VMEM((2, 16, 448, 128), bf16),
                pltpu.SemaphoreType.DMA((2,)),
            ],
        ),
        out_shape=[
            shape_of(s, f32) for s in ((384, 1152), (384, 384), (384, 2048), (1024, 384))
        ],
        compiler_params=params(32),
        cost_estimate=cost(2_000_000, 11_000_000),
        name="unpack_sums",
    )(at, own, got)


def flat(y, z, x, c):
    return ((((y * 8 + z) * 2 + x % 2) * 2 + c) * 2) + x // 2


def groups(axes):
    rest = [a for a in "yzxc" if a not in axes]
    out = []
    for fixed in itertools.product(*[range(SIZES[a]) for a in rest]):
        place = dict(zip(rest, fixed))
        row = []
        for moving in itertools.product(*[range(SIZES[a]) for a in axes]):
            row.append(flat(**{**place, **dict(zip(axes, moving))}))
        out.append(row)
    return out


def exchange(v, axes):
    return lax.all_to_all(v, AXES, 0, 0, tiled=True, axis_index_groups=groups(axes))


def gather(v, axes):
    n = math.prod(SIZES[a] for a in axes)
    return exchange(jnp.broadcast_to(v[None], (n,) + v.shape), axes)


BAND_SWAP = [(n, n ^ 1) for n in range(256)]
CORE_SWAP = [(n, n ^ 2) for n in range(256)]


def swap(v):
    return lax.ppermute(v, AXES, BAND_SWAP)


def core_swap(v):
    return lax.ppermute(v, AXES, CORE_SWAP)


def silu(v):
    return v / (1.0 + jnp.exp(-v))


def condition(t_w1, t_w2, label_table, mod_w, tsteps, labs):
    high = lax.Precision.HIGHEST
    freqs = jnp.exp(-math.log(10000.0) * jnp.arange(128, dtype=f32) / 128)
    angle = tsteps.astype(f32)[:, None] * freqs[None, :]
    emb = jnp.concatenate([jnp.cos(angle), jnp.sin(angle)], axis=-1)
    hidden = jax.nn.silu(jnp.dot(emb, t_w1.astype(f32), precision=high))
    hot = (labs[:, None] == jnp.arange(label_table.shape[0], dtype=jnp.int32)[None, :]).astype(f32)
    cond = jnp.dot(hidden, t_w2.astype(f32), precision=high) + jnp.dot(
        hot, label_table.astype(f32), precision=high
    )
    return emb, cond, jnp.dot(jax.nn.silu(cond), mod_w.astype(f32), precision=high)


def body(
    latents,
    pos_row,
    pos_col,
    timesteps,
    labels,
    t_w1,
    t_w2,
    label_table,
    mod_w,
    qkv_w,
    q_gain,
    k_gain,
    proj_w,
    gate_up_w,
    down_w,
    out_grad,
):
    band = lax.axis_index("band")
    core = lax.axis_index("img") % 2
    at = jnp.stack([band, core]).astype(jnp.int32)
    mine = 2 * band
    other = 2 - mine

    def theirs(v):
        return lax.dynamic_slice_in_dim(v, other, 2, 0)

    def ours(v):
        return lax.dynamic_slice_in_dim(v, mine, 2, 0)

    got = swap(theirs(latents))
    pos = jnp.stack([pos_row, pos_col], axis=-1)
    pos = jnp.concatenate([ours(pos), swap(theirs(pos))], axis=1)
    dgot = swap(theirs(out_grad))
    tsteps, labs = ours(timesteps), ours(labels)
    emb, cond, mod = condition(t_w1, t_w2, label_table, mod_w, tsteps, labs)
    mod = mod.reshape(2, 6, 384)
    gains = jnp.stack([jnp.tile(q_gain, 2), jnp.tile(k_gain, 2)])
    cosine, sine = turn_tables(pos)
    q, k, v, att = forward_call(at, latents, got, mod, qkv_w, gains, cosine, sine)
    keep1, send1, block_out, out_send, d_mid, sums1 = mlp_call(
        at, latents, got, out_grad, dgot, att.reshape(512, 384), mod, proj_w, gate_up_w, down_w
    )
    got1 = core_swap(send1)
    keep2, send2, latents_grad, grad_send, sums2 = backward_call(
        at, latents, got, mod, qkv_w, gains, cosine, sine, q, k, v, att, d_mid, proj_w
    )
    codes = jnp.concatenate([labs // 32, labs % 32]).astype(f32)
    codes = jnp.pad(codes[None], ((0, 0), (0, 124)))
    extra = jnp.concatenate(
        [sums1, sums2[:13], codes, emb.reshape(4, 128), cond.reshape(6, 128)]
    ).astype(bf16)
    chunk, extra = sum_call(
        exchange(join_call(keep1, got1, keep2, core_swap(send2), extra), "xy")
    )
    extra = lax.all_gather(
        extra.reshape(768, 128), AXES, axis=0, tiled=True, axis_index_groups=groups("z")
    )
    chunk = jnp.sum(exchange(chunk.reshape(8, 56, 128), "z").astype(f32), axis=0).astype(bf16)
    chunk = gather(chunk, "z").reshape(448, 128)
    chunk, extra = lax.optimization_barrier((chunk, extra))
    summed = gather(chunk, "xy")
    conditioned = condition_call(at, extra, core_swap(extra), t_w1, t_w2, mod_w)
    out_got, grad_got = swap(out_send), swap(grad_send)
    summed, conditioned, out_got, grad_got = lax.optimization_barrier(
        (summed, conditioned, out_got, grad_got)
    )
    tw1_grad, tw2_grad, table_grad, modw_grad, gain_sums = conditioned
    qkv_sum, proj_sum, gu_sum, down_sum = unpack_call(at, summed, core_swap(summed))
    block_out = lax.dynamic_update_slice_in_dim(block_out, out_got, other, 0)
    latents_grad = lax.dynamic_update_slice_in_dim(
        latents_grad, grad_got.astype(f32), other, 0
    )
    return (
        block_out,
        latents_grad,
        tw1_grad,
        tw2_grad,
        table_grad,
        modw_grad,
        qkv_sum,
        gain_sums[0, :64],
        gain_sums[0, 64:],
        proj_sum,
        gu_sum,
        down_sum,
    )


def solution(mesh):
    split = P("img", "band", None)
    return jax.shard_map(
        body,
        mesh=mesh,
        in_specs=(split, P("img", "band"), P("img", "band"), P("img"), P("img"))
        + (P(),) * 10
        + (split,),
        out_specs=(split, split) + (P(),) * 10,
        check_vma=False,
    )
```

```python
import itertools
import math

import jax
import jax.numpy as jnp
from jax import lax
from jax.experimental import pallas as pl
from jax.experimental.pallas import tpu as pltpu
from jax.sharding import PartitionSpec as P
import ml_dtypes
import numpy as np

AXES = ("img", "band")
SIZES = {"y": 4, "z": 8, "x": 4, "c": 2}
f32 = jnp.float32
bf16 = jnp.bfloat16
EPS = 1e-06
MIB = 1024 * 1024


def dot(a, b):
    return jnp.dot(a, b, preferred_element_type=f32)


def dot_nt(a, b):
    return lax.dot_general(a, b, (((1,), (1,)), ((), ())), preferred_element_type=f32)


def dot_tn(a, b):
    return lax.dot_general(a, b, (((0,), (0,)), ((), ())), preferred_element_type=f32)


def inv_rms(v):
    return lax.rsqrt(jnp.mean(v * v, axis=-1, keepdims=True) + EPS)


def lane_iota(shape):
    return lax.broadcasted_iota(jnp.int32, shape, len(shape) - 1)


def head_mean(v):
    r = lax.broadcasted_iota(jnp.int32, (128, 128), 0) < 64
    c = lax.broadcasted_iota(jnp.int32, (128, 128), 1) < 64
    same = jnp.where(r == c, 1.0 / 64, 0.0).astype(bf16)
    hi = v.astype(bf16)
    lo = (v - hi.astype(f32)).astype(bf16)
    return dot(hi, same) + dot(lo, same)


def partner(v):
    first = (lane_iota((1, 128)) % 32) < 16
    return jnp.where(first, pltpu.roll(v, 112, 1), pltpu.roll(v, 16, 1))


def head_masks():
    low = (lane_iota((1, 128)) < 64).astype(f32)
    return low.astype(bf16), (1.0 - low).astype(bf16)


def both(a_ref, b_ref):
    return jnp.concatenate([a_ref[0], b_ref[0, :128]], axis=0).astype(f32)


def turns(at_ref, image, row_ref, col_ref, got, table_ref):
    here = pl.ds(2 * at_ref[0] + image, 1)
    hot = []
    for n, ref in enumerate((row_ref, col_ref)):
        kept = ref[here, :].astype(f32)
        pos = jnp.concatenate([kept, got[0:1, n * 128 : n * 128 + 128].astype(f32)], axis=1)
        spots = lax.broadcasted_iota(jnp.int32, (16, 256), 0).astype(f32)
        hot.append(jnp.where(spots == pos, 1.0, 0.0))
    hot = jnp.concatenate(hot, axis=0).astype(bf16)
    return [dot_tn(hot, table_ref[n]) + dot_tn(hot, table_ref[n + 1]) for n in (0, 2)]


def turn_table():
    lane = np.arange(128)
    rates = 10000.0 ** (-(lane % 16) / 16)
    angle = np.arange(16)[:, None] * rates
    row_lane = (lane % 64) < 32
    out = []
    for v in (np.cos(angle), np.sin(angle) * np.where(lane % 32 < 16, -1.0, 1.0)):
        v = np.concatenate([np.where(row_lane, v, 0.0), np.where(row_lane, 0.0, v)])
        high = v.astype(ml_dtypes.bfloat16)
        out += [high, (v - high.astype(np.float64)).astype(ml_dtypes.bfloat16)]
    return np.stack(out)


def pack_kernel(at_ref, lat_ref, dy_ref, row_ref, col_ref, lat_out, dy_out):
    other = 2 - 2 * at_ref[0]
    dy_out[...] = dy_ref[...]
    for i in range(2):
        lat_out[i, :128] = lat_ref[i]
        here = pl.ds(other + i, 1)
        line = jnp.concatenate(
            [row_ref[here, :].astype(f32), col_ref[here, :].astype(f32), jnp.zeros((1, 128), f32)],
            axis=1,
        )
        lat_out[i, 128:] = jnp.broadcast_to(line, (16, 384)).astype(bf16)


def split(v):
    hi = v.astype(bf16)
    return jnp.concatenate([hi, (v - hi.astype(f32)).astype(bf16)], axis=0)


def fine_dot(v, w):
    n = v.shape[0]
    out = dot(split(v), w)
    return out[:n] + out[n:]


def silu(v):
    return v / (1.0 + jnp.exp(-v))


def modulation_kernel(
    at_ref, t_ref, l_ref, tw1_ref, tw2_ref, row0_ref, row1_ref, modw_ref, mod_ref, extra_ref
):
    first = 2 * at_ref[0]
    freqs = jnp.exp(lane_iota((1, 128)).astype(f32) * (-math.log(10000.0) / 128))
    spot = lax.broadcasted_iota(jnp.int32, (16, 1), 0)
    steps = jnp.where(
        spot == 0,
        t_ref[first].astype(f32),
        jnp.where(spot == 1, t_ref[first + 1].astype(f32), 0.0),
    )
    angle = steps * freqs
    emb = jnp.concatenate([jnp.cos(angle), jnp.sin(angle)], axis=1)
    hidden = silu(fine_dot(emb, tw1_ref[...]))
    cond = fine_dot(hidden, tw2_ref[...])
    for i, ref in enumerate((row0_ref, row1_ref)):
        label = l_ref[first + i]
        row = jnp.sum(
            jnp.where(spot == (label & 15), ref[...].astype(f32), 0.0), axis=0, keepdims=True
        )
        cond = cond + jnp.where(spot == i, row, 0.0)
    mod = fine_dot(silu(cond), modw_ref[...])
    lane = lane_iota((1, 128))
    codes = jnp.zeros((1, 128), f32)
    for i in range(2):
        label = l_ref[first + i]
        codes = jnp.where(lane == i, (label >> 5).astype(f32), codes)
        codes = jnp.where(lane == 2 + i, (label & 31).astype(f32), codes)
        for k in range(6):
            mod_ref[i, k : k + 1] = mod[i : i + 1, k * 384 : k * 384 + 384]
        for b in range(2):
            extra_ref[1 + i * 2 + b : 2 + i * 2 + b] = emb[i : i + 1, b * 128 : b * 128 + 128]
        for b, p in enumerate(pairs()):
            extra_ref[5 + i * 3 + b : 6 + i * 3 + b] = cond[i : i + 1, p]
    extra_ref[0:1] = codes
    extra_ref[11:] = jnp.zeros((5, 128), f32)


def pairs(width=384):
    return [slice(j, j + 128) for j in range(0, width, 128)]


def forward_kernel(
    at_ref,
    kept_ref,
    got_ref,
    mod_ref,
    w_ref,
    qgain_ref,
    kgain_ref,
    row_ref,
    col_ref,
    table_ref,
    q_ref,
    k_ref,
    v_ref,
    att_ref,
):
    x = both(kept_ref, got_ref)
    h1 = (x * inv_rms(x) * (1.0 + mod_ref[0, 1:2]) + mod_ref[0, 0:1]).astype(bf16)
    z = dot(h1, w_ref[...])
    cosine, sine = turns(
        at_ref, pl.program_id(0), row_ref, col_ref, got_ref[0, 128:144], table_ref
    )
    gains = [jnp.concatenate([r[...], r[...]], axis=1) for r in (qgain_ref, kgain_ref)]
    masks = head_masks()
    for p in pairs():
        turned = []
        for part in range(2):
            zp = z[:, part * 384 + p.start : part * 384 + p.stop]
            n = zp * lax.rsqrt(head_mean(zp * zp) + EPS) * gains[part]
            turned.append(n * cosine + partner(n) * sine)
        q = (turned[0].astype(bf16).astype(f32) * 0.125).astype(bf16)
        k = turned[1].astype(bf16)
        v = z[:, 768 + p.start : 768 + p.stop].astype(bf16)
        q_ref[0, :, p], k_ref[0, :, p], v_ref[0, :, p] = q, k, v
        out = None
        for m in masks:
            e = jnp.exp(dot_nt(q * m, k))
            probs = (e * (1.0 / jnp.sum(e, axis=-1, keepdims=True))).astype(bf16)
            part_out = dot(probs, v * m)
            out = part_out if out is None else out + part_out
        att_ref[0, :, p] = out.astype(bf16)


def mlp_kernel(
    at_ref,
    kept_ref,
    got_ref,
    dkept_ref,
    dgot_ref,
    att_ref,
    mod_ref,
    proj_ref,
    wg_ref,
    wu_ref,
    wd_ref,
    keep_ref,
    send_ref,
    out_ref,
    outsend_ref,
    dmid_ref,
    sums_ref,
    branch_s,
    mid_s,
    h2_s,
    h2t_s,
    dmlp_s,
    mlp_s,
    dh2_s,
    units_s,
):
    j = pl.program_id(0)
    images = range(2)

    def rows(i):
        return slice(i * 256, (i + 1) * 256)

    def dy_of(i):
        return jnp.concatenate([dkept_ref[i], dgot_ref[i]], axis=0).astype(f32)

    @pl.when(j == 0)
    def _():
        branch_s[...] = dot(att_ref[...], proj_ref[...])
        for i in images:
            x = jnp.concatenate([kept_ref[i], got_ref[i, :128]], axis=0).astype(f32)
            mid = x + mod_ref[i, 2:3] * branch_s[rows(i)]
            mid_s[rows(i)] = mid
            h2_s[rows(i)] = (mid * inv_rms(mid) * (1.0 + mod_ref[i, 4:5]) + mod_ref[i, 3:4]).astype(
                bf16
            )
            dmlp_s[rows(i)] = (mod_ref[i, 5:6] * dy_of(i)).astype(bf16)
        h2t_s[...] = h2_s[...].T
        mlp_s[...] = jnp.zeros_like(mlp_s)
        dh2_s[...] = jnp.zeros_like(dh2_s)

    h2 = h2_s[...]
    d_mlp = dmlp_s[...]
    g = dot(h2, wg_ref[...])
    u = dot(h2, wu_ref[...])
    d_hid = dot_nt(d_mlp, wd_ref[...])
    sig = 1.0 / (1.0 + jnp.exp(-g))
    act = g * sig
    hid = (act * u).astype(bf16)
    du = (d_hid * act).astype(bf16)
    dg = (d_hid * u * (sig + act * (1.0 - sig))).astype(bf16)
    mlp_s[...] += dot(hid, wd_ref[...])
    dh2_s[...] += dot_nt(dg, wg_ref[...]) + dot_nt(du, wu_ref[...])
    h2t = h2t_s[...]
    for n, d in ((0, dg), (2, du)):
        grad = dot(h2t, d).astype(bf16)
        for b in range(2):
            units_s[(n + b) // 3, pl.ds((n + b) % 3 * 384, 384)] = grad[:, b * 128 : b * 128 + 128]
    down = dot_tn(hid, d_mlp).astype(bf16)
    for b in range(2):
        for c in range(3):
            units_s[1, pl.ds((b + 1) * 384 + c * 128, 128)] = down[
                b * 128 : b * 128 + 128, c * 128 : c * 128 + 128
            ]
    keep_ref[...] = units_s[at_ref[1]]
    send_ref[...] = units_s[1 - at_ref[1]]

    @pl.when(j == 3)
    def _():
        for i in images:
            mid, mlp, dh2, dy = mid_s[rows(i)], mlp_s[rows(i)], dh2_s[rows(i)], dy_of(i)
            out = (mid + mod_ref[i, 5:6] * mlp).astype(bf16)
            out_ref[i] = out[:128]
            outsend_ref[i] = out[128:]
            s = inv_rms(mid)
            n = mid * s
            e2 = dh2 * (1.0 + mod_ref[i, 4:5])
            d_mid = dy + s * (e2 - n * jnp.mean(e2 * n, axis=-1, keepdims=True))
            dmid_ref[rows(i)] = d_mid
            for k, v in enumerate((d_mid * branch_s[rows(i)], dh2, dh2 * n, dy * mlp)):
                total = jnp.sum(v, axis=0, keepdims=True)
                for b, p in enumerate(pairs()):
                    sums_ref[pl.ds(i * 12 + k * 3 + b, 1)] = total[:, p]


def backward_kernel(
    at_ref,
    kept_ref,
    got_ref,
    mod_ref,
    w_ref,
    qgain_ref,
    kgain_ref,
    row_ref,
    col_ref,
    table_ref,
    q_ref,
    k_ref,
    v_ref,
    att_ref,
    dmid_ref,
    proj_ref,
    keep_ref,
    send_ref,
    grad_ref,
    gradsend_ref,
    sums_ref,
    h1_s,
    dqkv_s,
    dbranch_s,
    att_s,
    gain_s,
    units_s,
):
    i = pl.program_id(0)
    here = pl.ds(pl.multiple_of(i * 256, 256), 256)
    x = both(kept_ref, got_ref)
    s1 = inv_rms(x)
    n1 = x * s1
    h1 = (n1 * (1.0 + mod_ref[0, 1:2]) + mod_ref[0, 0:1]).astype(bf16)
    h1_s[here] = h1
    att_s[here] = att_ref[0]
    d_mid = dmid_ref[...]
    d_branch = (mod_ref[0, 2:3] * d_mid).astype(bf16)
    dbranch_s[here] = d_branch
    d_att = dot_nt(d_branch, proj_ref[...]).astype(bf16)
    z = dot(h1, w_ref[:, :768])
    cosine, sine = turns(
        at_ref, pl.program_id(0), row_ref, col_ref, got_ref[0, 128:144], table_ref
    )
    gains = [jnp.concatenate([r[...], r[...]], axis=1) for r in (qgain_ref, kgain_ref)]
    masks = head_masks()
    gain_sums = [None, None]
    for p in pairs():
        q, k, v, do = q_ref[0, :, p], k_ref[0, :, p], v_ref[0, :, p], d_att[:, p]
        dq = dk = dv = 0.0
        for m in masks:
            qm, km, vm, dom = q * m, k * m, v * m, do * m
            e = jnp.exp(dot_nt(qm, k))
            soft = e * (1.0 / jnp.sum(e, axis=-1, keepdims=True))
            d_probs = dot_nt(dom, v)
            delta = jnp.sum(soft * d_probs, axis=-1, keepdims=True)
            ds = (soft * (d_probs - delta)).astype(bf16)
            dq = dq + dot(ds, km)
            dk = dk + dot_tn(ds, qm)
            dv = dv + dot_tn(soft.astype(bf16), dom)
        for part, d in enumerate((dq * 0.125, dk)):
            zp = z[:, part * 384 + p.start : part * 384 + p.stop]
            r = lax.rsqrt(head_mean(zp * zp) + EPS)
            n = zp * r
            dn = d * cosine - partner(d) * sine
            total = jnp.sum(dn * n, axis=0, keepdims=True)
            gain_sums[part] = total if gain_sums[part] is None else gain_sums[part] + total
            e = dn * gains[part]
            dz = r * (e - n * head_mean(e * n))
            dqkv_s[here, part * 384 + p.start : part * 384 + p.stop] = dz.astype(bf16)
        dqkv_s[here, 768 + p.start : 768 + p.stop] = dv.astype(bf16)
    d_h1 = dot_nt(dqkv_s[here], w_ref[...])
    e1 = d_h1 * (1.0 + mod_ref[0, 1:2])
    grad = d_mid + s1 * (e1 - n1 * jnp.mean(e1 * n1, axis=-1, keepdims=True))
    grad_ref[0] = grad[:128]
    gradsend_ref[0] = grad[128:].astype(bf16)
    gain_sums = [g + pltpu.roll(g, 64, 1) for g in gain_sums]
    gain_sums = jnp.where(lane_iota((1, 128)) < 64, gain_sums[0], gain_sums[1])

    def put_sums(at):
        for k, v in enumerate((d_h1, d_h1 * n1)):
            total = jnp.sum(v, axis=0, keepdims=True)
            for b, p in enumerate(pairs()):
                sums_ref[pl.ds(at * 6 + k * 3 + b, 1)] = total[:, p]

    @pl.when(i == 0)
    def _():
        put_sums(0)
        gain_s[...] = jnp.broadcast_to(gain_sums, (8, 128))

    @pl.when(i == 1)
    def _():
        put_sums(1)
        sums_ref[pl.ds(12, 1)] = gain_s[0:1] + gain_sums
        sums_ref[pl.ds(13, 3)] = jnp.zeros((3, 128), f32)
        h1t = h1_s[...].T
        for part in range(3):
            w = dot(h1t, dqkv_s[:, part * 384 : part * 384 + 384]).astype(bf16)
            for b, p in enumerate(pairs()):
                n = part * 3 + b
                units_s[n // 6, pl.ds(n % 6 * 384, 384)] = w[:, p]
        w = dot_tn(att_s[...], dbranch_s[...]).astype(bf16)
        for b, p in enumerate(pairs()):
            units_s[1, pl.ds((3 + b) * 384, 384)] = w[:, p]
        keep_ref[...] = units_s[at_ref[1]]
        send_ref[...] = units_s[1 - at_ref[1]]


def whole_spec(shape):
    return pl.BlockSpec(shape, lambda *_: (0,) * len(shape))


def params(mib):
    return pltpu.CompilerParams(vmem_limit_bytes=mib * MIB)


def shape_of(shape, dtype):
    return jax.ShapeDtypeStruct(shape, dtype)


def image_spec(shape):
    return pl.BlockSpec((1,) + shape, lambda i, at: (i,) + (0,) * len(shape))


KEPT = pl.BlockSpec((1, 128, 384), lambda i, at: (2 * at[0] + i, 0, 0))
KEPT2 = pl.BlockSpec((2, 128, 384), lambda j, at: (at[0], 0, 0))


def cost(flops, nbytes):
    return pl.CostEstimate(flops=flops, bytes_accessed=nbytes, transcendentals=0)


def pack_call(at, latents, out_grad, pos_row, pos_col):
    theirs = pl.BlockSpec((2, 128, 384), lambda j, at: (1 - at[0], 0, 0))
    shapes = [(2, 144, 384), (2, 128, 384)]
    return pl.pallas_call(
        pack_kernel,
        grid_spec=pltpu.PrefetchScalarGridSpec(
            num_scalar_prefetch=1,
            grid=(1,),
            in_specs=[theirs, theirs, whole_spec((4, 128)), whole_spec((4, 128))],
            out_specs=[whole_spec(s) for s in shapes],
        ),
        out_shape=[shape_of(s, bf16) for s in shapes],
        compiler_params=params(8),
        cost_estimate=cost(200_000, 800_000),
        name="pack_swaps",
    )(at, latents, out_grad, pos_row, pos_col)


def modulation_call(at, timesteps, labels, t_w1, t_w2, label_table, mod_w):
    def row_spec(i):
        return pl.BlockSpec((16, 384), lambda j, at, t, l: (l[2 * at[0] + i] >> 4, 0))

    shapes = [(2, 6, 384), (16, 128)]
    return pl.pallas_call(
        modulation_kernel,
        grid_spec=pltpu.PrefetchScalarGridSpec(
            num_scalar_prefetch=3,
            grid=(1,),
            in_specs=[
                whole_spec((256, 384)),
                whole_spec((384, 384)),
                row_spec(0),
                row_spec(1),
                whole_spec((384, 2304)),
            ],
            out_specs=[whole_spec(s) for s in shapes],
        ),
        out_shape=[shape_of(s, f32) for s in shapes],
        compiler_params=params(16),
        cost_estimate=cost(1_000_000_000, 3_000_000),
        name="modulation",
    )(at, timesteps, labels, t_w1, t_w2, label_table, label_table, mod_w)


def forward_call(at, latents, got, mod, qkv_w, *rest):
    act = shape_of((2, 256, 384), bf16)
    return pl.pallas_call(
        forward_kernel,
        grid_spec=pltpu.PrefetchScalarGridSpec(
            num_scalar_prefetch=1,
            grid=(2,),
            in_specs=[
                KEPT,
                image_spec((144, 384)),
                image_spec((6, 384)),
                whole_spec((384, 1152)),
                whole_spec((1, 64)),
                whole_spec((1, 64)),
                whole_spec((4, 128)),
                whole_spec((4, 128)),
                whole_spec((4, 32, 128)),
            ],
            out_specs=[image_spec((256, 384))] * 4,
        ),
        out_shape=[act] * 4,
        compiler_params=params(12),
        cost_estimate=cost(3_000_000_000, 4_000_000),
        name="attention_forward",
    )(at, latents, got, mod, qkv_w, *rest)


def mlp_call(at, latents, got, out_grad, dgot, att, mod, proj_w, gate_up_w, down_w):
    return pl.pallas_call(
        mlp_kernel,
        grid_spec=pltpu.PrefetchScalarGridSpec(
            num_scalar_prefetch=1,
            grid=(4,),
            in_specs=[
                KEPT2,
                whole_spec((2, 144, 384)),
                KEPT2,
                whole_spec((2, 128, 384)),
                whole_spec((512, 384)),
                whole_spec((2, 6, 384)),
                whole_spec((384, 384)),
                pl.BlockSpec((384, 256), lambda j, at: (0, j)),
                pl.BlockSpec((384, 256), lambda j, at: (0, j + 4)),
                pl.BlockSpec((256, 384), lambda j, at: (j, 0)),
            ],
            out_specs=[
                pl.BlockSpec((1152, 128), lambda j, at: (j, 0)),
                pl.BlockSpec((1152, 128), lambda j, at: (j, 0)),
                KEPT2,
                whole_spec((2, 128, 384)),
                whole_spec((512, 384)),
                whole_spec((24, 128)),
            ],
            scratch_shapes=[
                pltpu.VMEM((512, 384), f32),
                pltpu.VMEM((512, 384), f32),
                pltpu.VMEM((512, 384), bf16),
                pltpu.VMEM((384, 512), bf16),
                pltpu.VMEM((512, 384), bf16),
                pltpu.VMEM((512, 384), f32),
                pltpu.VMEM((512, 384), f32),
                pltpu.VMEM((2, 1152, 128), bf16),
            ],
        ),
        out_shape=[
            shape_of((4608, 128), bf16),
            shape_of((4608, 128), bf16),
            shape_of((4, 128, 384), bf16),
            shape_of((2, 128, 384), bf16),
            shape_of((512, 384), f32),
            shape_of((24, 128), f32),
        ],
        compiler_params=params(16),
        cost_estimate=cost(6_000_000_000, 8_000_000),
        name="mlp_both_ways",
    )(at, latents, got, out_grad, dgot, att, mod, proj_w, gate_up_w, gate_up_w, down_w)


def backward_call(at, latents, got, mod, qkv_w, *rest):
    return pl.pallas_call(
        backward_kernel,
        grid_spec=pltpu.PrefetchScalarGridSpec(
            num_scalar_prefetch=1,
            grid=(2,),
            in_specs=[
                KEPT,
                image_spec((144, 384)),
                image_spec((6, 384)),
                whole_spec((384, 1152)),
                whole_spec((1, 64)),
                whole_spec((1, 64)),
                whole_spec((4, 128)),
                whole_spec((4, 128)),
                whole_spec((4, 32, 128)),
            ]
            + [image_spec((256, 384))] * 4
            + [pl.BlockSpec((256, 384), lambda i, at: (i, 0)), whole_spec((384, 384))],
            out_specs=[
                whole_spec((2304, 128)),
                whole_spec((2304, 128)),
                KEPT,
                image_spec((128, 384)),
                whole_spec((16, 128)),
            ],
            scratch_shapes=[
                pltpu.VMEM((512, 384), bf16),
                pltpu.VMEM((512, 1152), bf16),
                pltpu.VMEM((512, 384), bf16),
                pltpu.VMEM((512, 384), bf16),
                pltpu.VMEM((8, 128), f32),
                pltpu.VMEM((2, 2304, 128), bf16),
            ],
        ),
        out_shape=[
            shape_of((2304, 128), bf16),
            shape_of((2304, 128), bf16),
            shape_of((4, 128, 384), f32),
            shape_of((2, 128, 384), bf16),
            shape_of((16, 128), f32),
        ],
        compiler_params=params(20),
        cost_estimate=cost(5_000_000_000, 6_000_000),
        name="attention_backward",
    )(at, latents, got, mod, qkv_w, *rest)


def join_kernel(
    a_ref, a_got_ref, b_ref, b_got_ref, sums1_ref, sums2_ref, extra_ref, out_ref, lines
):
    lines[:24] = sums1_ref[...]
    lines[24:40] = sums2_ref[...]
    lines[37:48] = extra_ref[:11]
    out_ref[:, :288] = (a_ref[...].astype(f32) + a_got_ref[...].astype(f32)).astype(bf16)
    out_ref[:, 288:432] = (b_ref[...].astype(f32) + b_got_ref[...].astype(f32)).astype(bf16)
    out_ref[:, 432:] = jnp.broadcast_to(lines[...].astype(bf16)[None], (16, 48, 128))


def join_call(keep1, got1, keep2, got2, *lines):
    big, small = (16, 288, 128), (16, 144, 128)
    return pl.pallas_call(
        join_kernel,
        out_shape=shape_of((16, 480, 128), bf16),
        scratch_shapes=[pltpu.VMEM((48, 128), f32)],
        compiler_params=params(14),
        cost_estimate=cost(2_000_000, 6_000_000),
        name="join_messages",
    )(keep1.reshape(big), got1.reshape(big), keep2.reshape(small), got2.reshape(small), *lines)


def sum_kernel(a_ref, out_ref, extra_ref):
    total = a_ref[0, :432].astype(f32)
    for n in range(1, 16):
        total = total + a_ref[n, :432].astype(f32)
    out_ref[:432] = total.astype(bf16)
    out_ref[432:] = jnp.zeros((16, 128), bf16)
    extra_ref[...] = a_ref[:, 432:]


def sum_call(a):
    return pl.pallas_call(
        sum_kernel,
        out_shape=[shape_of((448, 128), bf16), shape_of((16, 48, 128), bf16)],
        compiler_params=params(14),
        cost_estimate=cost(2_000_000, 3_000_000),
        name="sum_xy",
    )(a)


def fetch(at_ref, own_ref, got_ref, slots, sems):
    c = at_ref[1]
    copies = [
        pltpu.make_async_copy(own_ref, slots.at[c], sems.at[0]),
        pltpu.make_async_copy(got_ref, slots.at[1 - c], sems.at[1]),
    ]
    for copy in copies:
        copy.start()
    for copy in copies:
        copy.wait()


def condition_kernel(
    at_ref,
    own_ref,
    got_ref,
    tw1_ref,
    tw2_ref,
    modw_ref,
    tw1g_ref,
    tw2g_ref,
    tableg_ref,
    modwg_ref,
    gains_ref,
    slots,
    rows_s,
    dmod_s,
    cond_s,
    emb_s,
    sems,
):
    fetch(at_ref, own_ref, got_ref, slots, sems)
    for h in range(2):
        for n in range(8):
            part = slots[h, pl.ds(n * 768, 768)]
            rows_s[pl.ds(h * 6144 + n * 768, 768)] = part.astype(f32)

    def line(r):
        return rows_s[pl.ds(r, 256, stride=48), :]

    for i in range(2):
        here = slice(i * 256, i * 256 + 256)
        for k in range(6):
            for b in range(3):
                r = 24 + i * 6 + k * 3 + b if k < 2 else i * 12 + (k - 2) * 3 + b
                at = k * 384 + b * 128
                dmod_s[here, at : at + 128] = line(r).astype(bf16)
        for b in range(2):
            emb_s[here, b * 128 : b * 128 + 128] = line(38 + i * 2 + b).astype(bf16)
        for b in range(3):
            cond_s[here, b * 128 : b * 128 + 128] = line(42 + i * 3 + b)
    gains_ref[...] = jnp.sum(line(36), axis=0, keepdims=True)
    codes = line(37)
    labels = jnp.concatenate([codes[:, i : i + 1] * 32.0 + codes[:, i + 2 : i + 3] for i in range(2)])
    cond = cond_s[...]
    sig = 1.0 / (1.0 + jnp.exp(-cond))
    act_t = (cond * sig).astype(bf16).T
    for k in range(6):
        cols = slice(k * 384, k * 384 + 384)
        modwg_ref[:, cols] = dot(act_t, dmod_s[:, cols])
    d_cond = dot_nt(dmod_s[...], modw_ref[...]) * (sig + cond * sig * (1.0 - sig))
    dc = d_cond.astype(bf16)
    labels = labels.astype(jnp.int32)
    for n in range(4):
        hot = jnp.where(lane_iota((512, 256)) + n * 256 == labels, 1.0, 0.0).astype(bf16)
        rows = dot_tn(hot, dc)
        top = min(256, 1001 - n * 256)
        tableg_ref[n * 256 : n * 256 + top] = rows[:top]
    emb = emb_s[...]
    pre = dot(emb, tw1_ref[...])
    sig = 1.0 / (1.0 + jnp.exp(-pre))
    hid = pre * sig
    tw2g_ref[...] = dot_tn(hid.astype(bf16), dc)
    d_pre = (dot_nt(dc, tw2_ref[...]) * (sig + hid * (1.0 - sig))).astype(bf16)
    tw1g_ref[...] = dot_tn(emb, d_pre)


def condition_call(at, own, got, t_w1, t_w2, mod_w):
    anywhere = pl.BlockSpec(memory_space=pl.ANY)
    shapes = [(256, 384), (384, 384), (1001, 384), (384, 2304), (1, 128)]
    return pl.pallas_call(
        condition_kernel,
        grid_spec=pltpu.PrefetchScalarGridSpec(
            num_scalar_prefetch=1,
            grid=(1,),
            in_specs=[anywhere, anywhere]
            + [whole_spec(s) for s in ((256, 384), (384, 384), (384, 2304))],
            out_specs=[whole_spec(s) for s in shapes],
            scratch_shapes=[
                pltpu.VMEM((2, 6144, 128), bf16),
                pltpu.VMEM((12288, 128), f32),
                pltpu.VMEM((512, 2304), bf16),
                pltpu.VMEM((512, 384), f32),
                pltpu.VMEM((512, 256), bf16),
                pltpu.SemaphoreType.DMA((2,)),
            ],
        ),
        out_shape=[shape_of(s, f32) for s in shapes],
        compiler_params=params(36),
        cost_estimate=cost(100_000_000, 100_000),
        name="condition_gradients",
    )(at, own, got, t_w1, t_w2, mod_w)


def cuts(start, chunk):
    out, at = [], start
    while at < start + 384:
        n = at // chunk
        stop = min((n + 1) * chunk, start + 384)
        out.append((n, at - n * chunk, stop - n * chunk))
        at = stop
    return out


def unpack_kernel(at_ref, own_ref, got_ref, qkv_ref, proj_ref, gu_ref, down_ref, slots, sems):
    t = pl.program_id(0)

    @pl.when(t == 0)
    def _():
        fetch(at_ref, own_ref, got_ref, slots, sems)

    def unit(half, first, u, chunk, base):
        return jnp.concatenate(
            [slots[half, first + n, base + a : base + b] for n, a, b in cuts(u * 384, chunk)]
        ).astype(f32)

    @pl.when(t < 4)
    def _():
        gu_ref[:, :128] = unit(0, 4 * t, 0, 288, 0)
        gu_ref[:, 128:] = unit(0, 4 * t, 1, 288, 0)
        for b, p in enumerate(pairs()):
            block = unit(t // 2, 8 * (t % 2), b, 144, 288)

            @pl.when(t < 3)
            def _():
                qkv_ref[:, p] = block

            @pl.when(t == 3)
            def _():
                proj_ref[:, p] = block

    @pl.when(t >= 4)
    def _():
        gu_ref[:, :128] = unit(0, 4 * (t - 4), 2, 288, 0)
        gu_ref[:, 128:] = unit(1, 4 * (t - 4), 0, 288, 0)

    for odd in range(2):

        @pl.when(t % 2 == odd)
        def _():
            rows = unit(1, 4 * (t // 2), 1 + odd, 288, 0)
            for b, p in enumerate(pairs()):
                down_ref[:, p] = rows[b * 128 : b * 128 + 128]


def unpack_call(at, own, got):
    anywhere = pl.BlockSpec(memory_space=pl.ANY)
    return pl.pallas_call(
        unpack_kernel,
        grid_spec=pltpu.PrefetchScalarGridSpec(
            num_scalar_prefetch=1,
            grid=(8,),
            in_specs=[anywhere, anywhere],
            out_specs=[
                pl.BlockSpec((384, 384), lambda t, at: (0, jnp.minimum(t, 2))),
                whole_spec((384, 384)),
                pl.BlockSpec((384, 256), lambda t, at: (0, t)),
                pl.BlockSpec((128, 384), lambda t, at: (t, 0)),
            ],
            scratch_shapes=[
                pltpu.VMEM((2, 16, 448, 128), bf16),
                pltpu.SemaphoreType.DMA((2,)),
            ],
        ),
        out_shape=[
            shape_of(s, f32) for s in ((384, 1152), (384, 384), (384, 2048), (1024, 384))
        ],
        compiler_params=params(14),
        cost_estimate=cost(2_000_000, 11_000_000),
        name="unpack_sums",
    )(at, own, got)


def flat(y, z, x, c):
    return ((((y * 8 + z) * 2 + x % 2) * 2 + c) * 2) + x // 2


def groups(axes):
    rest = [a for a in "yzxc" if a not in axes]
    out = []
    for fixed in itertools.product(*[range(SIZES[a]) for a in rest]):
        place = dict(zip(rest, fixed))
        row = []
        for moving in itertools.product(*[range(SIZES[a]) for a in axes]):
            row.append(flat(**{**place, **dict(zip(axes, moving))}))
        out.append(row)
    return out


def exchange(v, axes):
    return lax.all_to_all(v, AXES, 0, 0, tiled=True, axis_index_groups=groups(axes))


def gather(v, axes):
    n = math.prod(SIZES[a] for a in axes)
    return exchange(jnp.broadcast_to(v[None], (n,) + v.shape), axes)


BAND_SWAP = [(n, n ^ 1) for n in range(256)]
CORE_SWAP = [(n, n ^ 2) for n in range(256)]


def swap(v):
    return lax.ppermute(v, AXES, BAND_SWAP)


def core_swap(v):
    return lax.ppermute(v, AXES, CORE_SWAP)


def body(
    latents,
    pos_row,
    pos_col,
    timesteps,
    labels,
    t_w1,
    t_w2,
    label_table,
    mod_w,
    qkv_w,
    q_gain,
    k_gain,
    proj_w,
    gate_up_w,
    down_w,
    out_grad,
):
    band = lax.axis_index("band")
    core = lax.axis_index("img") % 2
    at = jnp.stack([band, core]).astype(jnp.int32)
    send, dsend = pack_call(at, latents, out_grad, pos_row, pos_col)
    got, dgot = swap(send), swap(dsend)
    mod, extra = modulation_call(at, timesteps, labels, t_w1, t_w2, label_table, mod_w)
    turn = (q_gain.reshape(1, 64), k_gain.reshape(1, 64), pos_row, pos_col, turn_table())
    q, k, v, att = forward_call(at, latents, got, mod, qkv_w, *turn)
    keep1, send1, block_out, out_send, d_mid, sums1 = mlp_call(
        at, latents, got, out_grad, dgot, att.reshape(512, 384), mod, proj_w, gate_up_w, down_w
    )
    got1 = core_swap(send1)
    out_got = swap(out_send)
    keep2, send2, latents_grad, grad_send, sums2 = backward_call(
        at, latents, got, mod, qkv_w, *turn, q, k, v, att, d_mid, proj_w
    )
    send2, out_got = lax.optimization_barrier((send2, out_got))
    chunk, extra = sum_call(
        exchange(join_call(keep1, got1, keep2, core_swap(send2), sums1, sums2, extra), "xy")
    )
    extra = lax.all_gather(
        extra.reshape(768, 128), AXES, axis=0, tiled=True, axis_index_groups=groups("z")
    )
    chunk = jnp.sum(exchange(chunk.reshape(8, 56, 128), "z").astype(f32), axis=0).astype(bf16)
    chunk = gather(chunk, "z").reshape(448, 128)
    chunk, grad_got = lax.optimization_barrier((chunk, swap(grad_send)))
    wide = lax.optimization_barrier(jnp.broadcast_to(chunk[None], (16, 448, 128)))
    summed = exchange(wide, "xy")
    extra, _ = lax.optimization_barrier((extra, wide))
    conditioned = condition_call(at, extra, core_swap(extra), t_w1, t_w2, mod_w)
    summed, conditioned = lax.optimization_barrier((summed, conditioned))
    tw1_grad, tw2_grad, table_grad, modw_grad, gain_sums = conditioned
    qkv_sum, proj_sum, gu_sum, down_sum = unpack_call(at, summed, core_swap(summed))
    other = 2 - 2 * band
    block_out = lax.dynamic_update_slice_in_dim(block_out, out_got, other, 0)
    latents_grad = lax.dynamic_update_slice_in_dim(latents_grad, grad_got.astype(f32), other, 0)
    return (
        block_out,
        latents_grad,
        tw1_grad,
        tw2_grad,
        table_grad,
        modw_grad,
        qkv_sum,
        gain_sums[0, :64],
        gain_sums[0, 64:],
        proj_sum,
        gu_sum,
        down_sum,
    )


def solution(mesh):
    split = P("img", "band", None)
    return jax.shard_map(
        body,
        mesh=mesh,
        in_specs=(split, P("img", "band"), P("img", "band"), P("img"), P("img"))
        + (P(),) * 10
        + (split,),
        out_specs=(split, split) + (P(),) * 10,
        check_vma=False,
    )
```

```python
import itertools
import math

import jax
import jax.numpy as jnp
from jax import lax
from jax.experimental import pallas as pl
from jax.experimental.pallas import tpu as pltpu
from jax.sharding import PartitionSpec as P
import ml_dtypes
import numpy as np

AXES = ("img", "band")
SIZES = {"y": 4, "z": 8, "x": 4, "c": 2}
f32 = jnp.float32
bf16 = jnp.bfloat16
EPS = 1e-06
MIB = 1024 * 1024
CHUNK = 256


def dot(a, b):
    return jnp.dot(a, b, preferred_element_type=f32)


def dot_nt(a, b):
    return lax.dot_general(a, b, (((1,), (1,)), ((), ())), preferred_element_type=f32)


def dot_tn(a, b):
    return lax.dot_general(a, b, (((0,), (0,)), ((), ())), preferred_element_type=f32)


def inv_rms(v):
    return lax.rsqrt(jnp.mean(v * v, axis=-1, keepdims=True) + EPS)


def lane_iota(shape):
    return lax.broadcasted_iota(jnp.int32, shape, len(shape) - 1)


def head_mean(v):
    r = lax.broadcasted_iota(jnp.int32, (256, 256), 0) >> 6
    c = lax.broadcasted_iota(jnp.int32, (256, 256), 1) >> 6
    same = jnp.where(r == c, 1.0 / 64, 0.0).astype(bf16)
    v = v.astype(bf16)
    return jnp.concatenate(
        [dot(v[:, n : n + 256], same) for n in range(0, v.shape[1], 256)], axis=1
    )


def partner(v):
    first = (lane_iota((1, 128)) % 32) < 16
    return jnp.where(first, pltpu.roll(v, 112, 1), pltpu.roll(v, 16, 1))


def head_masks():
    low = (lane_iota((1, 128)) < 64).astype(f32)
    return low.astype(bf16), (1.0 - low).astype(bf16)


def both(at_ref, a_ref, b_ref, i):
    return jnp.concatenate([a_ref[2 * at_ref[0] + i], b_ref[i, :128]], axis=0).astype(f32)


def turns(at_ref, image, row_ref, col_ref, got, table_ref):
    here = pl.ds(2 * at_ref[0] + image, 1)
    hot = []
    for n, ref in enumerate((row_ref, col_ref)):
        kept = ref[here, :].astype(f32)
        pos = jnp.concatenate([kept, got[0:1, n * 128 : n * 128 + 128].astype(f32)], axis=1)
        spots = lax.broadcasted_iota(jnp.int32, (16, 256), 0).astype(f32)
        hot.append(jnp.where(spots == pos, 1.0, 0.0))
    hot = jnp.concatenate(hot, axis=0).astype(bf16)
    return [dot_tn(hot, table_ref[n]) + dot_tn(hot, table_ref[n + 1]) for n in (0, 2)]


def turn_table():
    lane = np.arange(128)
    rates = 10000.0 ** (-(lane % 16) / 16)
    angle = np.arange(16)[:, None] * rates
    row_lane = (lane % 64) < 32
    out = []
    for v in (np.cos(angle), np.sin(angle) * np.where(lane % 32 < 16, -1.0, 1.0)):
        v = np.concatenate([np.where(row_lane, v, 0.0), np.where(row_lane, 0.0, v)])
        high = v.astype(ml_dtypes.bfloat16)
        out += [high, (v - high.astype(np.float64)).astype(ml_dtypes.bfloat16)]
    return np.stack(out)


def pack_kernel(at_ref, lat_ref, dy_ref, row_ref, col_ref, lat_out, dy_out):
    other = 2 - 2 * at_ref[0]
    dy_out[...] = dy_ref[...]
    for i in range(2):
        lat_out[i, :128] = lat_ref[i]
        here = pl.ds(other + i, 1)
        line = jnp.concatenate(
            [row_ref[here, :].astype(f32), col_ref[here, :].astype(f32), jnp.zeros((1, 128), f32)],
            axis=1,
        )
        lat_out[i, 128:] = jnp.broadcast_to(line, (16, 384)).astype(bf16)


def split(v):
    hi = v.astype(bf16)
    return jnp.concatenate([hi, (v - hi.astype(f32)).astype(bf16)], axis=0)


def fine_dot(v, w):
    n = v.shape[0]
    out = dot(split(v), w)
    return out[:n] + out[n:]


def silu(v):
    return v / (1.0 + jnp.exp(-v))


def modulation_kernel(
    at_ref, t_ref, l_ref, tw1_ref, tw2_ref, row0_ref, row1_ref, modw_ref, mod_ref, extra_ref
):
    first = 2 * at_ref[0]
    freqs = jnp.exp(lane_iota((1, 128)).astype(f32) * (-math.log(10000.0) / 128))
    spot = lax.broadcasted_iota(jnp.int32, (16, 1), 0)
    steps = jnp.where(
        spot == 0,
        t_ref[first].astype(f32),
        jnp.where(spot == 1, t_ref[first + 1].astype(f32), 0.0),
    )
    angle = steps * freqs
    emb = jnp.concatenate([jnp.cos(angle), jnp.sin(angle)], axis=1)
    hidden = silu(fine_dot(emb, tw1_ref[...]))
    cond = fine_dot(hidden, tw2_ref[...])
    for i, ref in enumerate((row0_ref, row1_ref)):
        label = l_ref[first + i]
        row = jnp.sum(
            jnp.where(spot == (label & 15), ref[...].astype(f32), 0.0), axis=0, keepdims=True
        )
        cond = cond + jnp.where(spot == i, row, 0.0)
    mod = fine_dot(silu(cond), modw_ref[...])
    lane = lane_iota((1, 128))
    codes = jnp.zeros((1, 128), f32)
    for i in range(2):
        label = l_ref[first + i]
        codes = jnp.where(lane == i, (label >> 5).astype(f32), codes)
        codes = jnp.where(lane == 2 + i, (label & 31).astype(f32), codes)
        for k in range(6):
            mod_ref[i, k : k + 1] = mod[i : i + 1, k * 384 : k * 384 + 384]
        for b in range(2):
            extra_ref[1 + i * 2 + b : 2 + i * 2 + b] = emb[i : i + 1, b * 128 : b * 128 + 128]
        for b, p in enumerate(pairs()):
            extra_ref[5 + i * 3 + b : 6 + i * 3 + b] = cond[i : i + 1, p]
    extra_ref[0:1] = codes
    extra_ref[11:] = jnp.zeros((5, 128), f32)


def pairs(width=384):
    return [slice(j, j + 128) for j in range(0, width, 128)]


def forward_kernel(
    at_ref,
    kept_ref,
    got_ref,
    mod_ref,
    w_ref,
    qgain_ref,
    kgain_ref,
    row_ref,
    col_ref,
    table_ref,
    q_ref,
    k_ref,
    v_ref,
    att_ref,
):
    gains = [jnp.concatenate([r[...], r[...]], axis=1) for r in (qgain_ref, kgain_ref)]
    masks = head_masks()
    for i in range(2):
        x = both(at_ref, kept_ref, got_ref, i)
        h1 = (x * inv_rms(x) * (1.0 + mod_ref[i, 1:2]) + mod_ref[i, 0:1]).astype(bf16)
        z = dot(h1, w_ref[:, :768])
        v_ref[i] = dot(h1, w_ref[:, 768:]).astype(bf16)
        z = z * lax.rsqrt(head_mean(z * z) + EPS)
        cosine, sine = turns(at_ref, i, row_ref, col_ref, got_ref[i, 128:144], table_ref)
        for p in pairs():
            turned = []
            for part in range(2):
                n = z[:, part * 384 + p.start : part * 384 + p.stop] * gains[part]
                turned.append(n * cosine + partner(n) * sine)
            q = (turned[0].astype(bf16).astype(f32) * 0.125).astype(bf16)
            k = turned[1].astype(bf16)
            q_ref[i, :, p], k_ref[i, :, p] = q, k
            v = v_ref[i, :, p]
            out = None
            for m in masks:
                e = jnp.exp(dot_nt(q * m, k))
                part_out = dot(e.astype(bf16), v * m) / jnp.sum(e, axis=-1, keepdims=True)
                out = part_out if out is None else out + part_out
            att_ref[i * 256 : i * 256 + 256, p] = out.astype(bf16)


def mlp_kernel(
    at_ref,
    kept_ref,
    got_ref,
    dkept_ref,
    dgot_ref,
    att_ref,
    mod_ref,
    proj_ref,
    wgu_ref,
    wd_ref,
    keep_ref,
    send_ref,
    out_ref,
    outsend_ref,
    dmid_ref,
    sums_ref,
    branch_s,
    mid_s,
    h2_s,
    h2t_s,
    dmlp_s,
    mlp_s,
    dh2_s,
):
    images = range(2)

    def rows(i):
        return slice(i * 256, (i + 1) * 256)

    branch_s[...] = dot(att_ref[...], proj_ref[...])
    for i in images:
        mid = both(at_ref, kept_ref, got_ref, i) + mod_ref[i, 2:3] * branch_s[rows(i)]
        mid_s[rows(i)] = mid
        h2_s[rows(i)] = (mid * inv_rms(mid) * (1.0 + mod_ref[i, 4:5]) + mod_ref[i, 3:4]).astype(
            bf16
        )
        dmlp_s[rows(i)] = (mod_ref[i, 5:6] * both(at_ref, dkept_ref, dgot_ref, i)).astype(bf16)
    h2t_s[...] = h2_s[...].T
    h2 = h2_s[...]
    d_mlp = dmlp_s[...]
    first = True
    for ref, half in ((send_ref, 1 - at_ref[1]), (keep_ref, at_ref[1])):
        for n in range(2):
            base = half * 512 + n * CHUNK
            wg = wgu_ref[:, pl.ds(pl.multiple_of(base, CHUNK), CHUNK)]
            wu = wgu_ref[:, pl.ds(pl.multiple_of(base + 1024, CHUNK), CHUNK)]
            wd = wd_ref[pl.ds(pl.multiple_of(base, CHUNK), CHUNK), :]
            g = dot(h2, wg)
            u = dot(h2, wu)
            d_hid = dot_nt(d_mlp, wd)
            sig = 1.0 / (1.0 + jnp.exp(-g))
            act = g * sig
            hid = (act * u).astype(bf16)
            du = (d_hid * act).astype(bf16)
            dg = (d_hid * u * (sig + act * (1.0 - sig))).astype(bf16)
            mlp = dot(hid, wd)
            d_h2 = dot_nt(dg, wg) + dot_nt(du, wu)
            mlp_s[...] = mlp if first else mlp_s[...] + mlp
            dh2_s[...] = d_h2 if first else dh2_s[...] + d_h2
            first = False
            for m, d in ((0, dg), (4, du)):
                grad = dot(h2t_s[...], d).astype(bf16)
                for b in range(2):
                    ref[pl.ds((m + 2 * n + b) * 384, 384)] = grad[:, b * 128 : b * 128 + 128]
            down = dot_tn(hid, d_mlp).astype(bf16)
            for b in range(2):
                for c in range(3):
                    ref[pl.ds((8 + 2 * n + b) * 384 + c * 128, 128)] = down[
                        b * 128 : b * 128 + 128, c * 128 : c * 128 + 128
                    ]
    for i in images:
        mid, mlp, dh2 = mid_s[rows(i)], mlp_s[rows(i)], dh2_s[rows(i)]
        dy = both(at_ref, dkept_ref, dgot_ref, i)
        out = (mid + mod_ref[i, 5:6] * mlp).astype(bf16)
        out_ref[2 * at_ref[0] + i] = out[:128]
        outsend_ref[i] = out[128:]
        s = inv_rms(mid)
        n = mid * s
        e2 = dh2 * (1.0 + mod_ref[i, 4:5])
        d_mid = dy + s * (e2 - n * jnp.mean(e2 * n, axis=-1, keepdims=True))
        dmid_ref[rows(i)] = d_mid
        for k, v in enumerate((d_mid * branch_s[rows(i)], dh2, dh2 * n, dy * mlp)):
            total = jnp.sum(v, axis=0, keepdims=True)
            for b, p in enumerate(pairs()):
                sums_ref[pl.ds(i * 12 + k * 3 + b, 1)] = total[:, p]


def backward_kernel(
    at_ref,
    kept_ref,
    got_ref,
    mod_ref,
    w_ref,
    qgain_ref,
    kgain_ref,
    row_ref,
    col_ref,
    table_ref,
    q_ref,
    k_ref,
    v_ref,
    att_ref,
    dmid_ref,
    proj_ref,
    outsend_ref,
    keep_ref,
    send_ref,
    grad_ref,
    swap_ref,
    sums_ref,
    h1_s,
    dqkv_s,
    dbranch_s,
    units_s,
):
    gains = [jnp.concatenate([r[...], r[...]], axis=1) for r in (qgain_ref, kgain_ref)]
    masks = head_masks()
    gain_sums = [0.0, 0.0]
    for i in range(2):
        here = slice(i * 256, i * 256 + 256)
        x = both(at_ref, kept_ref, got_ref, i)
        s1 = inv_rms(x)
        n1 = x * s1
        h1 = (n1 * (1.0 + mod_ref[i, 1:2]) + mod_ref[i, 0:1]).astype(bf16)
        h1_s[here] = h1
        d_mid = dmid_ref[here]
        d_branch = (mod_ref[i, 2:3] * d_mid).astype(bf16)
        dbranch_s[here] = d_branch
        d_att = dot_nt(d_branch, proj_ref[...]).astype(bf16)
        z = dot(h1, w_ref[:, :768])
        r = lax.rsqrt(head_mean(z * z) + EPS)
        z = z * r
        cosine, sine = turns(at_ref, i, row_ref, col_ref, got_ref[i, 128:144], table_ref)
        turned = [[], []]
        for p in pairs():
            q, k, v, do = q_ref[i, :, p], k_ref[i, :, p], v_ref[i, :, p], d_att[:, p]
            dq = dk = dv = 0.0
            for m in masks:
                qm, km, dom = q * m, k * m, do * m
                e = jnp.exp(dot_nt(k, qm))
                soft = e * (1.0 / jnp.sum(e, axis=0, keepdims=True))
                d_probs = dot_nt(v, dom)
                delta = jnp.sum(soft * d_probs, axis=0, keepdims=True)
                ds = (soft * (d_probs - delta)).astype(bf16)
                dq = dq + dot_tn(ds, km)
                dk = dk + dot(ds, qm)
                dv = dv + dot(soft.astype(bf16), dom)
            for part, d in enumerate((dq * 0.125, dk)):
                n = z[:, part * 384 + p.start : part * 384 + p.stop]
                dn = d * cosine - partner(d) * sine
                gain_sums[part] = gain_sums[part] + jnp.sum(dn * n, axis=0, keepdims=True)
                turned[part].append(dn * gains[part])
            dqkv_s[here, 768 + p.start : 768 + p.stop] = dv.astype(bf16)
        e = jnp.concatenate(turned[0] + turned[1], axis=1)
        dqkv_s[here, :768] = (r * (e - z * head_mean(e * z))).astype(bf16)
        d_h1 = dot_nt(dqkv_s[here], w_ref[...])
        e1 = d_h1 * (1.0 + mod_ref[i, 1:2])
        grad = d_mid + s1 * (e1 - n1 * jnp.mean(e1 * n1, axis=-1, keepdims=True))
        grad_ref[2 * at_ref[0] + i] = grad[:128]
        swap_ref[i, 0] = outsend_ref[i]
        swap_ref[i, 1] = grad[128:].astype(bf16)
        for k, v in enumerate((d_h1, d_h1 * n1)):
            total = jnp.sum(v, axis=0, keepdims=True)
            for b, p in enumerate(pairs()):
                sums_ref[pl.ds(i * 6 + k * 3 + b, 1)] = total[:, p]
    gain_sums = [g + pltpu.roll(g, 64, 1) for g in gain_sums]
    sums_ref[pl.ds(12, 1)] = jnp.where(lane_iota((1, 128)) < 64, gain_sums[0], gain_sums[1])
    sums_ref[pl.ds(13, 3)] = jnp.zeros((3, 128), f32)
    h1t = h1_s[...].T
    for part in range(3):
        w = dot(h1t, dqkv_s[:, part * 384 : part * 384 + 384]).astype(bf16)
        for b, p in enumerate(pairs()):
            n = part * 3 + b
            units_s[n // 6, pl.ds(n % 6 * 384, 384)] = w[:, p]
    w = dot_tn(att_ref[...], dbranch_s[...]).astype(bf16)
    for b, p in enumerate(pairs()):
        units_s[1, pl.ds((3 + b) * 384, 384)] = w[:, p]
    keep_ref[...] = units_s[at_ref[1]]
    send_ref[...] = units_s[1 - at_ref[1]]


def whole_spec(shape):
    return pl.BlockSpec(shape, lambda *_: (0,) * len(shape))


def params(mib):
    return pltpu.CompilerParams(vmem_limit_bytes=mib * MIB)


def shape_of(shape, dtype):
    return jax.ShapeDtypeStruct(shape, dtype)


def cost(flops, nbytes):
    return pl.CostEstimate(flops=flops, bytes_accessed=nbytes, transcendentals=0)


def pack_call(at, latents, out_grad, pos_row, pos_col):
    theirs = pl.BlockSpec((2, 128, 384), lambda j, at: (1 - at[0], 0, 0))
    shapes = [(2, 144, 384), (2, 128, 384)]
    return pl.pallas_call(
        pack_kernel,
        grid_spec=pltpu.PrefetchScalarGridSpec(
            num_scalar_prefetch=1,
            grid=(1,),
            in_specs=[theirs, theirs, whole_spec((4, 128)), whole_spec((4, 128))],
            out_specs=[whole_spec(s) for s in shapes],
        ),
        out_shape=[shape_of(s, bf16) for s in shapes],
        compiler_params=params(56),
        cost_estimate=cost(200_000, 800_000),
        name="pack_swaps",
    )(at, latents, out_grad, pos_row, pos_col)


def modulation_call(at, timesteps, labels, t_w1, t_w2, label_table, mod_w):
    def row_spec(i):
        return pl.BlockSpec((16, 384), lambda j, at, t, l: (l[2 * at[0] + i] >> 4, 0))

    shapes = [(2, 6, 384), (16, 128)]
    return pl.pallas_call(
        modulation_kernel,
        grid_spec=pltpu.PrefetchScalarGridSpec(
            num_scalar_prefetch=3,
            grid=(1,),
            in_specs=[
                whole_spec((256, 384)),
                whole_spec((384, 384)),
                row_spec(0),
                row_spec(1),
                whole_spec((384, 2304)),
            ],
            out_specs=[whole_spec(s) for s in shapes],
        ),
        out_shape=[shape_of(s, f32) for s in shapes],
        compiler_params=params(56),
        cost_estimate=cost(1_000_000_000, 3_000_000),
        name="modulation",
    )(at, timesteps, labels, t_w1, t_w2, label_table, label_table, mod_w)


SCALARS = pl.BlockSpec(memory_space=pltpu.SMEM)
RESIDENT = pl.BlockSpec(memory_space=pltpu.VMEM)


def resident_call(kernel, name, outs, estimate, mib, scratch=(), loose=(), loose_out=()):
    def spec(is_loose, shape):
        return whole_spec(shape) if is_loose else RESIDENT

    def call(at, *arrays):
        return pl.pallas_call(
            kernel,
            grid=(1,),
            in_specs=[SCALARS] + [spec(n in loose, a.shape) for n, a in enumerate(arrays)],
            out_specs=[spec(n in loose_out, o[0]) for n, o in enumerate(outs)],
            out_shape=[shape_of(*o) for o in outs],
            scratch_shapes=[pltpu.VMEM(*o) for o in scratch],
            compiler_params=params(mib),
            cost_estimate=estimate,
            name=name,
        )(at, *arrays)

    return call


forward_call = resident_call(
    forward_kernel,
    "attention_forward",
    [((2, 256, 384), bf16)] * 3 + [((512, 384), bf16)],
    cost(3_000_000_000, 4_000_000),
    12,
    loose_out=range(4),
)
mlp_call = resident_call(
    mlp_kernel,
    "mlp_both_ways",
    [
        ((4608, 128), bf16),
        ((4608, 128), bf16),
        ((4, 128, 384), bf16),
        ((2, 128, 384), bf16),
        ((512, 384), f32),
        ((24, 128), f32),
    ],
    cost(6_000_000_000, 8_000_000),
    24,
    [
        ((512, 384), f32),
        ((512, 384), f32),
        ((512, 384), bf16),
        ((384, 512), bf16),
        ((512, 384), bf16),
        ((512, 384), f32),
        ((512, 384), f32),
    ],
    loose=(4,),
    loose_out=(2, 3, 4, 5),
)
backward_call = resident_call(
    backward_kernel,
    "attention_backward",
    [
        ((2304, 128), bf16),
        ((2304, 128), bf16),
        ((4, 128, 384), f32),
        ((2, 2, 128, 384), bf16),
        ((16, 128), f32),
    ],
    cost(5_000_000_000, 6_000_000),
    24,
    [((512, 384), bf16), ((512, 1152), bf16), ((512, 384), bf16), ((2, 2304, 128), bf16)],
    loose=range(9, 16),
    loose_out=(2, 3, 4),
)


def join_kernel(
    a_ref, a_got_ref, b_ref, b_got_ref, sums1_ref, sums2_ref, extra_ref, out_ref, lines
):
    lines[:24] = sums1_ref[...]
    lines[24:40] = sums2_ref[...]
    lines[37:48] = extra_ref[:11]
    out_ref[:, :288] = (a_ref[...].astype(f32) + a_got_ref[...].astype(f32)).astype(bf16)
    out_ref[:, 288:432] = (b_ref[...].astype(f32) + b_got_ref[...].astype(f32)).astype(bf16)
    out_ref[:, 432:] = jnp.broadcast_to(lines[...].astype(bf16)[None], (16, 48, 128))


def join_call(keep1, got1, keep2, got2, *lines):
    big, small = (16, 288, 128), (16, 144, 128)
    return pl.pallas_call(
        join_kernel,
        out_shape=shape_of((16, 480, 128), bf16),
        scratch_shapes=[pltpu.VMEM((48, 128), f32)],
        compiler_params=params(14),
        cost_estimate=cost(2_000_000, 6_000_000),
        name="join_messages",
    )(keep1.reshape(big), got1.reshape(big), keep2.reshape(small), got2.reshape(small), *lines)


def sum_kernel(a_ref, out_ref, extra_ref):
    total = a_ref[0, :432].astype(f32)
    for n in range(1, 16):
        total = total + a_ref[n, :432].astype(f32)
    out_ref[:432] = total.astype(bf16)
    out_ref[432:] = jnp.zeros((16, 128), bf16)
    extra_ref[...] = a_ref[:, 432:]


def sum_call(a):
    return pl.pallas_call(
        sum_kernel,
        out_shape=[shape_of((448, 128), bf16), shape_of((16, 48, 128), bf16)],
        compiler_params=params(14),
        cost_estimate=cost(2_000_000, 3_000_000),
        name="sum_xy",
    )(a)


def fetch(at_ref, own_ref, got_ref, slots, sems):
    c = at_ref[1]
    copies = [
        pltpu.make_async_copy(own_ref, slots.at[c], sems.at[0]),
        pltpu.make_async_copy(got_ref, slots.at[1 - c], sems.at[1]),
    ]
    for copy in copies:
        copy.start()
    for copy in copies:
        copy.wait()


def condition_kernel(
    at_ref,
    own_ref,
    got_ref,
    tw1_ref,
    tw2_ref,
    modw_ref,
    tw1g_ref,
    tw2g_ref,
    tableg_ref,
    modwg_ref,
    gains_ref,
    slots,
    rows_s,
    dmod_s,
    cond_s,
    emb_s,
    sems,
):
    fetch(at_ref, own_ref, got_ref, slots, sems)
    for h in range(2):
        for n in range(8):
            part = slots[h, pl.ds(n * 768, 768)]
            rows_s[pl.ds(h * 6144 + n * 768, 768)] = part.astype(f32)

    def line(r):
        return rows_s[pl.ds(r, 256, stride=48), :]

    for i in range(2):
        here = slice(i * 256, i * 256 + 256)
        for k in range(6):
            for b in range(3):
                r = 24 + i * 6 + k * 3 + b if k < 2 else i * 12 + (k - 2) * 3 + b
                at = k * 384 + b * 128
                dmod_s[here, at : at + 128] = line(r).astype(bf16)
        for b in range(2):
            emb_s[here, b * 128 : b * 128 + 128] = line(38 + i * 2 + b).astype(bf16)
        for b in range(3):
            cond_s[here, b * 128 : b * 128 + 128] = line(42 + i * 3 + b)
    gains_ref[...] = jnp.sum(line(36), axis=0, keepdims=True)
    codes = line(37)
    labels = jnp.concatenate([codes[:, i : i + 1] * 32.0 + codes[:, i + 2 : i + 3] for i in range(2)])
    cond = cond_s[...]
    sig = 1.0 / (1.0 + jnp.exp(-cond))
    act_t = (cond * sig).astype(bf16).T
    for k in range(6):
        cols = slice(k * 384, k * 384 + 384)
        modwg_ref[:, cols] = dot(act_t, dmod_s[:, cols])
    d_cond = dot_nt(dmod_s[...], modw_ref[...]) * (sig + cond * sig * (1.0 - sig))
    dc = d_cond.astype(bf16)
    labels = labels.astype(jnp.int32)
    for n in range(4):
        hot = jnp.where(lane_iota((512, 256)) + n * 256 == labels, 1.0, 0.0).astype(bf16)
        rows = dot_tn(hot, dc)
        top = min(256, 1001 - n * 256)
        tableg_ref[n * 256 : n * 256 + top] = rows[:top]
    emb = emb_s[...]
    pre = dot(emb, tw1_ref[...])
    sig = 1.0 / (1.0 + jnp.exp(-pre))
    hid = pre * sig
    tw2g_ref[...] = dot_tn(hid.astype(bf16), dc)
    d_pre = (dot_nt(dc, tw2_ref[...]) * (sig + hid * (1.0 - sig))).astype(bf16)
    tw1g_ref[...] = dot_tn(emb, d_pre)


def condition_call(at, own, got, t_w1, t_w2, mod_w):
    anywhere = pl.BlockSpec(memory_space=pl.ANY)
    shapes = [(256, 384), (384, 384), (1001, 384), (384, 2304), (1, 128)]
    return pl.pallas_call(
        condition_kernel,
        grid_spec=pltpu.PrefetchScalarGridSpec(
            num_scalar_prefetch=1,
            grid=(1,),
            in_specs=[anywhere, anywhere]
            + [whole_spec(s) for s in ((256, 384), (384, 384), (384, 2304))],
            out_specs=[whole_spec(s) for s in shapes],
            scratch_shapes=[
                pltpu.VMEM((2, 6144, 128), bf16),
                pltpu.VMEM((12288, 128), f32),
                pltpu.VMEM((512, 2304), bf16),
                pltpu.VMEM((512, 384), f32),
                pltpu.VMEM((512, 256), bf16),
                pltpu.SemaphoreType.DMA((2,)),
            ],
        ),
        out_shape=[shape_of(s, f32) for s in shapes],
        compiler_params=params(36),
        cost_estimate=cost(100_000_000, 100_000),
        name="condition_gradients",
    )(at, own, got, t_w1, t_w2, mod_w)


def cuts(start, chunk):
    out, at = [], start
    while at < start + 384:
        n = at // chunk
        stop = min((n + 1) * chunk, start + 384)
        out.append((n, at - n * chunk, stop - n * chunk))
        at = stop
    return out


def unpack_kernel(own, at_ref, sums_ref, *refs):
    qkv_ref, proj_ref, gu_ref, down_ref = refs[-4:]
    t = pl.program_id(0)
    half = at_ref[1] if own else 1 - at_ref[1]

    def first(u):
        rows = [sums_ref[n, a:b] for n, a, b in cuts(u * 384, 288)]
        return jnp.concatenate(rows).astype(f32)

    def second(u):
        rows = [sums_ref[n, 288 + a : 288 + b] for n, a, b in cuts(u * 384, 144)]
        return jnp.concatenate(rows).astype(f32)

    @pl.when(t == 0)
    def _():
        for b in range(4):
            gu_ref[:, b * 128 : b * 128 + 128] = first(b)
        for b, p in enumerate(pairs()):
            qkv_ref[:, p] = second(b)

    @pl.when(t == 1)
    def _():
        for n in range(4):
            gu_ref[:, n * 128 : n * 128 + 128] = first(4 + n)
            rows = first(8 + n)
            for b, p in enumerate(pairs()):
                down_ref[n * 128 : n * 128 + 128, p] = rows[b * 128 : b * 128 + 128]

        @pl.when(half == 0)
        def _():
            for b, p in enumerate(pairs()):
                qkv_ref[:, p] = second(3 + b)
            proj_ref[...] = jnp.zeros((384, 384), f32) if own else refs[0][...]

        @pl.when(half == 1)
        def _():
            for b, p in enumerate(pairs()):
                proj_ref[:, p] = second(3 + b)


def unpack_call(own, at, sums, earlier=()):
    def half_of(at):
        return at[1] if own else 1 - at[1]

    shapes = [(384, 1152), (384, 384), (384, 2048), (1024, 384)]
    anywhere = pl.BlockSpec(memory_space=pl.ANY)
    kept = [whole_spec((384, 384))] + [anywhere] * 3 if earlier else []
    earlier = [earlier[n] for n in (1, 0, 2, 3)] if earlier else []
    return pl.pallas_call(
        lambda *refs: unpack_kernel(own, *refs),
        grid_spec=pltpu.PrefetchScalarGridSpec(
            num_scalar_prefetch=1,
            grid=(2,),
            in_specs=[RESIDENT] + kept,
            out_specs=[
                pl.BlockSpec((384, 384), lambda t, at: (0, half_of(at) * (2 - t) + t)),
                whole_spec((384, 384)),
                pl.BlockSpec((384, 512), lambda t, at: (0, 2 * t + half_of(at))),
                pl.BlockSpec((512, 384), lambda t, at: (half_of(at), 0)),
            ],
        ),
        out_shape=[shape_of(s, f32) for s in shapes],
        input_output_aliases={2: 1, 3: 0, 4: 2, 5: 3} if earlier else {},
        compiler_params=params(20),
        cost_estimate=cost(2_000_000, 6_000_000),
        name="unpack_own" if own else "unpack_other",
    )(at, sums, *earlier)


def flat(y, z, x, c):
    return ((((y * 8 + z) * 2 + x % 2) * 2 + c) * 2) + x // 2


def groups(axes):
    rest = [a for a in "yzxc" if a not in axes]
    out = []
    for fixed in itertools.product(*[range(SIZES[a]) for a in rest]):
        place = dict(zip(rest, fixed))
        row = []
        for moving in itertools.product(*[range(SIZES[a]) for a in axes]):
            row.append(flat(**{**place, **dict(zip(axes, moving))}))
        out.append(row)
    return out


def exchange(v, axes):
    return lax.all_to_all(v, AXES, 0, 0, tiled=True, axis_index_groups=groups(axes))


def gather(v, axes):
    n = math.prod(SIZES[a] for a in axes)
    return exchange(jnp.broadcast_to(v[None], (n,) + v.shape), axes)


BAND_SWAP = [(n, n ^ 1) for n in range(256)]
CORE_SWAP = [(n, n ^ 2) for n in range(256)]


def swap(v):
    return lax.ppermute(v, AXES, BAND_SWAP)


def core_swap(v):
    return lax.ppermute(v, AXES, CORE_SWAP)


def body(
    latents,
    pos_row,
    pos_col,
    timesteps,
    labels,
    t_w1,
    t_w2,
    label_table,
    mod_w,
    qkv_w,
    q_gain,
    k_gain,
    proj_w,
    gate_up_w,
    down_w,
    out_grad,
):
    band = lax.axis_index("band")
    core = lax.axis_index("img") % 2
    at = jnp.stack([band, core]).astype(jnp.int32)
    send, dsend = pack_call(at, latents, out_grad, pos_row, pos_col)
    got = swap(send)
    mod, extra = modulation_call(at, timesteps, labels, t_w1, t_w2, label_table, mod_w)
    mod, dsend = lax.optimization_barrier((mod, dsend))
    dgot = swap(dsend)
    turn = (q_gain.reshape(1, 64), k_gain.reshape(1, 64), pos_row, pos_col, turn_table())
    q, k, v, att = forward_call(at, latents, got, mod, qkv_w, *turn)
    keep1, send1, block_out, out_send, d_mid, sums1 = mlp_call(
        at, latents, got, out_grad, dgot, att, mod, proj_w, gate_up_w, down_w
    )
    got1 = core_swap(send1)
    keep2, send2, latents_grad, swaps, sums2 = backward_call(
        at, latents, got, mod, qkv_w, *turn, q, k, v, att, d_mid, proj_w, out_send
    )
    joined = join_call(keep1, got1, keep2, core_swap(send2), sums1, sums2, extra)
    chunk, extra = sum_call(exchange(joined, "xy"))
    extra = lax.all_gather(
        extra.reshape(768, 128), AXES, axis=0, tiled=True, axis_index_groups=groups("z")
    )
    chunk = jnp.sum(exchange(chunk.reshape(8, 56, 128), "z").astype(f32), axis=0).astype(bf16)
    chunk = gather(chunk, "z").reshape(448, 128)
    chunk, swaps = lax.optimization_barrier((chunk, swap(swaps)))
    wide = lax.optimization_barrier(jnp.broadcast_to(chunk[None], (16, 448, 128)))
    summed = exchange(wide, "xy")
    extra, _ = lax.optimization_barrier((extra, wide))
    conditioned = condition_call(at, extra, core_swap(extra), t_w1, t_w2, mod_w)
    summed, conditioned = lax.optimization_barrier((summed, conditioned))
    tw1_grad, tw2_grad, table_grad, modw_grad, gain_sums = conditioned
    sums = unpack_call(True, at, summed)
    qkv_sum, proj_sum, gu_sum, down_sum = unpack_call(False, at, core_swap(summed), sums)
    other = 2 - 2 * band
    block_out = lax.dynamic_update_slice_in_dim(block_out, swaps[:, 0], other, 0)
    latents_grad = lax.dynamic_update_slice_in_dim(latents_grad, swaps[:, 1].astype(f32), other, 0)
    return (
        block_out,
        latents_grad,
        tw1_grad,
        tw2_grad,
        table_grad,
        modw_grad,
        qkv_sum,
        gain_sums[0, :64],
        gain_sums[0, 64:],
        proj_sum,
        gu_sum,
        down_sum,
    )


def solution(mesh):
    split = P("img", "band", None)
    return jax.shard_map(
        body,
        mesh=mesh,
        in_specs=(split, P("img", "band"), P("img", "band"), P("img"), P("img"))
        + (P(),) * 10
        + (split,),
        out_specs=(split, split) + (P(),) * 10,
        check_vma=False,
    )
```

```python
import itertools
import math

import jax
import jax.numpy as jnp
from jax import lax
from jax.experimental import pallas as pl
from jax.experimental.pallas import tpu as pltpu
from jax.sharding import PartitionSpec as P
import ml_dtypes
import numpy as np

AXES = ("img", "band")
f32 = jnp.float32
bf16 = jnp.bfloat16
EPS = 1e-06
MIB = 1024 * 1024
CHUNK = 256


def dot(a, b):
    return jnp.dot(a, b, preferred_element_type=f32)


def dot_nt(a, b):
    return lax.dot_general(a, b, (((1,), (1,)), ((), ())), preferred_element_type=f32)


def dot_tn(a, b):
    return lax.dot_general(a, b, (((0,), (0,)), ((), ())), preferred_element_type=f32)


def inv_rms(v):
    return lax.rsqrt(jnp.mean(v * v, axis=-1, keepdims=True) + EPS)


def lane_iota(shape):
    return lax.broadcasted_iota(jnp.int32, shape, len(shape) - 1)


def head_mean(v):
    r = lax.broadcasted_iota(jnp.int32, (256, 256), 0) >> 6
    c = lax.broadcasted_iota(jnp.int32, (256, 256), 1) >> 6
    same = jnp.where(r == c, 1.0 / 64, 0.0).astype(bf16)
    v = v.astype(bf16)
    return jnp.concatenate(
        [dot(v[:, n : n + 256], same) for n in range(0, v.shape[1], 256)], axis=1
    )


def partner(v):
    first = (lane_iota((1, 128)) % 32) < 16
    return jnp.where(first, pltpu.roll(v, 112, 1), pltpu.roll(v, 16, 1))


def head_masks():
    low = (lane_iota((1, 128)) < 64).astype(f32)
    return low.astype(bf16), (1.0 - low).astype(bf16)


def both(at_ref, a_ref, b_ref, i):
    return jnp.concatenate([a_ref[2 * at_ref[0] + i], b_ref[i, :128]], axis=0).astype(f32)


def turns(at_ref, image, row_ref, col_ref, got, table_ref):
    here = pl.ds(2 * at_ref[0] + image, 1)
    hot = []
    for n, ref in enumerate((row_ref, col_ref)):
        kept = ref[here, :].astype(f32)
        pos = jnp.concatenate([kept, got[0:1, n * 128 : n * 128 + 128].astype(f32)], axis=1)
        spots = lax.broadcasted_iota(jnp.int32, (16, 256), 0).astype(f32)
        hot.append(jnp.where(spots == pos, 1.0, 0.0))
    hot = jnp.concatenate(hot, axis=0).astype(bf16)
    return [dot_tn(hot, table_ref[n]) + dot_tn(hot, table_ref[n + 1]) for n in (0, 2)]


def turn_table():
    lane = np.arange(128)
    rates = 10000.0 ** (-(lane % 16) / 16)
    angle = np.arange(16)[:, None] * rates
    row_lane = (lane % 64) < 32
    out = []
    for v in (np.cos(angle), np.sin(angle) * np.where(lane % 32 < 16, -1.0, 1.0)):
        v = np.concatenate([np.where(row_lane, v, 0.0), np.where(row_lane, 0.0, v)])
        high = v.astype(ml_dtypes.bfloat16)
        out += [high, (v - high.astype(np.float64)).astype(ml_dtypes.bfloat16)]
    return np.stack(out)


def pack_kernel(at_ref, lat_ref, dy_ref, row_ref, col_ref, lat_out, dy_out):
    other = 2 - 2 * at_ref[0]
    dy_out[...] = dy_ref[...]
    for i in range(2):
        lat_out[i, :128] = lat_ref[i]
        here = pl.ds(other + i, 1)
        line = jnp.concatenate(
            [row_ref[here, :].astype(f32), col_ref[here, :].astype(f32), jnp.zeros((1, 128), f32)],
            axis=1,
        )
        lat_out[i, 128:] = jnp.broadcast_to(line, (16, 384)).astype(bf16)


def split(v):
    hi = v.astype(bf16)
    return jnp.concatenate([hi, (v - hi.astype(f32)).astype(bf16)], axis=0)


def fine_dot(v, w):
    n = v.shape[0]
    out = dot(split(v), w)
    return out[:n] + out[n:]


def silu(v):
    return v / (1.0 + jnp.exp(-v))


def modulation_kernel(
    at_ref, t_ref, l_ref, tw1_ref, tw2_ref, row0_ref, row1_ref, modw_ref, mod_ref, extra_ref
):
    first = 2 * at_ref[0]
    freqs = jnp.exp(lane_iota((1, 128)).astype(f32) * (-math.log(10000.0) / 128))
    spot = lax.broadcasted_iota(jnp.int32, (16, 1), 0)
    steps = jnp.where(
        spot == 0,
        t_ref[first].astype(f32),
        jnp.where(spot == 1, t_ref[first + 1].astype(f32), 0.0),
    )
    angle = steps * freqs
    emb = jnp.concatenate([jnp.cos(angle), jnp.sin(angle)], axis=1)
    hidden = silu(fine_dot(emb, tw1_ref[...]))
    cond = fine_dot(hidden, tw2_ref[...])
    for i, ref in enumerate((row0_ref, row1_ref)):
        label = l_ref[first + i]
        row = jnp.sum(
            jnp.where(spot == (label & 15), ref[...].astype(f32), 0.0), axis=0, keepdims=True
        )
        cond = cond + jnp.where(spot == i, row, 0.0)
    mod = fine_dot(silu(cond), modw_ref[...])
    lane = lane_iota((1, 128))
    codes = jnp.zeros((1, 128), f32)
    for i in range(2):
        label = l_ref[first + i]
        codes = jnp.where(lane == i, (label >> 5).astype(f32), codes)
        codes = jnp.where(lane == 2 + i, (label & 31).astype(f32), codes)
        for k in range(6):
            mod_ref[i, k : k + 1] = mod[i : i + 1, k * 384 : k * 384 + 384]
        for b in range(2):
            extra_ref[1 + i * 2 + b : 2 + i * 2 + b] = emb[i : i + 1, b * 128 : b * 128 + 128]
        for b, p in enumerate(pairs()):
            extra_ref[5 + i * 3 + b : 6 + i * 3 + b] = cond[i : i + 1, p]
    extra_ref[0:1] = codes
    extra_ref[11:] = jnp.zeros((5, 128), f32)


def pairs(width=384):
    return [slice(j, j + 128) for j in range(0, width, 128)]


def forward_kernel(
    at_ref,
    kept_ref,
    got_ref,
    mod_ref,
    w_ref,
    qgain_ref,
    kgain_ref,
    row_ref,
    col_ref,
    table_ref,
    q_ref,
    k_ref,
    v_ref,
    att_ref,
):
    gains = [jnp.concatenate([r[...], r[...]], axis=1) for r in (qgain_ref, kgain_ref)]
    masks = head_masks()
    for i in range(2):
        x = both(at_ref, kept_ref, got_ref, i)
        h1 = (x * inv_rms(x) * (1.0 + mod_ref[i, 1:2]) + mod_ref[i, 0:1]).astype(bf16)
        z = dot(h1, w_ref[:, :768])
        v_ref[i] = dot(h1, w_ref[:, 768:]).astype(bf16)
        z = z * lax.rsqrt(head_mean(z * z) + EPS)
        cosine, sine = turns(at_ref, i, row_ref, col_ref, got_ref[i, 128:144], table_ref)
        for p in pairs():
            turned = []
            for part in range(2):
                n = z[:, part * 384 + p.start : part * 384 + p.stop] * gains[part]
                turned.append(n * cosine + partner(n) * sine)
            q = (turned[0].astype(bf16).astype(f32) * 0.125).astype(bf16)
            k = turned[1].astype(bf16)
            q_ref[i, :, p], k_ref[i, :, p] = q, k
            v = v_ref[i, :, p]
            out = None
            for m in masks:
                e = jnp.exp(dot_nt(q * m, k))
                part_out = dot(e.astype(bf16), v * m) / jnp.sum(e, axis=-1, keepdims=True)
                out = part_out if out is None else out + part_out
            att_ref[i * 256 : i * 256 + 256, p] = out.astype(bf16)


def mlp_kernel(
    at_ref,
    kept_ref,
    got_ref,
    dkept_ref,
    dgot_ref,
    att_ref,
    mod_ref,
    proj_ref,
    wgu_ref,
    wd_ref,
    keep_ref,
    send_ref,
    out_ref,
    outsend_ref,
    dmid_ref,
    sums_ref,
    branch_s,
    mid_s,
    h2_s,
    h2t_s,
    dmlp_s,
    mlp_s,
    dh2_s,
):
    images = range(2)

    def rows(i):
        return slice(i * 256, (i + 1) * 256)

    branch_s[...] = dot(att_ref[...], proj_ref[...])
    for i in images:
        mid = both(at_ref, kept_ref, got_ref, i) + mod_ref[i, 2:3] * branch_s[rows(i)]
        mid_s[rows(i)] = mid
        h2_s[rows(i)] = (mid * inv_rms(mid) * (1.0 + mod_ref[i, 4:5]) + mod_ref[i, 3:4]).astype(
            bf16
        )
        dmlp_s[rows(i)] = (mod_ref[i, 5:6] * both(at_ref, dkept_ref, dgot_ref, i)).astype(bf16)
    h2t_s[...] = h2_s[...].T
    h2 = h2_s[...]
    d_mlp = dmlp_s[...]
    first = True
    for ref, half in ((send_ref, 1 - at_ref[1]), (keep_ref, at_ref[1])):
        for n in range(2):
            base = half * 512 + n * CHUNK
            wg = wgu_ref[:, pl.ds(pl.multiple_of(base, CHUNK), CHUNK)]
            wu = wgu_ref[:, pl.ds(pl.multiple_of(base + 1024, CHUNK), CHUNK)]
            wd = wd_ref[pl.ds(pl.multiple_of(base, CHUNK), CHUNK), :]
            g = dot(h2, wg)
            u = dot(h2, wu)
            d_hid = dot_nt(d_mlp, wd)
            sig = 1.0 / (1.0 + jnp.exp(-g))
            act = g * sig
            hid = (act * u).astype(bf16)
            du = (d_hid * act).astype(bf16)
            dg = (d_hid * u * (sig + act * (1.0 - sig))).astype(bf16)
            mlp = dot(hid, wd)
            d_h2 = dot_nt(dg, wg) + dot_nt(du, wu)
            mlp_s[...] = mlp if first else mlp_s[...] + mlp
            dh2_s[...] = d_h2 if first else dh2_s[...] + d_h2
            first = False
            for m, d in ((0, dg), (4, du)):
                grad = dot(h2t_s[...], d).astype(bf16)
                for b in range(2):
                    ref[pl.ds((m + 2 * n + b) * 384, 384)] = grad[:, b * 128 : b * 128 + 128]
            down = dot_tn(hid, d_mlp).astype(bf16)
            for b in range(2):
                for c in range(3):
                    ref[pl.ds((8 + 2 * n + b) * 384 + c * 128, 128)] = down[
                        b * 128 : b * 128 + 128, c * 128 : c * 128 + 128
                    ]
    for i in images:
        mid, mlp, dh2 = mid_s[rows(i)], mlp_s[rows(i)], dh2_s[rows(i)]
        dy = both(at_ref, dkept_ref, dgot_ref, i)
        out = (mid + mod_ref[i, 5:6] * mlp).astype(bf16)
        out_ref[2 * at_ref[0] + i] = out[:128]
        outsend_ref[i] = out[128:]
        s = inv_rms(mid)
        n = mid * s
        e2 = dh2 * (1.0 + mod_ref[i, 4:5])
        d_mid = dy + s * (e2 - n * jnp.mean(e2 * n, axis=-1, keepdims=True))
        dmid_ref[rows(i)] = d_mid
        for k, v in enumerate((d_mid * branch_s[rows(i)], dh2, dh2 * n, dy * mlp)):
            total = jnp.sum(v, axis=0, keepdims=True)
            for b, p in enumerate(pairs()):
                sums_ref[pl.ds(i * 12 + k * 3 + b, 1)] = total[:, p]


def backward_kernel(
    at_ref,
    kept_ref,
    got_ref,
    mod_ref,
    w_ref,
    qgain_ref,
    kgain_ref,
    row_ref,
    col_ref,
    table_ref,
    q_ref,
    k_ref,
    v_ref,
    att_ref,
    dmid_ref,
    proj_ref,
    outsend_ref,
    keep_ref,
    send_ref,
    grad_ref,
    swap_ref,
    sums_ref,
    h1_s,
    dqkv_s,
    dbranch_s,
    units_s,
):
    gains = [jnp.concatenate([r[...], r[...]], axis=1) for r in (qgain_ref, kgain_ref)]
    masks = head_masks()
    gain_sums = [0.0, 0.0]
    for i in range(2):
        here = slice(i * 256, i * 256 + 256)
        x = both(at_ref, kept_ref, got_ref, i)
        s1 = inv_rms(x)
        n1 = x * s1
        h1 = (n1 * (1.0 + mod_ref[i, 1:2]) + mod_ref[i, 0:1]).astype(bf16)
        h1_s[here] = h1
        d_mid = dmid_ref[here]
        d_branch = (mod_ref[i, 2:3] * d_mid).astype(bf16)
        dbranch_s[here] = d_branch
        d_att = dot_nt(d_branch, proj_ref[...]).astype(bf16)
        z = dot(h1, w_ref[:, :768])
        r = lax.rsqrt(head_mean(z * z) + EPS)
        z = z * r
        cosine, sine = turns(at_ref, i, row_ref, col_ref, got_ref[i, 128:144], table_ref)
        turned = [[], []]
        for p in pairs():
            q, k, v, do = q_ref[i, :, p], k_ref[i, :, p], v_ref[i, :, p], d_att[:, p]
            dq = dk = dv = 0.0
            for m in masks:
                qm, km, dom = q * m, k * m, do * m
                e = jnp.exp(dot_nt(k, qm))
                soft = e * (1.0 / jnp.sum(e, axis=0, keepdims=True))
                d_probs = dot_nt(v, dom)
                delta = jnp.sum(soft * d_probs, axis=0, keepdims=True)
                ds = (soft * (d_probs - delta)).astype(bf16)
                dq = dq + dot_tn(ds, km)
                dk = dk + dot(ds, qm)
                dv = dv + dot(soft.astype(bf16), dom)
            for part, d in enumerate((dq * 0.125, dk)):
                n = z[:, part * 384 + p.start : part * 384 + p.stop]
                dn = d * cosine - partner(d) * sine
                gain_sums[part] = gain_sums[part] + jnp.sum(dn * n, axis=0, keepdims=True)
                turned[part].append(dn * gains[part])
            dqkv_s[here, 768 + p.start : 768 + p.stop] = dv.astype(bf16)
        e = jnp.concatenate(turned[0] + turned[1], axis=1)
        dqkv_s[here, :768] = (r * (e - z * head_mean(e * z))).astype(bf16)
        d_h1 = dot_nt(dqkv_s[here], w_ref[...])
        e1 = d_h1 * (1.0 + mod_ref[i, 1:2])
        grad = d_mid + s1 * (e1 - n1 * jnp.mean(e1 * n1, axis=-1, keepdims=True))
        grad_ref[2 * at_ref[0] + i] = grad[:128]
        swap_ref[i, 0] = outsend_ref[i]
        swap_ref[i, 1] = grad[128:].astype(bf16)
        for k, v in enumerate((d_h1, d_h1 * n1)):
            total = jnp.sum(v, axis=0, keepdims=True)
            for b, p in enumerate(pairs()):
                sums_ref[pl.ds(i * 6 + k * 3 + b, 1)] = total[:, p]
    gain_sums = [g + pltpu.roll(g, 64, 1) for g in gain_sums]
    sums_ref[pl.ds(12, 1)] = jnp.where(lane_iota((1, 128)) < 64, gain_sums[0], gain_sums[1])
    sums_ref[pl.ds(13, 3)] = jnp.zeros((3, 128), f32)
    h1t = h1_s[...].T
    for part in range(3):
        w = dot(h1t, dqkv_s[:, part * 384 : part * 384 + 384]).astype(bf16)
        for b, p in enumerate(pairs()):
            n = part * 3 + b
            units_s[n // 6, pl.ds(n % 6 * 384, 384)] = w[:, p]
    w = dot_tn(att_ref[...], dbranch_s[...]).astype(bf16)
    for b, p in enumerate(pairs()):
        units_s[1, pl.ds((3 + b) * 384, 384)] = w[:, p]
    keep_ref[...] = units_s[at_ref[1]]
    send_ref[...] = units_s[1 - at_ref[1]]


def whole_spec(shape):
    return pl.BlockSpec(shape, lambda *_: (0,) * len(shape))


def params(mib):
    return pltpu.CompilerParams(vmem_limit_bytes=mib * MIB)


def shape_of(shape, dtype):
    return jax.ShapeDtypeStruct(shape, dtype)


SCALARS = pl.BlockSpec(memory_space=pltpu.SMEM)
RESIDENT = pl.BlockSpec(memory_space=pltpu.VMEM)
IN_HBM = pl.BlockSpec(memory_space=pltpu.HBM)


def cost(flops, nbytes):
    return pl.CostEstimate(flops=flops, bytes_accessed=nbytes, transcendentals=0)


def pack_call(at, latents, out_grad, pos_row, pos_col):
    theirs = pl.BlockSpec((2, 128, 384), lambda j, at: (1 - at[0], 0, 0))
    shapes = [(2, 144, 384), (2, 128, 384)]
    return pl.pallas_call(
        pack_kernel,
        grid_spec=pltpu.PrefetchScalarGridSpec(
            num_scalar_prefetch=1,
            grid=(1,),
            in_specs=[theirs, theirs, whole_spec((4, 128)), whole_spec((4, 128))],
            out_specs=[whole_spec(s) for s in shapes],
        ),
        out_shape=[shape_of(s, bf16) for s in shapes],
        compiler_params=params(56),
        cost_estimate=cost(200_000, 800_000),
        name="pack_swaps",
    )(at, latents, out_grad, pos_row, pos_col)


def modulation_call(at, timesteps, labels, t_w1, t_w2, label_table, mod_w):
    def row_spec(i):
        return pl.BlockSpec((16, 384), lambda j, at, t, l: (l[2 * at[0] + i] >> 4, 0))

    shapes = [(2, 6, 384), (16, 128)]
    return pl.pallas_call(
        modulation_kernel,
        grid_spec=pltpu.PrefetchScalarGridSpec(
            num_scalar_prefetch=3,
            grid=(1,),
            in_specs=[
                whole_spec((256, 384)),
                whole_spec((384, 384)),
                row_spec(0),
                row_spec(1),
                whole_spec((384, 2304)),
            ],
            out_specs=[whole_spec(s) for s in shapes],
        ),
        out_shape=[shape_of(s, f32) for s in shapes],
        compiler_params=params(56),
        cost_estimate=cost(1_000_000_000, 3_000_000),
        name="modulation",
    )(at, timesteps, labels, t_w1, t_w2, label_table, label_table, mod_w)


def resident_call(kernel, name, outs, estimate, mib, scratch=(), loose=(), loose_out=()):
    def spec(is_loose, shape):
        return whole_spec(shape) if is_loose else RESIDENT

    def call(at, *arrays):
        return pl.pallas_call(
            kernel,
            grid=(1,),
            in_specs=[SCALARS] + [spec(n in loose, a.shape) for n, a in enumerate(arrays)],
            out_specs=[spec(n in loose_out, o[0]) for n, o in enumerate(outs)],
            out_shape=[shape_of(*o) for o in outs],
            scratch_shapes=[pltpu.VMEM(*o) for o in scratch],
            compiler_params=params(mib),
            cost_estimate=estimate,
            name=name,
        )(at, *arrays)

    return call


forward_call = resident_call(
    forward_kernel,
    "attention_forward",
    [((2, 256, 384), bf16)] * 3 + [((512, 384), bf16)],
    cost(3_000_000_000, 4_000_000),
    12,
    loose_out=range(4),
)
mlp_call = resident_call(
    mlp_kernel,
    "mlp_both_ways",
    [
        ((4608, 128), bf16),
        ((4608, 128), bf16),
        ((4, 128, 384), bf16),
        ((2, 128, 384), bf16),
        ((512, 384), f32),
        ((24, 128), f32),
    ],
    cost(6_000_000_000, 8_000_000),
    24,
    [
        ((512, 384), f32),
        ((512, 384), f32),
        ((512, 384), bf16),
        ((384, 512), bf16),
        ((512, 384), bf16),
        ((512, 384), f32),
        ((512, 384), f32),
    ],
    loose=(4,),
    loose_out=(2, 3, 4, 5),
)
backward_call = resident_call(
    backward_kernel,
    "attention_backward",
    [
        ((2304, 128), bf16),
        ((2304, 128), bf16),
        ((4, 128, 384), f32),
        ((2, 2, 128, 384), bf16),
        ((16, 128), f32),
    ],
    cost(5_000_000_000, 6_000_000),
    24,
    [((512, 384), bf16), ((512, 1152), bf16), ((512, 384), bf16), ((2, 2304, 128), bf16)],
    loose=range(9, 16),
    loose_out=(2, 3, 4),
)


def join_kernel(
    a_ref, a_got_ref, b_ref, b_got_ref, sums1_ref, sums2_ref, extra_ref, out_ref, lines
):
    lines[:24] = sums1_ref[...]
    lines[24:40] = sums2_ref[...]
    lines[37:48] = extra_ref[:11]
    out_ref[:, :288] = (a_ref[...].astype(f32) + a_got_ref[...].astype(f32)).astype(bf16)
    out_ref[:, 288:432] = (b_ref[...].astype(f32) + b_got_ref[...].astype(f32)).astype(bf16)
    out_ref[:, 432:] = jnp.broadcast_to(lines[...].astype(bf16)[None], (16, 48, 128))


def join_call(keep1, got1, keep2, got2, *lines):
    big, small = (16, 288, 128), (16, 144, 128)
    return pl.pallas_call(
        join_kernel,
        out_shape=shape_of((16, 480, 128), bf16),
        scratch_shapes=[pltpu.VMEM((48, 128), f32)],
        compiler_params=params(14),
        cost_estimate=cost(2_000_000, 6_000_000),
        name="join_messages",
    )(keep1.reshape(big), got1.reshape(big), keep2.reshape(small), got2.reshape(small), *lines)


def extra_kernel(a_ref, out_ref):
    out_ref[...] = a_ref[:, 432:]


def extra_call(a):
    return pl.pallas_call(
        extra_kernel,
        in_specs=[RESIDENT],
        out_specs=RESIDENT,
        out_shape=shape_of((16, 48, 128), bf16),
        compiler_params=params(4),
        cost_estimate=cost(1_000, 200_000),
        name="extra_rows",
    )(a)


def sum_kernel(at_ref, a_ref, keep_ref, send_ref, total_s):
    total = a_ref[0, :432].astype(f32)
    for n in range(1, 16):
        total = total + a_ref[n, :432].astype(f32)
    total = total.astype(bf16)
    total_s[0] = total[:224]
    total_s[1, :208] = total[224:]
    total_s[1, 208:] = jnp.zeros((16, 128), bf16)
    keep_ref[...] = total_s[at_ref[2]]
    send_ref[...] = total_s[1 - at_ref[2]]


def sum_call(at, a):
    return pl.pallas_call(
        sum_kernel,
        in_specs=[SCALARS, RESIDENT],
        out_specs=[RESIDENT] * 2,
        out_shape=[shape_of((224, 128), bf16)] * 2,
        scratch_shapes=[pltpu.VMEM((2, 224, 128), bf16)],
        compiler_params=params(14),
        cost_estimate=cost(2_000_000, 3_000_000),
        name="sum_layer",
    )(at, a)


def pick_lines(rows_ref, rows_s, here, dmod_ref, cond_ref, emb_ref, codes_ref, gains_ref):
    for n in range(8):
        rows_s[pl.ds(n * 768, 768)] = rows_ref[pl.ds(n * 768, 768)].astype(f32)

    def line(r):
        return rows_s[pl.ds(r, 128, stride=48), :]

    for i in range(2):
        spot = pl.ds(pl.multiple_of(here + i * 128, 128), 128)
        for k in range(6):
            for b in range(3):
                r = 24 + i * 6 + k * 3 + b if k < 2 else i * 12 + (k - 2) * 3 + b
                at = k * 384 + b * 128
                dmod_ref[spot, at : at + 128] = line(r).astype(bf16)
        for b in range(2):
            emb_ref[spot, b * 128 : b * 128 + 128] = line(38 + i * 2 + b).astype(bf16)
        for b in range(3):
            cond_ref[spot, b * 128 : b * 128 + 128] = line(42 + i * 3 + b)
        codes = line(37)
        label = codes[:, i : i + 1] * 32.0 + codes[:, i + 2 : i + 3]
        codes_ref[spot, :] = jnp.broadcast_to(label, (128, 128)).astype(jnp.int32)
    gains_ref[...] = jnp.sum(line(36), axis=0, keepdims=True)


def lines(rows):
    return [
        ((rows, 2304), bf16),
        ((rows, 384), f32),
        ((rows, 256), bf16),
        ((rows, 128), jnp.int32),
    ]


GAINS = ((1, 128), f32)


def line_kernel(rows_ref, modw_ref, *refs):
    outs, rows_s = refs[:5], refs[5]
    pick_lines(rows_ref, rows_s, 0, *outs)


def line_call(rows, mod_w):
    return pl.pallas_call(
        line_kernel,
        in_specs=[RESIDENT] * 2,
        out_shape=[shape_of(*o) for o in lines(256) + [GAINS]],
        scratch_shapes=[pltpu.VMEM((6144, 128), f32)],
        compiler_params=params(14),
        cost_estimate=cost(100_000, 100_000),
        name="image_lines",
    )(rows, mod_w)


CONDITIONS = [(256, 384), (384, 384), (1001, 384), (384, 2304), (1, 64), (1, 64)]


def condition_kernel(at_ref, *refs):
    own, got_ref, (tw1_ref, tw2_ref, modw_ref) = refs[:5], refs[5], refs[6:9]
    stages = refs[9:15]
    whole, gains_s, rows_s = refs[15:19], refs[19], refs[20]
    tw1g, tw2g, tableg, modwg, qgain, kgain = stages
    mine = pl.ds(pl.multiple_of(at_ref[1] * 256, 256), 256)
    for ref, own_ref in zip(whole, own):
        ref[mine, :] = own_ref[...]
    pick_lines(got_ref, rows_s, (1 - at_ref[1]) * 256, *whole, gains_s)
    dmod_s, cond_s, emb_s, label_s = whole
    gain_sums = own[4][...] + gains_s[...]
    qgain[...], kgain[...] = gain_sums[:, :64], gain_sums[:, 64:]
    cond = cond_s[...]
    sig = 1.0 / (1.0 + jnp.exp(-cond))
    act_t = (cond * sig).astype(bf16).T
    for k in range(6):
        cols = slice(k * 384, k * 384 + 384)
        modwg[:, cols] = dot(act_t, dmod_s[:, cols])
    d_cond = dot_nt(dmod_s[...], modw_ref[...]) * (sig + cond * sig * (1.0 - sig))
    dc = d_cond.astype(bf16)
    label = label_s[...]
    label = jnp.concatenate([label, label], axis=1)
    for n in range(4):
        hot = jnp.where(lane_iota((512, 256)) + n * 256 == label, 1.0, 0.0).astype(bf16)
        rows = dot_tn(hot, dc)
        top = min(256, 1001 - n * 256)
        tableg[n * 256 : n * 256 + top] = rows[:top]
    emb = emb_s[...]
    pre = dot(emb, tw1_ref[...])
    sig = 1.0 / (1.0 + jnp.exp(-pre))
    hid = pre * sig
    tw2g[...] = dot_tn(hid.astype(bf16), dc)
    d_pre = (dot_nt(dc, tw2_ref[...]) * (sig + hid * (1.0 - sig))).astype(bf16)
    tw1g[...] = dot_tn(emb, d_pre)


def condition_call(at, own, got, t_w1, t_w2, mod_w):
    return pl.pallas_call(
        condition_kernel,
        grid=(1,),
        in_specs=[SCALARS] + [RESIDENT] * 9,
        out_specs=[whole_spec(v) for v in CONDITIONS],
        out_shape=[shape_of(s, f32) for s in CONDITIONS],
        scratch_shapes=[pltpu.VMEM(*o) for o in lines(512) + [GAINS, ((6144, 128), f32)]],
        compiler_params=params(36),
        cost_estimate=cost(100_000_000, 100_000),
        name="condition_gradients",
    )(at, *own, got, t_w1, t_w2, mod_w)


def place_kernel(at_ref, swaps_ref, out_in, grad_in, out_ref, grad_ref):
    out_ref[...] = swaps_ref[:, 0]
    grad_ref[...] = swaps_ref[:, 1].astype(f32)


def place_call(at, swaps, block_out, latents_grad):
    anywhere = pl.BlockSpec(memory_space=pl.ANY)
    theirs = pl.BlockSpec((2, 128, 384), lambda j, at: (1 - at[0], 0, 0))
    return pl.pallas_call(
        place_kernel,
        grid_spec=pltpu.PrefetchScalarGridSpec(
            num_scalar_prefetch=1,
            grid=(1,),
            in_specs=[whole_spec((2, 2, 128, 384)), anywhere, anywhere],
            out_specs=[theirs, theirs],
        ),
        out_shape=[shape_of((4, 128, 384), bf16), shape_of((4, 128, 384), f32)],
        input_output_aliases={2: 0, 3: 1},
        compiler_params=params(8),
        cost_estimate=cost(200_000, 1_500_000),
        name="place_swaps",
    )(at, swaps, block_out, latents_grad)


def cuts(start, chunk):
    out, at = [], start
    while at < start + 384:
        n = at // chunk
        stop = min((n + 1) * chunk, start + 384)
        out.append((n, at - n * chunk, stop - n * chunk))
        at = stop
    return out


def unpack_kernel(own, at_ref, sums_ref, *refs):
    qkv_ref, proj_ref, gu_ref, down_ref, proj_s, sem = refs[-6:]
    t = pl.program_id(0)
    half = at_ref[1] if own else 1 - at_ref[1]

    def piece(n, a, b):
        low = [sums_ref[n, a : min(b, 224)]] if a < 224 else []
        return low + ([sums_ref[16 + n, max(a, 224) - 224 : b - 224]] if b > 224 else [])

    def first(u):
        rows = [v for n, a, b in cuts(u * 384, 288) for v in piece(n, a, b)]
        return jnp.concatenate(rows).astype(f32)

    def second(u):
        rows = [v for n, a, b in cuts(u * 384, 144) for v in piece(n, 288 + a, 288 + b)]
        return jnp.concatenate(rows).astype(f32)

    proj_copy = pltpu.make_async_copy(proj_s, proj_ref, sem)
    for n in range(4):

        @pl.when(t == n)
        def _():
            for b in range(2):
                gu_ref[:, b * 128 : b * 128 + 128] = first(2 * n + b)
            rows = first(8 + n)
            for b, p in enumerate(pairs()):
                down_ref[:, p] = rows[b * 128 : b * 128 + 128]

    @pl.when((t == 0) & (half == 1))
    def _():
        for b, p in enumerate(pairs()):
            proj_s[:, p] = second(3 + b)
        proj_copy.start()

    @pl.when(t == 0)
    def _():
        for b, p in enumerate(pairs()):
            qkv_ref[:, p] = second(b)

    @pl.when((t == 2) & (half == 0))
    def _():
        for b, p in enumerate(pairs()):
            qkv_ref[:, p] = second(3 + b)

    @pl.when((t == 3) & (half == 1))
    def _():
        proj_copy.wait()


def unpack_call(own, at, sums, earlier=()):
    def half_of(at):
        return at[1] if own else 1 - at[1]

    shapes = [(384, 1152), (384, 384), (384, 2048), (1024, 384)]
    return pl.pallas_call(
        lambda *refs: unpack_kernel(own, *refs),
        grid_spec=pltpu.PrefetchScalarGridSpec(
            num_scalar_prefetch=1,
            grid=(4,),
            in_specs=[RESIDENT] + [pl.BlockSpec(memory_space=pl.ANY)] * len(earlier),
            out_specs=[
                pl.BlockSpec(
                    (384, 384), lambda t, at: (0, half_of(at) * 2 + (1 - half_of(at)) * (t >> 1))
                ),
                IN_HBM,
                pl.BlockSpec(
                    (384, 256), lambda t, at: (0, 4 * (t >> 1) + 2 * half_of(at) + (t & 1))
                ),
                pl.BlockSpec((128, 384), lambda t, at: (4 * half_of(at) + t, 0)),
            ],
            scratch_shapes=[pltpu.VMEM((384, 384), f32), pltpu.SemaphoreType.DMA],
        ),
        out_shape=[shape_of(s, f32) for s in shapes],
        input_output_aliases={2 + n: n for n in range(len(earlier))},
        compiler_params=params(20),
        cost_estimate=cost(2_000_000, 6_000_000),
        name="unpack_own" if own else "unpack_other",
    )(at, sums, *earlier)


def flat(y, z, x, c):
    return ((((y * 8 + z) * 2 + x % 2) * 2 + c) * 2) + x // 2


PLACES = [(y, z, x, c) for z, y, x, c in itertools.product(range(8), range(4), range(4), range(2))]


def groups(key):
    found = {}
    for place in PLACES:
        found.setdefault(key(*place), []).append(flat(*place))
    return list(found.values())


PLANE = groups(lambda y, z, x, c: (z // 2, c))
LAYER = groups(lambda y, z, x, c: (z, c))
RING = groups(lambda y, z, x, c: (y, x, c))


def moves(to):
    return [(flat(*place), flat(*to(*place))) for place in PLACES]


def exchange(v, lists):
    return lax.all_to_all(v, AXES, 0, 0, tiled=True, axis_index_groups=lists)


def plus(a, b):
    return (a.astype(f32) + b.astype(f32)).astype(bf16)


def column_sum(keep, send):
    v = plus(keep, lax.ppermute(send, AXES, moves(lambda y, z, x, c: (y, z ^ 1, x, c))))
    for to in (
        lambda y, z, x, c: (y, z ^ 2, x, c),
        lambda y, z, x, c: (y, (6 - (z & 6)) + (z & 1), x, c),
    ):
        v = plus(v, lax.ppermute(v, AXES, moves(to)))
    return v


BAND_SWAP = [(n, n ^ 1) for n in range(256)]
CORE_SWAP = [(n, n ^ 2) for n in range(256)]


def swap(v):
    return lax.ppermute(v, AXES, BAND_SWAP)


def core_swap(v):
    return lax.ppermute(v, AXES, CORE_SWAP)


def body(
    latents,
    pos_row,
    pos_col,
    timesteps,
    labels,
    t_w1,
    t_w2,
    label_table,
    mod_w,
    qkv_w,
    q_gain,
    k_gain,
    proj_w,
    gate_up_w,
    down_w,
    out_grad,
):
    band, img = lax.axis_index("band"), lax.axis_index("img")
    at = jnp.stack([band, img % 2, img // 4 % 2]).astype(jnp.int32)
    send, dsend = pack_call(at, latents, out_grad, pos_row, pos_col)
    got, dgot = swap(send), swap(dsend)
    mod, extra = modulation_call(at, timesteps, labels, t_w1, t_w2, label_table, mod_w)
    turn = (q_gain.reshape(1, 64), k_gain.reshape(1, 64), pos_row, pos_col, turn_table())
    q, k, v, att = forward_call(at, latents, got, mod, qkv_w, *turn)
    keep1, send1, block_out, out_send, d_mid, sums1 = mlp_call(
        at, latents, got, out_grad, dgot, att, mod, proj_w, gate_up_w, down_w
    )
    got1 = core_swap(send1)
    keep2, send2, latents_grad, swaps, sums2 = backward_call(
        at, latents, got, mod, qkv_w, *turn, q, k, v, att, d_mid, proj_w, out_send
    )
    joined = join_call(keep1, got1, keep2, core_swap(send2), sums1, sums2, extra)
    joined = exchange(joined, LAYER)
    joined, extra = lax.optimization_barrier((joined, extra_call(joined)))
    keep, send = sum_call(at, joined)
    extra = lax.all_gather(
        extra.reshape(768, 128), AXES, axis=0, tiled=True, axis_index_groups=RING
    )
    chunk = column_sum(keep, send)
    chunk, swaps = lax.optimization_barrier((chunk, swap(swaps)))
    wide = lax.optimization_barrier(jnp.broadcast_to(chunk[None], (32, 224, 128)))
    summed = exchange(wide, PLANE)
    block_out, latents_grad = place_call(at, swaps, block_out, latents_grad)
    extra, block_out, latents_grad, _ = lax.optimization_barrier(
        (extra, block_out, latents_grad, wide)
    )
    conditioned = condition_call(at, line_call(extra, mod_w), core_swap(extra), t_w1, t_w2, mod_w)
    summed, conditioned = lax.optimization_barrier((summed, conditioned))
    tw1_grad, tw2_grad, table_grad, modw_grad, q_sum, k_sum = conditioned
    sums = unpack_call(True, at, summed)
    qkv_sum, proj_sum, gu_sum, down_sum = unpack_call(False, at, core_swap(summed), sums)
    return (
        block_out,
        latents_grad,
        tw1_grad,
        tw2_grad,
        table_grad,
        modw_grad,
        qkv_sum,
        q_sum.reshape(64),
        k_sum.reshape(64),
        proj_sum,
        gu_sum,
        down_sum,
    )


def solution(mesh):
    split = P("img", "band", None)
    return jax.shard_map(
        body,
        mesh=mesh,
        in_specs=(split, P("img", "band"), P("img", "band"), P("img"), P("img"))
        + (P(),) * 10
        + (split,),
        out_specs=(split, split) + (P(),) * 10,
        check_vma=False,
    )
```

```python
import itertools
import math

import jax
import jax.numpy as jnp
from jax import lax
from jax.experimental import pallas as pl
from jax.experimental.pallas import tpu as pltpu
from jax.sharding import PartitionSpec as P
import ml_dtypes
import numpy as np

AXES = ("img", "band")
f32 = jnp.float32
bf16 = jnp.bfloat16
EPS = 1e-06
MIB = 1024 * 1024
CHUNK = 256


def dot(a, b):
    return jnp.dot(a, b, preferred_element_type=f32)


def dot_nt(a, b):
    return lax.dot_general(a, b, (((1,), (1,)), ((), ())), preferred_element_type=f32)


def dot_tn(a, b):
    return lax.dot_general(a, b, (((0,), (0,)), ((), ())), preferred_element_type=f32)


def inv_rms(v):
    return lax.rsqrt(jnp.mean(v * v, axis=-1, keepdims=True) + EPS)


def lane_iota(shape):
    return lax.broadcasted_iota(jnp.int32, shape, len(shape) - 1)


def head_mean(v):
    r = lax.broadcasted_iota(jnp.int32, (256, 256), 0) >> 6
    c = lax.broadcasted_iota(jnp.int32, (256, 256), 1) >> 6
    same = jnp.where(r == c, 1.0 / 64, 0.0).astype(bf16)
    v = v.astype(bf16)
    return jnp.concatenate(
        [dot(v[:, n : n + 256], same) for n in range(0, v.shape[1], 256)], axis=1
    )


def partner(v):
    first = (lane_iota((1, 128)) % 32) < 16
    return jnp.where(first, pltpu.roll(v, 112, 1), pltpu.roll(v, 16, 1))


def by_head(v):
    low = (lane_iota((1, 128)) < 64).astype(f32)
    return jnp.concatenate([v * low.astype(bf16), v * (1.0 - low).astype(bf16)], axis=0)


def both(at_ref, a_ref, b_ref, i):
    return jnp.concatenate([a_ref[2 * at_ref[0] + i], b_ref[i, :128]], axis=0).astype(f32)


def turns(at_ref, image, row_ref, col_ref, got, table_ref):
    here = pl.ds(2 * at_ref[0] + image, 1)
    hot = []
    for n, ref in enumerate((row_ref, col_ref)):
        kept = ref[here, :].astype(f32)
        pos = jnp.concatenate([kept, got[0:1, n * 128 : n * 128 + 128].astype(f32)], axis=1)
        spots = lax.broadcasted_iota(jnp.int32, (16, 256), 0).astype(f32)
        hot.append(jnp.where(spots == pos, 1.0, 0.0))
    hot = jnp.concatenate(hot, axis=0).astype(bf16)
    return [dot_tn(hot, table_ref[n]) + dot_tn(hot, table_ref[n + 1]) for n in (0, 2)]


def turn_table():
    lane = np.arange(128)
    rates = 10000.0 ** (-(lane % 16) / 16)
    angle = np.arange(16)[:, None] * rates
    row_lane = (lane % 64) < 32
    out = []
    for v in (np.cos(angle), np.sin(angle) * np.where(lane % 32 < 16, -1.0, 1.0)):
        v = np.concatenate([np.where(row_lane, v, 0.0), np.where(row_lane, 0.0, v)])
        high = v.astype(ml_dtypes.bfloat16)
        out += [high, (v - high.astype(np.float64)).astype(ml_dtypes.bfloat16)]
    return np.stack(out)


def pack_kernel(at_ref, lat_ref, dy_ref, row_ref, col_ref, lat_out, dy_out):
    other = 2 - 2 * at_ref[0]
    dy_out[...] = dy_ref[...]
    for i in range(2):
        lat_out[i, :128] = lat_ref[i]
        here = pl.ds(other + i, 1)
        line = jnp.concatenate(
            [row_ref[here, :].astype(f32), col_ref[here, :].astype(f32), jnp.zeros((1, 128), f32)],
            axis=1,
        )
        lat_out[i, 128:] = jnp.broadcast_to(line, (16, 384)).astype(bf16)


def split(v):
    hi = v.astype(bf16)
    return jnp.concatenate([hi, (v - hi.astype(f32)).astype(bf16)], axis=0)


def fine_dot(v, w):
    n = v.shape[0]
    out = dot(split(v), w)
    return out[:n] + out[n:]


def silu(v):
    return v / (1.0 + jnp.exp(-v))


def modulation_kernel(
    at_ref, t_ref, l_ref, tw1_ref, tw2_ref, row0_ref, row1_ref, modw_ref, mod_ref, extra_ref
):
    first = 2 * at_ref[0]
    freqs = jnp.exp(lane_iota((1, 128)).astype(f32) * (-math.log(10000.0) / 128))
    spot = lax.broadcasted_iota(jnp.int32, (16, 1), 0)
    steps = jnp.where(
        spot == 0,
        t_ref[first].astype(f32),
        jnp.where(spot == 1, t_ref[first + 1].astype(f32), 0.0),
    )
    angle = steps * freqs
    emb = jnp.concatenate([jnp.cos(angle), jnp.sin(angle)], axis=1)
    hidden = silu(fine_dot(emb, tw1_ref[...]))
    cond = fine_dot(hidden, tw2_ref[...])
    for i, ref in enumerate((row0_ref, row1_ref)):
        label = l_ref[first + i]
        row = jnp.sum(
            jnp.where(spot == (label & 15), ref[...].astype(f32), 0.0), axis=0, keepdims=True
        )
        cond = cond + jnp.where(spot == i, row, 0.0)
    mod = fine_dot(silu(cond), modw_ref[...])
    lane = lane_iota((1, 128))
    codes = jnp.zeros((1, 128), f32)
    for i in range(2):
        label = l_ref[first + i]
        codes = jnp.where(lane == i, (label >> 5).astype(f32), codes)
        codes = jnp.where(lane == 2 + i, (label & 31).astype(f32), codes)
        for k in range(6):
            mod_ref[i, k : k + 1] = mod[i : i + 1, k * 384 : k * 384 + 384]
        for b in range(2):
            extra_ref[1 + i * 2 + b : 2 + i * 2 + b] = emb[i : i + 1, b * 128 : b * 128 + 128]
        for b, p in enumerate(pairs()):
            extra_ref[5 + i * 3 + b : 6 + i * 3 + b] = cond[i : i + 1, p]
    extra_ref[0:1] = codes
    extra_ref[11:] = jnp.zeros((5, 128), f32)


def pairs(width=384):
    return [slice(j, j + 128) for j in range(0, width, 128)]


def forward_kernel(
    at_ref,
    kept_ref,
    got_ref,
    mod_ref,
    w_ref,
    qgain_ref,
    kgain_ref,
    row_ref,
    col_ref,
    table_ref,
    q_ref,
    k_ref,
    v_ref,
    att_ref,
):
    gains = [jnp.concatenate([r[...], r[...]], axis=1) for r in (qgain_ref, kgain_ref)]
    for i in range(2):
        x = both(at_ref, kept_ref, got_ref, i)
        h1 = (x * inv_rms(x) * (1.0 + mod_ref[i, 1:2]) + mod_ref[i, 0:1]).astype(bf16)
        z = dot(h1, w_ref[:, :768])
        v_ref[i] = dot(h1, w_ref[:, 768:]).astype(bf16)
        z = z * lax.rsqrt(head_mean(z * z) + EPS)
        cosine, sine = turns(at_ref, i, row_ref, col_ref, got_ref[i, 128:144], table_ref)
        for p in pairs():
            turned = []
            for part in range(2):
                n = z[:, part * 384 + p.start : part * 384 + p.stop] * gains[part]
                turned.append(n * cosine + partner(n) * sine)
            q = (turned[0].astype(bf16).astype(f32) * 0.125).astype(bf16)
            k = turned[1].astype(bf16)
            q_ref[i, :, p], k_ref[i, :, p] = q, k
            v = v_ref[i, :, p]
            e = jnp.exp(dot_nt(by_head(q), k))
            out = dot(e.astype(bf16), v) / jnp.sum(e, axis=-1, keepdims=True)
            out = jnp.where(lane_iota((1, 128)) < 64, out[:256], out[256:])
            att_ref[i * 256 : i * 256 + 256, p] = out.astype(bf16)


def mlp_kernel(
    at_ref,
    kept_ref,
    got_ref,
    dkept_ref,
    dgot_ref,
    att_ref,
    mod_ref,
    proj_ref,
    wgu_ref,
    wd_ref,
    keep_ref,
    send_ref,
    out_ref,
    outsend_ref,
    dmid_ref,
    sums_ref,
    branch_s,
    mid_s,
    h2_s,
    h2t_s,
    dmlp_s,
    mlp_s,
    dh2_s,
):
    images = range(2)

    def rows(i):
        return slice(i * 256, (i + 1) * 256)

    branch_s[...] = dot(att_ref[...], proj_ref[...])
    for i in images:
        mid = both(at_ref, kept_ref, got_ref, i) + mod_ref[i, 2:3] * branch_s[rows(i)]
        mid_s[rows(i)] = mid
        h2_s[rows(i)] = (mid * inv_rms(mid) * (1.0 + mod_ref[i, 4:5]) + mod_ref[i, 3:4]).astype(
            bf16
        )
        dmlp_s[rows(i)] = (mod_ref[i, 5:6] * both(at_ref, dkept_ref, dgot_ref, i)).astype(bf16)
    h2t_s[...] = h2_s[...].T
    h2 = h2_s[...]
    d_mlp = dmlp_s[...]
    first = True
    for ref, half in ((send_ref, 1 - at_ref[1]), (keep_ref, at_ref[1])):
        for n in range(2):
            base = half * 512 + n * CHUNK
            wg = wgu_ref[:, pl.ds(pl.multiple_of(base, CHUNK), CHUNK)]
            wu = wgu_ref[:, pl.ds(pl.multiple_of(base + 1024, CHUNK), CHUNK)]
            wd = wd_ref[pl.ds(pl.multiple_of(base, CHUNK), CHUNK), :]
            g = dot(h2, wg)
            u = dot(h2, wu)
            d_hid = dot_nt(d_mlp, wd)
            sig = 0.5 * jnp.tanh(0.5 * g) + 0.5
            act = g * sig
            hid = (act * u).astype(bf16)
            du = (d_hid * act).astype(bf16)
            dg = (d_hid * u * (sig + act * (1.0 - sig))).astype(bf16)
            mlp = dot(hid, wd)
            d_h2 = dot_nt(dg, wg) + dot_nt(du, wu)
            mlp_s[...] = mlp if first else mlp_s[...] + mlp
            dh2_s[...] = d_h2 if first else dh2_s[...] + d_h2
            first = False
            for m, d in ((0, dg), (4, du)):
                grad = dot(h2t_s[...], d).astype(bf16)
                for b in range(2):
                    ref[pl.ds((m + 2 * n + b) * 384, 384)] = grad[:, b * 128 : b * 128 + 128]
            down = dot_tn(hid, d_mlp).astype(bf16)
            for b in range(2):
                for c in range(3):
                    ref[pl.ds((8 + 2 * n + b) * 384 + c * 128, 128)] = down[
                        b * 128 : b * 128 + 128, c * 128 : c * 128 + 128
                    ]
    for i in images:
        mid, mlp, dh2 = mid_s[rows(i)], mlp_s[rows(i)], dh2_s[rows(i)]
        dy = both(at_ref, dkept_ref, dgot_ref, i)
        out = (mid + mod_ref[i, 5:6] * mlp).astype(bf16)
        out_ref[2 * at_ref[0] + i] = out[:128]
        outsend_ref[i] = out[128:]
        s = inv_rms(mid)
        n = mid * s
        e2 = dh2 * (1.0 + mod_ref[i, 4:5])
        d_mid = dy + s * (e2 - n * jnp.mean(e2 * n, axis=-1, keepdims=True))
        dmid_ref[rows(i)] = d_mid
        for k, v in enumerate((d_mid * branch_s[rows(i)], dh2, dh2 * n, dy * mlp)):
            total = jnp.sum(v, axis=0, keepdims=True)
            for b, p in enumerate(pairs()):
                sums_ref[pl.ds(i * 12 + k * 3 + b, 1)] = total[:, p]


def backward_kernel(
    at_ref,
    kept_ref,
    got_ref,
    mod_ref,
    w_ref,
    qgain_ref,
    kgain_ref,
    row_ref,
    col_ref,
    table_ref,
    q_ref,
    k_ref,
    v_ref,
    att_ref,
    dmid_ref,
    proj_ref,
    outsend_ref,
    keep_ref,
    send_ref,
    grad_ref,
    swap_ref,
    sums_ref,
    h1_s,
    dqkv_s,
    dbranch_s,
    units_s,
):
    gains = [jnp.concatenate([r[...], r[...]], axis=1) for r in (qgain_ref, kgain_ref)]
    gain_sums = [0.0, 0.0]
    for i in range(2):
        here = slice(i * 256, i * 256 + 256)
        x = both(at_ref, kept_ref, got_ref, i)
        s1 = inv_rms(x)
        n1 = x * s1
        h1 = (n1 * (1.0 + mod_ref[i, 1:2]) + mod_ref[i, 0:1]).astype(bf16)
        h1_s[here] = h1
        d_mid = dmid_ref[here]
        d_branch = (mod_ref[i, 2:3] * d_mid).astype(bf16)
        dbranch_s[here] = d_branch
        d_att = dot_nt(d_branch, proj_ref[...]).astype(bf16)
        z = dot(h1, w_ref[:, :768])
        r = lax.rsqrt(head_mean(z * z) + EPS)
        z = z * r
        cosine, sine = turns(at_ref, i, row_ref, col_ref, got_ref[i, 128:144], table_ref)
        turned = [[], []]
        for p in pairs():
            q, k, v, do = q_ref[i, :, p], k_ref[i, :, p], v_ref[i, :, p], d_att[:, p]
            q2, do2 = by_head(q), by_head(do)
            e = jnp.exp(dot_nt(k, q2))
            soft = e * (1.0 / jnp.sum(e, axis=0, keepdims=True))
            d_probs = dot_nt(v, do2)
            delta = jnp.sum(soft * d_probs, axis=0, keepdims=True)
            ds = (soft * (d_probs - delta)).astype(bf16)
            dq = dot_tn(ds, k)
            dq = jnp.where(lane_iota((1, 128)) < 64, dq[:256], dq[256:])
            dk = dot(ds, q2)
            dv = dot(soft.astype(bf16), do2)
            for part, d in enumerate((dq * 0.125, dk)):
                n = z[:, part * 384 + p.start : part * 384 + p.stop]
                dn = d * cosine - partner(d) * sine
                gain_sums[part] = gain_sums[part] + jnp.sum(dn * n, axis=0, keepdims=True)
                turned[part].append(dn * gains[part])
            dqkv_s[here, 768 + p.start : 768 + p.stop] = dv.astype(bf16)
        e = jnp.concatenate(turned[0] + turned[1], axis=1)
        dqkv_s[here, :768] = (r * (e - z * head_mean(e * z))).astype(bf16)
        d_h1 = dot_nt(dqkv_s[here], w_ref[...])
        e1 = d_h1 * (1.0 + mod_ref[i, 1:2])
        grad = d_mid + s1 * (e1 - n1 * jnp.mean(e1 * n1, axis=-1, keepdims=True))
        grad_ref[2 * at_ref[0] + i] = grad[:128]
        swap_ref[i, 0] = outsend_ref[i]
        swap_ref[i, 1] = grad[128:].astype(bf16)
        for k, v in enumerate((d_h1, d_h1 * n1)):
            total = jnp.sum(v, axis=0, keepdims=True)
            for b, p in enumerate(pairs()):
                sums_ref[pl.ds(i * 6 + k * 3 + b, 1)] = total[:, p]
    gain_sums = [g + pltpu.roll(g, 64, 1) for g in gain_sums]
    sums_ref[pl.ds(12, 1)] = jnp.where(lane_iota((1, 128)) < 64, gain_sums[0], gain_sums[1])
    sums_ref[pl.ds(13, 3)] = jnp.zeros((3, 128), f32)
    h1t = h1_s[...].T
    for part in range(3):
        w = dot(h1t, dqkv_s[:, part * 384 : part * 384 + 384]).astype(bf16)
        for b, p in enumerate(pairs()):
            n = part * 3 + b
            units_s[n // 6, pl.ds(n % 6 * 384, 384)] = w[:, p]
    w = dot_tn(att_ref[...], dbranch_s[...]).astype(bf16)
    for b, p in enumerate(pairs()):
        units_s[1, pl.ds((3 + b) * 384, 384)] = w[:, p]
    keep_ref[...] = units_s[at_ref[1]]
    send_ref[...] = units_s[1 - at_ref[1]]


def whole_spec(shape):
    return pl.BlockSpec(shape, lambda *_: (0,) * len(shape))


def params(mib):
    return pltpu.CompilerParams(vmem_limit_bytes=mib * MIB)


def shape_of(shape, dtype):
    return jax.ShapeDtypeStruct(shape, dtype)


SCALARS = pl.BlockSpec(memory_space=pltpu.SMEM)
RESIDENT = pl.BlockSpec(memory_space=pltpu.VMEM)
IN_HBM = pl.BlockSpec(memory_space=pltpu.HBM)


def cost(flops, nbytes):
    return pl.CostEstimate(flops=flops, bytes_accessed=nbytes, transcendentals=0)


def pack_call(at, latents, out_grad, pos_row, pos_col):
    theirs = pl.BlockSpec((2, 128, 384), lambda j, at: (1 - at[0], 0, 0))
    shapes = [(2, 144, 384), (2, 128, 384)]
    return pl.pallas_call(
        pack_kernel,
        grid_spec=pltpu.PrefetchScalarGridSpec(
            num_scalar_prefetch=1,
            grid=(1,),
            in_specs=[theirs, theirs, whole_spec((4, 128)), whole_spec((4, 128))],
            out_specs=[RESIDENT] * 2,
        ),
        out_shape=[shape_of(s, bf16) for s in shapes],
        compiler_params=params(56),
        cost_estimate=cost(200_000, 800_000),
        name="pack_swaps",
    )(at, latents, out_grad, pos_row, pos_col)


def modulation_call(at, timesteps, labels, t_w1, t_w2, label_table, mod_w):
    def row_spec(i):
        return pl.BlockSpec((16, 384), lambda j, at, t, l: (l[2 * at[0] + i] >> 4, 0))

    shapes = [(2, 6, 384), (16, 128)]
    return pl.pallas_call(
        modulation_kernel,
        grid_spec=pltpu.PrefetchScalarGridSpec(
            num_scalar_prefetch=3,
            grid=(1,),
            in_specs=[
                whole_spec((256, 384)),
                whole_spec((384, 384)),
                row_spec(0),
                row_spec(1),
                whole_spec((384, 2304)),
            ],
            out_specs=[RESIDENT] * 2,
        ),
        out_shape=[shape_of(s, f32) for s in shapes],
        compiler_params=params(56),
        cost_estimate=cost(1_000_000_000, 3_000_000),
        name="modulation",
    )(at, timesteps, labels, t_w1, t_w2, label_table, label_table, mod_w)


def resident_call(kernel, name, outs, estimate, mib, scratch=(), loose=(), loose_out=()):
    def spec(is_loose, shape):
        return whole_spec(shape) if is_loose else RESIDENT

    def call(at, *arrays):
        return pl.pallas_call(
            kernel,
            grid=(1,),
            in_specs=[SCALARS] + [spec(n in loose, a.shape) for n, a in enumerate(arrays)],
            out_specs=[spec(n in loose_out, o[0]) for n, o in enumerate(outs)],
            out_shape=[shape_of(*o) for o in outs],
            scratch_shapes=[pltpu.VMEM(*o) for o in scratch],
            compiler_params=params(mib),
            cost_estimate=estimate,
            name=name,
        )(at, *arrays)

    return call


forward_call = resident_call(
    forward_kernel,
    "attention_forward",
    [((2, 256, 384), bf16)] * 3 + [((512, 384), bf16)],
    cost(3_000_000_000, 4_000_000),
    12,
    loose_out=range(4),
)
mlp_call = resident_call(
    mlp_kernel,
    "mlp_both_ways",
    [
        ((4608, 128), bf16),
        ((4608, 128), bf16),
        ((4, 128, 384), bf16),
        ((2, 128, 384), bf16),
        ((512, 384), f32),
        ((24, 128), f32),
    ],
    cost(6_000_000_000, 8_000_000),
    24,
    [
        ((512, 384), f32),
        ((512, 384), f32),
        ((512, 384), bf16),
        ((384, 512), bf16),
        ((512, 384), bf16),
        ((512, 384), f32),
        ((512, 384), f32),
    ],
    loose=(4,),
    loose_out=(2, 3, 4, 5),
)
backward_call = resident_call(
    backward_kernel,
    "attention_backward",
    [
        ((2304, 128), bf16),
        ((2304, 128), bf16),
        ((4, 128, 384), f32),
        ((2, 2, 128, 384), bf16),
        ((16, 128), f32),
    ],
    cost(5_000_000_000, 6_000_000),
    24,
    [((512, 384), bf16), ((512, 1152), bf16), ((512, 384), bf16), ((2, 2304, 128), bf16)],
    loose=range(9, 16),
    loose_out=(2, 3, 4),
)


def join_kernel(
    a_ref, a_got_ref, b_ref, b_got_ref, sums1_ref, sums2_ref, extra_ref, out_ref, lines
):
    lines[:24] = sums1_ref[...]
    lines[24:40] = sums2_ref[...]
    lines[37:48] = extra_ref[:11]
    out_ref[:, :288] = (a_ref[...].astype(f32) + a_got_ref[...].astype(f32)).astype(bf16)
    out_ref[:, 288:432] = (b_ref[...].astype(f32) + b_got_ref[...].astype(f32)).astype(bf16)
    out_ref[:, 432:] = jnp.broadcast_to(lines[...].astype(bf16)[None], (16, 48, 128))


def join_call(keep1, got1, keep2, got2, *lines):
    big, small = (16, 288, 128), (16, 144, 128)
    return pl.pallas_call(
        join_kernel,
        out_shape=shape_of((16, 480, 128), bf16),
        scratch_shapes=[pltpu.VMEM((48, 128), f32)],
        compiler_params=params(14),
        cost_estimate=cost(2_000_000, 6_000_000),
        name="join_messages",
    )(keep1.reshape(big), got1.reshape(big), keep2.reshape(small), got2.reshape(small), *lines)


def extra_kernel(a_ref, out_ref):
    out_ref[...] = a_ref[:, 432:]


def extra_call(a):
    return pl.pallas_call(
        extra_kernel,
        in_specs=[RESIDENT],
        out_specs=RESIDENT,
        out_shape=shape_of((16, 48, 128), bf16),
        compiler_params=params(4),
        cost_estimate=cost(1_000, 200_000),
        name="extra_rows",
    )(a)


def sum_kernel(at_ref, a_ref, keep_ref, send_ref, total_s):
    total = a_ref[0, :432].astype(f32)
    for n in range(1, 16):
        total = total + a_ref[n, :432].astype(f32)
    total = total.astype(bf16)
    total_s[0] = total[:224]
    total_s[1, :208] = total[224:]
    total_s[1, 208:] = jnp.zeros((16, 128), bf16)
    keep_ref[...] = total_s[at_ref[2]]
    send_ref[...] = total_s[1 - at_ref[2]]


def sum_call(at, a):
    return pl.pallas_call(
        sum_kernel,
        in_specs=[SCALARS, RESIDENT],
        out_specs=[RESIDENT] * 2,
        out_shape=[shape_of((224, 128), bf16)] * 2,
        scratch_shapes=[pltpu.VMEM((2, 224, 128), bf16)],
        compiler_params=params(14),
        cost_estimate=cost(2_000_000, 3_000_000),
        name="sum_layer",
    )(at, a)


def pick_lines(rows_ref, rows_s, here, dmod_ref, cond_ref, emb_ref, codes_ref, gains_ref):
    for n in range(8):
        rows_s[pl.ds(n * 768, 768)] = rows_ref[pl.ds(n * 768, 768)].astype(f32)

    def line(r):
        return rows_s[pl.ds(r, 128, stride=48), :]

    for i in range(2):
        spot = pl.ds(pl.multiple_of(here + i * 128, 128), 128)
        for k in range(6):
            for b in range(3):
                r = 24 + i * 6 + k * 3 + b if k < 2 else i * 12 + (k - 2) * 3 + b
                at = k * 384 + b * 128
                dmod_ref[spot, at : at + 128] = line(r).astype(bf16)
        for b in range(2):
            emb_ref[spot, b * 128 : b * 128 + 128] = line(38 + i * 2 + b).astype(bf16)
        for b in range(3):
            cond_ref[spot, b * 128 : b * 128 + 128] = line(42 + i * 3 + b)
        codes = line(37)
        label = codes[:, i : i + 1] * 32.0 + codes[:, i + 2 : i + 3]
        codes_ref[spot, :] = jnp.broadcast_to(label, (128, 128)).astype(jnp.int32)
    gains_ref[...] = jnp.sum(line(36), axis=0, keepdims=True)


def lines(rows):
    return [
        ((rows, 2304), bf16),
        ((rows, 384), f32),
        ((rows, 256), bf16),
        ((rows, 128), jnp.int32),
    ]


GAINS = ((1, 128), f32)


def line_kernel(rows_ref, modw_ref, *refs):
    outs, rows_s = refs[:5], refs[5]
    pick_lines(rows_ref, rows_s, 0, *outs)


def line_call(rows, mod_w):
    return pl.pallas_call(
        line_kernel,
        in_specs=[RESIDENT] * 2,
        out_shape=[shape_of(*o) for o in lines(256) + [GAINS]],
        scratch_shapes=[pltpu.VMEM((6144, 128), f32)],
        compiler_params=params(14),
        cost_estimate=cost(100_000, 100_000),
        name="image_lines",
    )(rows, mod_w)


CONDITIONS = [(256, 384), (384, 384), (1001, 384), (384, 2304), (1, 64), (1, 64)]


def condition_kernel(at_ref, *refs):
    own, got_ref, (tw1_ref, tw2_ref, modw_ref) = refs[:5], refs[5], refs[6:9]
    stages = refs[9:15]
    whole, gains_s, rows_s = refs[15:19], refs[19], refs[20]
    tw1g, tw2g, tableg, modwg, qgain, kgain = stages
    mine = pl.ds(pl.multiple_of(at_ref[1] * 256, 256), 256)
    for ref, own_ref in zip(whole, own):
        ref[mine, :] = own_ref[...]
    pick_lines(got_ref, rows_s, (1 - at_ref[1]) * 256, *whole, gains_s)
    dmod_s, cond_s, emb_s, label_s = whole
    gain_sums = own[4][...] + gains_s[...]
    qgain[...], kgain[...] = gain_sums[:, :64], gain_sums[:, 64:]
    cond = cond_s[...]
    sig = 1.0 / (1.0 + jnp.exp(-cond))
    act_t = (cond * sig).astype(bf16).T
    for k in range(6):
        cols = slice(k * 384, k * 384 + 384)
        modwg[:, cols] = dot(act_t, dmod_s[:, cols])
    d_cond = dot_nt(dmod_s[...], modw_ref[...]) * (sig + cond * sig * (1.0 - sig))
    dc = d_cond.astype(bf16)
    label = label_s[...]
    label = jnp.concatenate([label, label], axis=1)
    for n in range(4):
        hot = jnp.where(lane_iota((512, 256)) + n * 256 == label, 1.0, 0.0).astype(bf16)
        rows = dot_tn(hot, dc)
        top = min(256, 1001 - n * 256)
        tableg[n * 256 : n * 256 + top] = rows[:top]
    emb = emb_s[...]
    pre = dot(emb, tw1_ref[...])
    sig = 1.0 / (1.0 + jnp.exp(-pre))
    hid = pre * sig
    tw2g[...] = dot_tn(hid.astype(bf16), dc)
    d_pre = (dot_nt(dc, tw2_ref[...]) * (sig + hid * (1.0 - sig))).astype(bf16)
    tw1g[...] = dot_tn(emb, d_pre)


def condition_call(at, own, got, t_w1, t_w2, mod_w):
    return pl.pallas_call(
        condition_kernel,
        grid=(1,),
        in_specs=[SCALARS] + [RESIDENT] * 9,
        out_specs=[whole_spec(v) for v in CONDITIONS],
        out_shape=[shape_of(s, f32) for s in CONDITIONS],
        scratch_shapes=[pltpu.VMEM(*o) for o in lines(512) + [GAINS, ((6144, 128), f32)]],
        compiler_params=params(36),
        cost_estimate=cost(100_000_000, 100_000),
        name="condition_gradients",
    )(at, *own, got, t_w1, t_w2, mod_w)


def place_kernel(at_ref, swaps_ref, out_in, grad_in, out_ref, grad_ref):
    out_ref[...] = swaps_ref[:, 0]
    grad_ref[...] = swaps_ref[:, 1].astype(f32)


def place_call(at, swaps, block_out, latents_grad):
    anywhere = pl.BlockSpec(memory_space=pl.ANY)
    theirs = pl.BlockSpec((2, 128, 384), lambda j, at: (1 - at[0], 0, 0))
    return pl.pallas_call(
        place_kernel,
        grid_spec=pltpu.PrefetchScalarGridSpec(
            num_scalar_prefetch=1,
            grid=(1,),
            in_specs=[whole_spec((2, 2, 128, 384)), anywhere, anywhere],
            out_specs=[theirs, theirs],
        ),
        out_shape=[shape_of((4, 128, 384), bf16), shape_of((4, 128, 384), f32)],
        input_output_aliases={2: 0, 3: 1},
        compiler_params=params(8),
        cost_estimate=cost(200_000, 1_500_000),
        name="place_swaps",
    )(at, swaps, block_out, latents_grad)


def cuts(start, chunk):
    out, at = [], start
    while at < start + 384:
        n = at // chunk
        stop = min((n + 1) * chunk, start + 384)
        out.append((n, at - n * chunk, stop - n * chunk))
        at = stop
    return out


def unpack_kernel(own, at_ref, sums_ref, *refs):
    qkv_ref, proj_ref, gu_ref, down_ref, proj_s, sem = refs[-6:]
    t = pl.program_id(0)
    half = at_ref[1] if own else 1 - at_ref[1]

    def piece(n, a, b):
        low = [sums_ref[n, a : min(b, 224)]] if a < 224 else []
        return low + ([sums_ref[16 + n, max(a, 224) - 224 : b - 224]] if b > 224 else [])

    def first(u):
        rows = [v for n, a, b in cuts(u * 384, 288) for v in piece(n, a, b)]
        return jnp.concatenate(rows).astype(f32)

    def second(u):
        rows = [v for n, a, b in cuts(u * 384, 144) for v in piece(n, 288 + a, 288 + b)]
        return jnp.concatenate(rows).astype(f32)

    proj_copy = pltpu.make_async_copy(proj_s, proj_ref, sem)
    for n in range(2):

        @pl.when(t == n)
        def _():
            for b in range(4):
                gu_ref[:, b * 128 : b * 128 + 128] = first(4 * n + b)
            for m in range(2):
                rows = first(8 + 2 * n + m)
                for b, p in enumerate(pairs()):
                    down_ref[m * 128 : m * 128 + 128, p] = rows[b * 128 : b * 128 + 128]

    @pl.when((t == 0) & (half == 1))
    def _():
        for b, p in enumerate(pairs()):
            proj_s[:, p] = second(3 + b)
        proj_copy.start()

    @pl.when(t == 0)
    def _():
        for b, p in enumerate(pairs()):
            qkv_ref[:, p] = second(b)

    @pl.when((t == 1) & (half == 0))
    def _():
        for b, p in enumerate(pairs()):
            qkv_ref[:, p] = second(3 + b)

    @pl.when((t == 1) & (half == 1))
    def _():
        proj_copy.wait()


def unpack_call(own, at, sums, earlier=()):
    def half_of(at):
        return at[1] if own else 1 - at[1]

    shapes = [(384, 1152), (384, 384), (384, 2048), (1024, 384)]
    return pl.pallas_call(
        lambda *refs: unpack_kernel(own, *refs),
        grid_spec=pltpu.PrefetchScalarGridSpec(
            num_scalar_prefetch=1,
            grid=(2,),
            in_specs=[RESIDENT] + [pl.BlockSpec(memory_space=pl.ANY)] * len(earlier),
            out_specs=[
                pl.BlockSpec(
                    (384, 384), lambda t, at: (0, half_of(at) * 2 + (1 - half_of(at)) * t)
                ),
                IN_HBM,
                pl.BlockSpec((384, 512), lambda t, at: (0, 2 * t + half_of(at))),
                pl.BlockSpec((256, 384), lambda t, at: (2 * half_of(at) + t, 0)),
            ],
            scratch_shapes=[pltpu.VMEM((384, 384), f32), pltpu.SemaphoreType.DMA],
        ),
        out_shape=[shape_of(s, f32) for s in shapes],
        input_output_aliases={2 + n: n for n in range(len(earlier))},
        compiler_params=params(20),
        cost_estimate=cost(2_000_000, 6_000_000),
        name="unpack_own" if own else "unpack_other",
    )(at, sums, *earlier)


def flat(y, z, x, c):
    return ((((y * 8 + z) * 2 + x % 2) * 2 + c) * 2) + x // 2


PLACES = [(y, z, x, c) for z, y, x, c in itertools.product(range(8), range(4), range(4), range(2))]


def groups(key):
    found = {}
    for place in PLACES:
        found.setdefault(key(*place), []).append(flat(*place))
    return list(found.values())


PLANE = groups(lambda y, z, x, c: (z // 2, c))
LAYER = groups(lambda y, z, x, c: (z, c))
RING = groups(lambda y, z, x, c: (y, x, c))


def moves(to):
    return [(flat(*place), flat(*to(*place))) for place in PLACES]


def exchange(v, lists):
    return lax.all_to_all(v, AXES, 0, 0, tiled=True, axis_index_groups=lists)


def plus(a, b):
    return (a.astype(f32) + b.astype(f32)).astype(bf16)


def column_sum(keep, send):
    v = plus(keep, lax.ppermute(send, AXES, moves(lambda y, z, x, c: (y, z ^ 1, x, c))))
    for to in (
        lambda y, z, x, c: (y, z ^ 2, x, c),
        lambda y, z, x, c: (y, (6 - (z & 6)) + (z & 1), x, c),
    ):
        v = plus(v, lax.ppermute(v, AXES, moves(to)))
    return v


BAND_SWAP = [(n, n ^ 1) for n in range(256)]
CORE_SWAP = [(n, n ^ 2) for n in range(256)]


def swap(v):
    return lax.ppermute(v, AXES, BAND_SWAP)


def core_swap(v):
    return lax.ppermute(v, AXES, CORE_SWAP)


def body(
    latents,
    pos_row,
    pos_col,
    timesteps,
    labels,
    t_w1,
    t_w2,
    label_table,
    mod_w,
    qkv_w,
    q_gain,
    k_gain,
    proj_w,
    gate_up_w,
    down_w,
    out_grad,
):
    band, img = lax.axis_index("band"), lax.axis_index("img")
    at = jnp.stack([band, img % 2, img // 4 % 2]).astype(jnp.int32)
    send, dsend = pack_call(at, latents, out_grad, pos_row, pos_col)
    got, dgot = swap(send), swap(dsend)
    mod, extra = modulation_call(at, timesteps, labels, t_w1, t_w2, label_table, mod_w)
    turn = (q_gain.reshape(1, 64), k_gain.reshape(1, 64), pos_row, pos_col, turn_table())
    q, k, v, att = forward_call(at, latents, got, mod, qkv_w, *turn)
    keep1, send1, block_out, out_send, d_mid, sums1 = mlp_call(
        at, latents, got, out_grad, dgot, att, mod, proj_w, gate_up_w, down_w
    )
    got1 = core_swap(send1)
    keep2, send2, latents_grad, swaps, sums2 = backward_call(
        at, latents, got, mod, qkv_w, *turn, q, k, v, att, d_mid, proj_w, out_send
    )
    joined = join_call(keep1, got1, keep2, core_swap(send2), sums1, sums2, extra)
    joined = exchange(joined, LAYER)
    joined, extra = lax.optimization_barrier((joined, extra_call(joined)))
    keep, send = sum_call(at, joined)
    extra = lax.all_gather(
        extra.reshape(768, 128), AXES, axis=0, tiled=True, axis_index_groups=RING
    )
    chunk = column_sum(keep, send)
    chunk, swaps = lax.optimization_barrier((chunk, swap(swaps)))
    wide = lax.optimization_barrier(jnp.broadcast_to(chunk[None], (32, 224, 128)))
    summed = exchange(wide, PLANE)
    block_out, latents_grad = place_call(at, swaps, block_out, latents_grad)
    extra, block_out, latents_grad, _ = lax.optimization_barrier(
        (extra, block_out, latents_grad, wide)
    )
    conditioned = condition_call(at, line_call(extra, mod_w), core_swap(extra), t_w1, t_w2, mod_w)
    summed, conditioned = lax.optimization_barrier((summed, conditioned))
    tw1_grad, tw2_grad, table_grad, modw_grad, q_sum, k_sum = conditioned
    sums = unpack_call(True, at, summed)
    qkv_sum, proj_sum, gu_sum, down_sum = unpack_call(False, at, core_swap(summed), sums)
    return (
        block_out,
        latents_grad,
        tw1_grad,
        tw2_grad,
        table_grad,
        modw_grad,
        qkv_sum,
        q_sum.reshape(64),
        k_sum.reshape(64),
        proj_sum,
        gu_sum,
        down_sum,
    )


def solution(mesh):
    split = P("img", "band", None)
    return jax.shard_map(
        body,
        mesh=mesh,
        in_specs=(split, P("img", "band"), P("img", "band"), P("img"), P("img"))
        + (P(),) * 10
        + (split,),
        out_specs=(split, split) + (P(),) * 10,
        check_vma=False,
    )
```

```python
import itertools
import math

import jax
import jax.numpy as jnp
from jax import lax
from jax.experimental import pallas as pl
from jax.experimental.pallas import tpu as pltpu
from jax.sharding import PartitionSpec as P
import ml_dtypes
import numpy as np

AXES = ("img", "band")
f32 = jnp.float32
bf16 = jnp.bfloat16
EPS = 1e-06
MIB = 1024 * 1024
CHUNK = 256


def dot(a, b):
    return jnp.dot(a, b, preferred_element_type=f32)


def dot_nt(a, b):
    return lax.dot_general(a, b, (((1,), (1,)), ((), ())), preferred_element_type=f32)


def dot_tn(a, b):
    return lax.dot_general(a, b, (((0,), (0,)), ((), ())), preferred_element_type=f32)


def inv_rms(v):
    return lax.rsqrt(jnp.mean(v * v, axis=-1, keepdims=True) + EPS)


def lane_iota(shape):
    return lax.broadcasted_iota(jnp.int32, shape, len(shape) - 1)


def head_mean(v):
    r = lax.broadcasted_iota(jnp.int32, (256, 256), 0) >> 6
    c = lax.broadcasted_iota(jnp.int32, (256, 256), 1) >> 6
    same = jnp.where(r == c, 1.0 / 64, 0.0).astype(bf16)
    v = v.astype(bf16)
    return jnp.concatenate(
        [dot(v[:, n : n + 256], same) for n in range(0, v.shape[1], 256)], axis=1
    )


def partner(v):
    first = (lane_iota((1, 128)) % 32) < 16
    return jnp.where(first, pltpu.roll(v, 112, 1), pltpu.roll(v, 16, 1))


def by_head(v):
    low = (lane_iota((1, 128)) < 64).astype(f32)
    return jnp.concatenate([v * low.astype(bf16), v * (1.0 - low).astype(bf16)], axis=0)


def both(at_ref, a_ref, b_ref, i):
    return jnp.concatenate([a_ref[2 * at_ref[0] + i], b_ref[i, :128]], axis=0).astype(f32)


def turns(at_ref, image, row_ref, col_ref, got, table_ref):
    here = pl.ds(2 * at_ref[0] + image, 1)
    hot = []
    for n, ref in enumerate((row_ref, col_ref)):
        kept = ref[here, :].astype(f32)
        pos = jnp.concatenate([kept, got[0:1, n * 128 : n * 128 + 128].astype(f32)], axis=1)
        spots = lax.broadcasted_iota(jnp.int32, (16, 256), 0).astype(f32)
        hot.append(jnp.where(spots == pos, 1.0, 0.0))
    hot = jnp.concatenate(hot, axis=0).astype(bf16)
    return [dot_tn(hot, table_ref[n]) + dot_tn(hot, table_ref[n + 1]) for n in (0, 2)]


def turn_table():
    lane = np.arange(128)
    rates = 10000.0 ** (-(lane % 16) / 16)
    angle = np.arange(16)[:, None] * rates
    row_lane = (lane % 64) < 32
    out = []
    for v in (np.cos(angle), np.sin(angle) * np.where(lane % 32 < 16, -1.0, 1.0)):
        v = np.concatenate([np.where(row_lane, v, 0.0), np.where(row_lane, 0.0, v)])
        high = v.astype(ml_dtypes.bfloat16)
        out += [high, (v - high.astype(np.float64)).astype(ml_dtypes.bfloat16)]
    return np.stack(out)


def pack_kernel(at_ref, lat_ref, dy_ref, row_ref, col_ref, lat_out, dy_out):
    other = 2 - 2 * at_ref[0]
    dy_out[...] = dy_ref[...]
    for i in range(2):
        lat_out[i, :128] = lat_ref[i]
        here = pl.ds(other + i, 1)
        line = jnp.concatenate(
            [row_ref[here, :].astype(f32), col_ref[here, :].astype(f32), jnp.zeros((1, 128), f32)],
            axis=1,
        )
        lat_out[i, 128:] = jnp.broadcast_to(line, (16, 384)).astype(bf16)


def split(v):
    hi = v.astype(bf16)
    return jnp.concatenate([hi, (v - hi.astype(f32)).astype(bf16)], axis=0)


def fine_dot(v, w):
    n = v.shape[0]
    out = dot(split(v), w)
    return out[:n] + out[n:]


def silu(v):
    return v / (1.0 + jnp.exp(-v))


def modulation_kernel(
    at_ref, t_ref, l_ref, tw1_ref, tw2_ref, row0_ref, row1_ref, modw_ref, mod_ref, extra_ref
):
    first = 2 * at_ref[0]
    freqs = jnp.exp(lane_iota((1, 128)).astype(f32) * (-math.log(10000.0) / 128))
    spot = lax.broadcasted_iota(jnp.int32, (16, 1), 0)
    steps = jnp.where(
        spot == 0,
        t_ref[first].astype(f32),
        jnp.where(spot == 1, t_ref[first + 1].astype(f32), 0.0),
    )
    angle = steps * freqs
    emb = jnp.concatenate([jnp.cos(angle), jnp.sin(angle)], axis=1)
    hidden = silu(fine_dot(emb, tw1_ref[...]))
    cond = fine_dot(hidden, tw2_ref[...])
    for i, ref in enumerate((row0_ref, row1_ref)):
        label = l_ref[first + i]
        row = jnp.sum(
            jnp.where(spot == (label & 15), ref[...].astype(f32), 0.0), axis=0, keepdims=True
        )
        cond = cond + jnp.where(spot == i, row, 0.0)
    mod = fine_dot(silu(cond), modw_ref[...])
    lane = lane_iota((1, 128))
    codes = jnp.zeros((1, 128), f32)
    for i in range(2):
        label = l_ref[first + i]
        codes = jnp.where(lane == i, (label >> 5).astype(f32), codes)
        codes = jnp.where(lane == 2 + i, (label & 31).astype(f32), codes)
        for k in range(6):
            mod_ref[i, k : k + 1] = mod[i : i + 1, k * 384 : k * 384 + 384]
        for b in range(2):
            extra_ref[1 + i * 2 + b : 2 + i * 2 + b] = emb[i : i + 1, b * 128 : b * 128 + 128]
        for b, p in enumerate(pairs()):
            extra_ref[5 + i * 3 + b : 6 + i * 3 + b] = cond[i : i + 1, p]
    extra_ref[0:1] = codes
    extra_ref[11:] = jnp.zeros((5, 128), f32)


def pairs(width=384):
    return [slice(j, j + 128) for j in range(0, width, 128)]


def forward_kernel(
    at_ref,
    kept_ref,
    got_ref,
    mod_ref,
    w_ref,
    qgain_ref,
    kgain_ref,
    row_ref,
    col_ref,
    table_ref,
    q_ref,
    k_ref,
    v_ref,
    att_ref,
):
    gains = [jnp.concatenate([r[...], r[...]], axis=1) for r in (qgain_ref, kgain_ref)]
    for i in range(2):
        x = both(at_ref, kept_ref, got_ref, i)
        h1 = (x * inv_rms(x) * (1.0 + mod_ref[i, 1:2]) + mod_ref[i, 0:1]).astype(bf16)
        z = dot(h1, w_ref[:, :768])
        v_ref[i] = dot(h1, w_ref[:, 768:]).astype(bf16)
        z = z * lax.rsqrt(head_mean(z * z) + EPS)
        cosine, sine = turns(at_ref, i, row_ref, col_ref, got_ref[i, 128:144], table_ref)
        for p in pairs():
            turned = []
            for part in range(2):
                n = z[:, part * 384 + p.start : part * 384 + p.stop] * gains[part]
                turned.append(n * cosine + partner(n) * sine)
            q = (turned[0].astype(bf16).astype(f32) * 0.125).astype(bf16)
            k = turned[1].astype(bf16)
            q_ref[i, :, p], k_ref[i, :, p] = q, k
            v = v_ref[i, :, p]
            e = jnp.exp(dot_nt(by_head(q), k))
            out = dot(e.astype(bf16), v) / jnp.sum(e, axis=-1, keepdims=True)
            out = jnp.where(lane_iota((1, 128)) < 64, out[:256], out[256:])
            att_ref[i * 256 : i * 256 + 256, p] = out.astype(bf16)


def mlp_kernel(
    at_ref,
    kept_ref,
    got_ref,
    dkept_ref,
    dgot_ref,
    att_ref,
    mod_ref,
    proj_ref,
    wgu_ref,
    wd_ref,
    keep_ref,
    send_ref,
    out_ref,
    outsend_ref,
    dmid_ref,
    sums_ref,
    branch_s,
    mid_s,
    h2_s,
    h2t_s,
    dmlp_s,
    mlp_s,
    dh2_s,
):
    images = range(2)

    def rows(i):
        return slice(i * 256, (i + 1) * 256)

    branch_s[...] = dot(att_ref[...], proj_ref[...])
    for i in images:
        mid = both(at_ref, kept_ref, got_ref, i) + mod_ref[i, 2:3] * branch_s[rows(i)]
        mid_s[rows(i)] = mid
        h2_s[rows(i)] = (mid * inv_rms(mid) * (1.0 + mod_ref[i, 4:5]) + mod_ref[i, 3:4]).astype(
            bf16
        )
        dmlp_s[rows(i)] = (mod_ref[i, 5:6] * both(at_ref, dkept_ref, dgot_ref, i)).astype(bf16)
    h2t_s[...] = h2_s[...].T
    h2 = h2_s[...]
    d_mlp = dmlp_s[...]
    first = True
    for ref, half in ((send_ref, 1 - at_ref[1]), (keep_ref, at_ref[1])):
        for n in range(2):
            base = half * 512 + n * CHUNK
            wg = wgu_ref[:, pl.ds(pl.multiple_of(base, CHUNK), CHUNK)]
            wu = wgu_ref[:, pl.ds(pl.multiple_of(base + 1024, CHUNK), CHUNK)]
            wd = wd_ref[pl.ds(pl.multiple_of(base, CHUNK), CHUNK), :]
            g = dot(h2, wg)
            u = dot(h2, wu)
            d_hid = dot_nt(d_mlp, wd)
            sig = 0.5 * jnp.tanh(0.5 * g) + 0.5
            act = g * sig
            hid = (act * u).astype(bf16)
            du = (d_hid * act).astype(bf16)
            dg = (d_hid * u * (sig + act * (1.0 - sig))).astype(bf16)
            mlp = dot(hid, wd)
            d_h2 = dot_nt(dg, wg) + dot_nt(du, wu)
            mlp_s[...] = mlp if first else mlp_s[...] + mlp
            dh2_s[...] = d_h2 if first else dh2_s[...] + d_h2
            first = False
            for m, d in ((0, dg), (4, du)):
                grad = dot(h2t_s[...], d).astype(bf16)
                for b in range(2):
                    ref[pl.ds((m + 2 * n + b) * 384, 384)] = grad[:, b * 128 : b * 128 + 128]
            down = dot_tn(hid, d_mlp).astype(bf16)
            for b in range(2):
                for c in range(3):
                    ref[pl.ds((8 + 2 * n + b) * 384 + c * 128, 128)] = down[
                        b * 128 : b * 128 + 128, c * 128 : c * 128 + 128
                    ]
    for i in images:
        mid, mlp, dh2 = mid_s[rows(i)], mlp_s[rows(i)], dh2_s[rows(i)]
        dy = both(at_ref, dkept_ref, dgot_ref, i)
        out = (mid + mod_ref[i, 5:6] * mlp).astype(bf16)
        out_ref[2 * at_ref[0] + i] = out[:128]
        outsend_ref[i] = out[128:]
        s = inv_rms(mid)
        n = mid * s
        e2 = dh2 * (1.0 + mod_ref[i, 4:5])
        d_mid = dy + s * (e2 - n * jnp.mean(e2 * n, axis=-1, keepdims=True))
        dmid_ref[rows(i)] = d_mid
        for k, v in enumerate((d_mid * branch_s[rows(i)], dh2, dh2 * n, dy * mlp)):
            total = jnp.sum(v, axis=0, keepdims=True)
            for b, p in enumerate(pairs()):
                sums_ref[pl.ds(i * 12 + k * 3 + b, 1)] = total[:, p]


def backward_kernel(
    at_ref,
    kept_ref,
    got_ref,
    mod_ref,
    w_ref,
    qgain_ref,
    kgain_ref,
    row_ref,
    col_ref,
    table_ref,
    q_ref,
    k_ref,
    v_ref,
    att_ref,
    dmid_ref,
    proj_ref,
    outsend_ref,
    keep_ref,
    send_ref,
    grad_ref,
    swap_ref,
    sums_ref,
    h1_s,
    dqkv_s,
    dbranch_s,
    units_s,
):
    gains = [jnp.concatenate([r[...], r[...]], axis=1) for r in (qgain_ref, kgain_ref)]
    gain_sums = [0.0, 0.0]
    for i in range(2):
        here = slice(i * 256, i * 256 + 256)
        x = both(at_ref, kept_ref, got_ref, i)
        s1 = inv_rms(x)
        n1 = x * s1
        h1 = (n1 * (1.0 + mod_ref[i, 1:2]) + mod_ref[i, 0:1]).astype(bf16)
        h1_s[here] = h1
        d_mid = dmid_ref[here]
        d_branch = (mod_ref[i, 2:3] * d_mid).astype(bf16)
        dbranch_s[here] = d_branch
        d_att = dot_nt(d_branch, proj_ref[...]).astype(bf16)
        z = dot(h1, w_ref[:, :768])
        r = lax.rsqrt(head_mean(z * z) + EPS)
        z = z * r
        cosine, sine = turns(at_ref, i, row_ref, col_ref, got_ref[i, 128:144], table_ref)
        turned = [[], []]
        for p in pairs():
            q, k, v, do = q_ref[i, :, p], k_ref[i, :, p], v_ref[i, :, p], d_att[:, p]
            q2, do2 = by_head(q), by_head(do)
            e = jnp.exp(dot_nt(k, q2))
            soft = e * (1.0 / jnp.sum(e, axis=0, keepdims=True))
            d_probs = dot_nt(v, do2)
            delta = jnp.sum(soft * d_probs, axis=0, keepdims=True)
            ds = (soft * (d_probs - delta)).astype(bf16)
            dq = dot_tn(ds, k)
            dq = jnp.where(lane_iota((1, 128)) < 64, dq[:256], dq[256:])
            dk = dot(ds, q2)
            dv = dot(soft.astype(bf16), do2)
            for part, d in enumerate((dq * 0.125, dk)):
                n = z[:, part * 384 + p.start : part * 384 + p.stop]
                dn = d * cosine - partner(d) * sine
                gain_sums[part] = gain_sums[part] + jnp.sum(dn * n, axis=0, keepdims=True)
                turned[part].append(dn * gains[part])
            dqkv_s[here, 768 + p.start : 768 + p.stop] = dv.astype(bf16)
        e = jnp.concatenate(turned[0] + turned[1], axis=1)
        dqkv_s[here, :768] = (r * (e - z * head_mean(e * z))).astype(bf16)
        d_h1 = dot_nt(dqkv_s[here], w_ref[...])
        e1 = d_h1 * (1.0 + mod_ref[i, 1:2])
        grad = d_mid + s1 * (e1 - n1 * jnp.mean(e1 * n1, axis=-1, keepdims=True))
        grad_ref[2 * at_ref[0] + i] = grad[:128]
        swap_ref[i, 0] = outsend_ref[i]
        swap_ref[i, 1] = grad[128:].astype(bf16)
        for k, v in enumerate((d_h1, d_h1 * n1)):
            total = jnp.sum(v, axis=0, keepdims=True)
            for b, p in enumerate(pairs()):
                sums_ref[pl.ds(i * 6 + k * 3 + b, 1)] = total[:, p]
    gain_sums = [g + pltpu.roll(g, 64, 1) for g in gain_sums]
    sums_ref[pl.ds(12, 1)] = jnp.where(lane_iota((1, 128)) < 64, gain_sums[0], gain_sums[1])
    sums_ref[pl.ds(13, 3)] = jnp.zeros((3, 128), f32)
    h1t = h1_s[...].T
    for part in range(3):
        w = dot(h1t, dqkv_s[:, part * 384 : part * 384 + 384]).astype(bf16)
        for b, p in enumerate(pairs()):
            n = part * 3 + b
            units_s[n // 6, pl.ds(n % 6 * 384, 384)] = w[:, p]
    w = dot_tn(att_ref[...], dbranch_s[...]).astype(bf16)
    for b, p in enumerate(pairs()):
        units_s[1, pl.ds((3 + b) * 384, 384)] = w[:, p]
    keep_ref[...] = units_s[at_ref[1]]
    send_ref[...] = units_s[1 - at_ref[1]]


def whole_spec(shape):
    return pl.BlockSpec(shape, lambda *_: (0,) * len(shape))


def params(mib):
    return pltpu.CompilerParams(vmem_limit_bytes=mib * MIB)


def shape_of(shape, dtype):
    return jax.ShapeDtypeStruct(shape, dtype)


SCALARS = pl.BlockSpec(memory_space=pltpu.SMEM)
RESIDENT = pl.BlockSpec(memory_space=pltpu.VMEM)
IN_HBM = pl.BlockSpec(memory_space=pltpu.HBM)


def cost(flops, nbytes):
    return pl.CostEstimate(flops=flops, bytes_accessed=nbytes, transcendentals=0)


def pack_call(at, latents, out_grad, pos_row, pos_col):
    theirs = pl.BlockSpec((2, 128, 384), lambda j, at: (1 - at[0], 0, 0))
    shapes = [(2, 144, 384), (2, 128, 384)]
    return pl.pallas_call(
        pack_kernel,
        grid_spec=pltpu.PrefetchScalarGridSpec(
            num_scalar_prefetch=1,
            grid=(1,),
            in_specs=[theirs, theirs, whole_spec((4, 128)), whole_spec((4, 128))],
            out_specs=[RESIDENT] * 2,
        ),
        out_shape=[shape_of(s, bf16) for s in shapes],
        compiler_params=params(56),
        cost_estimate=cost(200_000, 800_000),
        name="pack_swaps",
    )(at, latents, out_grad, pos_row, pos_col)


def modulation_call(at, timesteps, labels, t_w1, t_w2, label_table, mod_w):
    def row_spec(i):
        return pl.BlockSpec((16, 384), lambda j, at, t, l: (l[2 * at[0] + i] >> 4, 0))

    shapes = [(2, 6, 384), (16, 128)]
    return pl.pallas_call(
        modulation_kernel,
        grid_spec=pltpu.PrefetchScalarGridSpec(
            num_scalar_prefetch=3,
            grid=(1,),
            in_specs=[
                whole_spec((256, 384)),
                whole_spec((384, 384)),
                row_spec(0),
                row_spec(1),
                whole_spec((384, 2304)),
            ],
            out_specs=[RESIDENT] * 2,
        ),
        out_shape=[shape_of(s, f32) for s in shapes],
        compiler_params=params(56),
        cost_estimate=cost(1_000_000_000, 3_000_000),
        name="modulation",
    )(at, timesteps, labels, t_w1, t_w2, label_table, label_table, mod_w)


def resident_call(kernel, name, outs, estimate, mib, scratch=(), loose=(), loose_out=()):
    def spec(is_loose, shape):
        return whole_spec(shape) if is_loose else RESIDENT

    def call(at, *arrays):
        return pl.pallas_call(
            kernel,
            grid=(1,),
            in_specs=[SCALARS] + [spec(n in loose, a.shape) for n, a in enumerate(arrays)],
            out_specs=[spec(n in loose_out, o[0]) for n, o in enumerate(outs)],
            out_shape=[shape_of(*o) for o in outs],
            scratch_shapes=[pltpu.VMEM(*o) for o in scratch],
            compiler_params=params(mib),
            cost_estimate=estimate,
            name=name,
        )(at, *arrays)

    return call


def relay_kernel(mod_ref, out_ref):
    out_ref[...] = mod_ref[...]


def relay_call(mod):
    return pl.pallas_call(
        relay_kernel,
        in_specs=[RESIDENT],
        out_specs=RESIDENT,
        out_shape=shape_of((2, 6, 384), f32),
        compiler_params=params(2),
        cost_estimate=cost(1_000, 40_000),
        name="relay_modulation",
    )(mod)


forward_call = resident_call(
    forward_kernel,
    "attention_forward",
    [((2, 256, 384), bf16)] * 3 + [((512, 384), bf16)],
    cost(3_000_000_000, 4_000_000),
    12,
    loose_out=range(4),
)
mlp_call = resident_call(
    mlp_kernel,
    "mlp_both_ways",
    [
        ((4608, 128), bf16),
        ((4608, 128), bf16),
        ((4, 128, 384), bf16),
        ((2, 128, 384), bf16),
        ((512, 384), f32),
        ((24, 128), f32),
    ],
    cost(6_000_000_000, 8_000_000),
    24,
    [
        ((512, 384), f32),
        ((512, 384), f32),
        ((512, 384), bf16),
        ((384, 512), bf16),
        ((512, 384), bf16),
        ((512, 384), f32),
        ((512, 384), f32),
    ],
    loose=(4,),
    loose_out=(2, 3, 4, 5),
)
backward_call = resident_call(
    backward_kernel,
    "attention_backward",
    [
        ((2304, 128), bf16),
        ((2304, 128), bf16),
        ((4, 128, 384), f32),
        ((2, 2, 128, 384), bf16),
        ((16, 128), f32),
    ],
    cost(5_000_000_000, 6_000_000),
    24,
    [((512, 384), bf16), ((512, 1152), bf16), ((512, 384), bf16), ((2, 2304, 128), bf16)],
    loose=range(9, 16),
    loose_out=(2, 3, 4),
)


def join_kernel(
    a_ref, a_got_ref, b_ref, b_got_ref, sums1_ref, sums2_ref, extra_ref, out_ref, lines
):
    lines[:24] = sums1_ref[...]
    lines[24:40] = sums2_ref[...]
    lines[37:48] = extra_ref[:11]
    out_ref[:, :288] = (a_ref[...].astype(f32) + a_got_ref[...].astype(f32)).astype(bf16)
    out_ref[:, 288:432] = (b_ref[...].astype(f32) + b_got_ref[...].astype(f32)).astype(bf16)
    out_ref[:, 432:] = jnp.broadcast_to(lines[...].astype(bf16)[None], (16, 48, 128))


def join_call(keep1, got1, keep2, got2, *lines):
    big, small = (16, 288, 128), (16, 144, 128)
    return pl.pallas_call(
        join_kernel,
        out_shape=shape_of((16, 480, 128), bf16),
        scratch_shapes=[pltpu.VMEM((48, 128), f32)],
        compiler_params=params(14),
        cost_estimate=cost(2_000_000, 6_000_000),
        name="join_messages",
    )(keep1.reshape(big), got1.reshape(big), keep2.reshape(small), got2.reshape(small), *lines)


def extra_kernel(a_ref, out_ref):
    out_ref[...] = a_ref[:, 432:]


def extra_call(a):
    return pl.pallas_call(
        extra_kernel,
        in_specs=[RESIDENT],
        out_specs=RESIDENT,
        out_shape=shape_of((16, 48, 128), bf16),
        compiler_params=params(4),
        cost_estimate=cost(1_000, 200_000),
        name="extra_rows",
    )(a)


def sum_kernel(at_ref, a_ref, keep_ref, send_ref, total_s):
    total = a_ref[0, :432].astype(f32)
    for n in range(1, 16):
        total = total + a_ref[n, :432].astype(f32)
    total = total.astype(bf16)
    total_s[0] = total[:224]
    total_s[1, :208] = total[224:]
    total_s[1, 208:] = jnp.zeros((16, 128), bf16)
    keep_ref[...] = total_s[at_ref[2]]
    send_ref[...] = total_s[1 - at_ref[2]]


def sum_call(at, a):
    return pl.pallas_call(
        sum_kernel,
        in_specs=[SCALARS, RESIDENT],
        out_specs=[RESIDENT] * 2,
        out_shape=[shape_of((224, 128), bf16)] * 2,
        scratch_shapes=[pltpu.VMEM((2, 224, 128), bf16)],
        compiler_params=params(14),
        cost_estimate=cost(2_000_000, 3_000_000),
        name="sum_layer",
    )(at, a)


def pick_lines(rows_ref, rows_s, here, dmod_ref, cond_ref, emb_ref, codes_ref, gains_ref):
    for n in range(8):
        rows_s[pl.ds(n * 768, 768)] = rows_ref[pl.ds(n * 768, 768)].astype(f32)

    def line(r):
        return rows_s[pl.ds(r, 128, stride=48), :]

    for i in range(2):
        spot = pl.ds(pl.multiple_of(here + i * 128, 128), 128)
        for k in range(6):
            for b in range(3):
                r = 24 + i * 6 + k * 3 + b if k < 2 else i * 12 + (k - 2) * 3 + b
                at = k * 384 + b * 128
                dmod_ref[spot, at : at + 128] = line(r).astype(bf16)
        for b in range(2):
            emb_ref[spot, b * 128 : b * 128 + 128] = line(38 + i * 2 + b).astype(bf16)
        for b in range(3):
            cond_ref[spot, b * 128 : b * 128 + 128] = line(42 + i * 3 + b)
        codes = line(37)
        label = codes[:, i : i + 1] * 32.0 + codes[:, i + 2 : i + 3]
        codes_ref[spot, :] = jnp.broadcast_to(label, (128, 128)).astype(jnp.int32)
    gains_ref[...] = jnp.sum(line(36), axis=0, keepdims=True)


def lines(rows):
    return [
        ((rows, 2304), bf16),
        ((rows, 384), f32),
        ((rows, 256), bf16),
        ((rows, 128), jnp.int32),
    ]


GAINS = ((1, 128), f32)


def line_kernel(rows_ref, modw_ref, *refs):
    outs, rows_s = refs[:5], refs[5]
    pick_lines(rows_ref, rows_s, 0, *outs)


def line_call(rows, mod_w):
    return pl.pallas_call(
        line_kernel,
        in_specs=[RESIDENT] * 2,
        out_shape=[shape_of(*o) for o in lines(256) + [GAINS]],
        scratch_shapes=[pltpu.VMEM((6144, 128), f32)],
        compiler_params=params(14),
        cost_estimate=cost(100_000, 100_000),
        name="image_lines",
    )(rows, mod_w)


CONDITIONS = [(256, 384), (384, 384), (1001, 384), (384, 2304), (1, 64), (1, 64)]


def condition_kernel(at_ref, *refs):
    own, got_ref, (tw1_ref, tw2_ref, modw_ref) = refs[:5], refs[5], refs[6:9]
    stages = refs[9:15]
    whole, gains_s, rows_s = refs[15:19], refs[19], refs[20]
    tw1g, tw2g, tableg, modwg, qgain, kgain = stages
    mine = pl.ds(pl.multiple_of(at_ref[1] * 256, 256), 256)
    for ref, own_ref in zip(whole, own):
        ref[mine, :] = own_ref[...]
    pick_lines(got_ref, rows_s, (1 - at_ref[1]) * 256, *whole, gains_s)
    dmod_s, cond_s, emb_s, label_s = whole
    gain_sums = own[4][...] + gains_s[...]
    qgain[...], kgain[...] = gain_sums[:, :64], gain_sums[:, 64:]
    cond = cond_s[...]
    sig = 1.0 / (1.0 + jnp.exp(-cond))
    act_t = (cond * sig).astype(bf16).T
    for k in range(6):
        cols = slice(k * 384, k * 384 + 384)
        modwg[:, cols] = dot(act_t, dmod_s[:, cols])
    d_cond = dot_nt(dmod_s[...], modw_ref[...]) * (sig + cond * sig * (1.0 - sig))
    dc = d_cond.astype(bf16)
    label = label_s[...]
    label = jnp.concatenate([label, label], axis=1)
    for n in range(4):
        hot = jnp.where(lane_iota((512, 256)) + n * 256 == label, 1.0, 0.0).astype(bf16)
        rows = dot_tn(hot, dc)
        top = min(256, 1001 - n * 256)
        tableg[n * 256 : n * 256 + top] = rows[:top]
    emb = emb_s[...]
    pre = dot(emb, tw1_ref[...])
    sig = 1.0 / (1.0 + jnp.exp(-pre))
    hid = pre * sig
    tw2g[...] = dot_tn(hid.astype(bf16), dc)
    d_pre = (dot_nt(dc, tw2_ref[...]) * (sig + hid * (1.0 - sig))).astype(bf16)
    tw1g[...] = dot_tn(emb, d_pre)


def condition_call(at, own, got, t_w1, t_w2, mod_w):
    return pl.pallas_call(
        condition_kernel,
        grid=(1,),
        in_specs=[SCALARS] + [RESIDENT] * 9,
        out_specs=[whole_spec(v) for v in CONDITIONS],
        out_shape=[shape_of(s, f32) for s in CONDITIONS],
        scratch_shapes=[pltpu.VMEM(*o) for o in lines(512) + [GAINS, ((6144, 128), f32)]],
        compiler_params=params(36),
        cost_estimate=cost(100_000_000, 100_000),
        name="condition_gradients",
    )(at, *own, got, t_w1, t_w2, mod_w)


def place_kernel(at_ref, swaps_ref, out_in, grad_in, out_ref, grad_ref):
    out_ref[...] = swaps_ref[:, 0]
    grad_ref[...] = swaps_ref[:, 1].astype(f32)


def place_call(at, swaps, block_out, latents_grad):
    anywhere = pl.BlockSpec(memory_space=pl.ANY)
    theirs = pl.BlockSpec((2, 128, 384), lambda j, at: (1 - at[0], 0, 0))
    return pl.pallas_call(
        place_kernel,
        grid_spec=pltpu.PrefetchScalarGridSpec(
            num_scalar_prefetch=1,
            grid=(1,),
            in_specs=[whole_spec((2, 2, 128, 384)), anywhere, anywhere],
            out_specs=[theirs, theirs],
        ),
        out_shape=[shape_of((4, 128, 384), bf16), shape_of((4, 128, 384), f32)],
        input_output_aliases={2: 0, 3: 1},
        compiler_params=params(8),
        cost_estimate=cost(200_000, 1_500_000),
        name="place_swaps",
    )(at, swaps, block_out, latents_grad)


def cuts(start, chunk):
    out, at = [], start
    while at < start + 384:
        n = at // chunk
        stop = min((n + 1) * chunk, start + 384)
        out.append((n, at - n * chunk, stop - n * chunk))
        at = stop
    return out


def unpack_kernel(own, at_ref, sums_ref, *refs):
    qkv_ref, proj_ref, gu_ref, down_ref, proj_s, sem = refs[-6:]
    t = pl.program_id(0)
    half = at_ref[1] if own else 1 - at_ref[1]

    def piece(n, a, b):
        low = [sums_ref[n, a : min(b, 224)]] if a < 224 else []
        return low + ([sums_ref[16 + n, max(a, 224) - 224 : b - 224]] if b > 224 else [])

    def first(u):
        rows = [v for n, a, b in cuts(u * 384, 288) for v in piece(n, a, b)]
        return jnp.concatenate(rows).astype(f32)

    def second(u):
        rows = [v for n, a, b in cuts(u * 384, 144) for v in piece(n, 288 + a, 288 + b)]
        return jnp.concatenate(rows).astype(f32)

    proj_copy = pltpu.make_async_copy(proj_s, proj_ref, sem)
    for n in range(2):

        @pl.when(t == n)
        def _():
            for b in range(4):
                gu_ref[:, b * 128 : b * 128 + 128] = first(4 * n + b)
            for m in range(2):
                rows = first(8 + 2 * n + m)
                for b, p in enumerate(pairs()):
                    down_ref[m * 128 : m * 128 + 128, p] = rows[b * 128 : b * 128 + 128]

    @pl.when((t == 0) & (half == 1))
    def _():
        for b, p in enumerate(pairs()):
            proj_s[:, p] = second(3 + b)
        proj_copy.start()

    @pl.when(t == 0)
    def _():
        for b, p in enumerate(pairs()):
            qkv_ref[:, p] = second(b)

    @pl.when((t == 1) & (half == 0))
    def _():
        for b, p in enumerate(pairs()):
            qkv_ref[:, p] = second(3 + b)

    @pl.when((t == 1) & (half == 1))
    def _():
        proj_copy.wait()


def unpack_call(own, at, sums, earlier=()):
    def half_of(at):
        return at[1] if own else 1 - at[1]

    shapes = [(384, 1152), (384, 384), (384, 2048), (1024, 384)]
    return pl.pallas_call(
        lambda *refs: unpack_kernel(own, *refs),
        grid_spec=pltpu.PrefetchScalarGridSpec(
            num_scalar_prefetch=1,
            grid=(2,),
            in_specs=[RESIDENT] + [pl.BlockSpec(memory_space=pl.ANY)] * len(earlier),
            out_specs=[
                pl.BlockSpec(
                    (384, 384), lambda t, at: (0, half_of(at) * 2 + (1 - half_of(at)) * t)
                ),
                IN_HBM,
                pl.BlockSpec((384, 512), lambda t, at: (0, 2 * t + half_of(at))),
                pl.BlockSpec((256, 384), lambda t, at: (2 * half_of(at) + t, 0)),
            ],
            scratch_shapes=[pltpu.VMEM((384, 384), f32), pltpu.SemaphoreType.DMA],
        ),
        out_shape=[shape_of(s, f32) for s in shapes],
        input_output_aliases={2 + n: n for n in range(len(earlier))},
        compiler_params=params(20),
        cost_estimate=cost(2_000_000, 6_000_000),
        name="unpack_own" if own else "unpack_other",
    )(at, sums, *earlier)


def flat(y, z, x, c):
    return ((((y * 8 + z) * 2 + x % 2) * 2 + c) * 2) + x // 2


PLACES = [(y, z, x, c) for z, y, x, c in itertools.product(range(8), range(4), range(4), range(2))]


def groups(key):
    found = {}
    for place in PLACES:
        found.setdefault(key(*place), []).append(flat(*place))
    return list(found.values())


PLANE = groups(lambda y, z, x, c: (z // 2, c))
LAYER = groups(lambda y, z, x, c: (z, c))
RING = groups(lambda y, z, x, c: (y, x, c))


def moves(to):
    return [(flat(*place), flat(*to(*place))) for place in PLACES]


def exchange(v, lists):
    return lax.all_to_all(v, AXES, 0, 0, tiled=True, axis_index_groups=lists)


def plus(a, b):
    return (a.astype(f32) + b.astype(f32)).astype(bf16)


def column_sum(keep, send):
    v = plus(keep, lax.ppermute(send, AXES, moves(lambda y, z, x, c: (y, z ^ 1, x, c))))
    for to in (
        lambda y, z, x, c: (y, z ^ 2, x, c),
        lambda y, z, x, c: (y, (6 - (z & 6)) + (z & 1), x, c),
    ):
        v = plus(v, lax.ppermute(v, AXES, moves(to)))
    return v


BAND_SWAP = [(n, n ^ 1) for n in range(256)]
CORE_SWAP = [(n, n ^ 2) for n in range(256)]


def swap(v):
    return lax.ppermute(v, AXES, BAND_SWAP)


def core_swap(v):
    return lax.ppermute(v, AXES, CORE_SWAP)


def body(
    latents,
    pos_row,
    pos_col,
    timesteps,
    labels,
    t_w1,
    t_w2,
    label_table,
    mod_w,
    qkv_w,
    q_gain,
    k_gain,
    proj_w,
    gate_up_w,
    down_w,
    out_grad,
):
    band, img = lax.axis_index("band"), lax.axis_index("img")
    at = jnp.stack([band, img % 2, img // 4 % 2]).astype(jnp.int32)
    send, dsend = pack_call(at, latents, out_grad, pos_row, pos_col)
    got, dgot = swap(send), swap(dsend)
    mod, extra = modulation_call(at, timesteps, labels, t_w1, t_w2, label_table, mod_w)
    mod = relay_call(mod)
    turn = (q_gain.reshape(1, 64), k_gain.reshape(1, 64), pos_row, pos_col, turn_table())
    q, k, v, att = forward_call(at, latents, got, mod, qkv_w, *turn)
    keep1, send1, block_out, out_send, d_mid, sums1 = mlp_call(
        at, latents, got, out_grad, dgot, att, mod, proj_w, gate_up_w, down_w
    )
    got1 = core_swap(send1)
    keep2, send2, latents_grad, swaps, sums2 = backward_call(
        at, latents, got, mod, qkv_w, *turn, q, k, v, att, d_mid, proj_w, out_send
    )
    joined = join_call(keep1, got1, keep2, core_swap(send2), sums1, sums2, extra)
    joined = exchange(joined, LAYER)
    joined, extra = lax.optimization_barrier((joined, extra_call(joined)))
    keep, send = sum_call(at, joined)
    extra = lax.all_gather(
        extra.reshape(768, 128), AXES, axis=0, tiled=True, axis_index_groups=RING
    )
    chunk = column_sum(keep, send)
    chunk, swaps = lax.optimization_barrier((chunk, swap(swaps)))
    wide = lax.optimization_barrier(jnp.broadcast_to(chunk[None], (32, 224, 128)))
    summed = exchange(wide, PLANE)
    block_out, latents_grad = place_call(at, swaps, block_out, latents_grad)
    extra, block_out, latents_grad, _ = lax.optimization_barrier(
        (extra, block_out, latents_grad, wide)
    )
    conditioned = condition_call(at, line_call(extra, mod_w), core_swap(extra), t_w1, t_w2, mod_w)
    summed, conditioned = lax.optimization_barrier((summed, conditioned))
    tw1_grad, tw2_grad, table_grad, modw_grad, q_sum, k_sum = conditioned
    sums = unpack_call(True, at, summed)
    qkv_sum, proj_sum, gu_sum, down_sum = unpack_call(False, at, core_swap(summed), sums)
    return (
        block_out,
        latents_grad,
        tw1_grad,
        tw2_grad,
        table_grad,
        modw_grad,
        qkv_sum,
        q_sum.reshape(64),
        k_sum.reshape(64),
        proj_sum,
        gu_sum,
        down_sum,
    )


def solution(mesh):
    split = P("img", "band", None)
    return jax.shard_map(
        body,
        mesh=mesh,
        in_specs=(split, P("img", "band"), P("img", "band"), P("img"), P("img"))
        + (P(),) * 10
        + (split,),
        out_specs=(split, split) + (P(),) * 10,
        check_vma=False,
    )
```

```python
import itertools
import math

import jax
import jax.numpy as jnp
from jax import lax
from jax.experimental import pallas as pl
from jax.experimental.pallas import tpu as pltpu
from jax.sharding import PartitionSpec as P
import ml_dtypes
import numpy as np

AXES = ("img", "band")
f32 = jnp.float32
bf16 = jnp.bfloat16
EPS = 1e-06
MIB = 1024 * 1024
CHUNK = 256


def dot(a, b):
    return jnp.dot(a, b, preferred_element_type=f32)


def dot_nt(a, b):
    return lax.dot_general(a, b, (((1,), (1,)), ((), ())), preferred_element_type=f32)


def dot_tn(a, b):
    return lax.dot_general(a, b, (((0,), (0,)), ((), ())), preferred_element_type=f32)


def inv_rms(v):
    return lax.rsqrt(jnp.mean(v * v, axis=-1, keepdims=True) + EPS)


def lane_iota(shape):
    return lax.broadcasted_iota(jnp.int32, shape, len(shape) - 1)


def head_mean(v):
    r = lax.broadcasted_iota(jnp.int32, (256, 256), 0) >> 6
    c = lax.broadcasted_iota(jnp.int32, (256, 256), 1) >> 6
    same = jnp.where(r == c, 1.0 / 64, 0.0).astype(bf16)
    v = v.astype(bf16)
    return jnp.concatenate(
        [dot(v[:, n : n + 256], same) for n in range(0, v.shape[1], 256)], axis=1
    )


def partner(v):
    first = (lane_iota((1, 128)) % 32) < 16
    return jnp.where(first, pltpu.roll(v, 112, 1), pltpu.roll(v, 16, 1))


def by_head(v):
    low = (lane_iota((1, 128)) < 64).astype(f32)
    return jnp.concatenate([v * low.astype(bf16), v * (1.0 - low).astype(bf16)], axis=0)


def both(at_ref, a_ref, b_ref, i):
    return jnp.concatenate([a_ref[2 * at_ref[0] + i], b_ref[i, :128]], axis=0).astype(f32)


def turns(at_ref, image, row_ref, col_ref, got, table_ref):
    here = pl.ds(2 * at_ref[0] + image, 1)
    hot = []
    for n, ref in enumerate((row_ref, col_ref)):
        kept = ref[here, :].astype(f32)
        pos = jnp.concatenate([kept, got[0:1, n * 128 : n * 128 + 128].astype(f32)], axis=1)
        spots = lax.broadcasted_iota(jnp.int32, (16, 256), 0).astype(f32)
        hot.append(jnp.where(spots == pos, 1.0, 0.0))
    hot = jnp.concatenate(hot, axis=0).astype(bf16)
    return [dot_tn(hot, table_ref[n]) + dot_tn(hot, table_ref[n + 1]) for n in (0, 2)]


def turn_table():
    lane = np.arange(128)
    rates = 10000.0 ** (-(lane % 16) / 16)
    angle = np.arange(16)[:, None] * rates
    row_lane = (lane % 64) < 32
    out = []
    for v in (np.cos(angle), np.sin(angle) * np.where(lane % 32 < 16, -1.0, 1.0)):
        v = np.concatenate([np.where(row_lane, v, 0.0), np.where(row_lane, 0.0, v)])
        high = v.astype(ml_dtypes.bfloat16)
        out += [high, (v - high.astype(np.float64)).astype(ml_dtypes.bfloat16)]
    return np.stack(out)


def pack_kernel(lat_ref, dy_ref, row_ref, col_ref, lat_out, dy_out):
    other = 2 - 2 * lax.axis_index("band")
    dy_out[...] = dy_ref[...]
    for i in range(2):
        lat_out[i, :128] = lat_ref[i]
        here = pl.ds(other + i, 1)
        line = jnp.concatenate(
            [row_ref[here, :].astype(f32), col_ref[here, :].astype(f32), jnp.zeros((1, 128), f32)],
            axis=1,
        )
        lat_out[i, 128:] = jnp.broadcast_to(line, (16, 384)).astype(bf16)


def split(v):
    hi = v.astype(bf16)
    return jnp.concatenate([hi, (v - hi.astype(f32)).astype(bf16)], axis=0)


def fine_dot(v, w):
    n = v.shape[0]
    out = dot(split(v), w)
    return out[:n] + out[n:]


def silu(v):
    return v / (1.0 + jnp.exp(-v))


def modulation_kernel(
    at_ref, t_ref, l_ref, tw1_ref, tw2_ref, row0_ref, row1_ref, modw_ref, mod_ref, extra_ref
):
    first = 2 * at_ref[0]
    freqs = jnp.exp(lane_iota((1, 128)).astype(f32) * (-math.log(10000.0) / 128))
    spot = lax.broadcasted_iota(jnp.int32, (16, 1), 0)
    steps = jnp.where(
        spot == 0,
        t_ref[first].astype(f32),
        jnp.where(spot == 1, t_ref[first + 1].astype(f32), 0.0),
    )
    angle = steps * freqs
    emb = jnp.concatenate([jnp.cos(angle), jnp.sin(angle)], axis=1)
    hidden = silu(fine_dot(emb, tw1_ref[...]))
    cond = fine_dot(hidden, tw2_ref[...])
    for i, ref in enumerate((row0_ref, row1_ref)):
        label = l_ref[first + i]
        row = jnp.sum(
            jnp.where(spot == (label & 15), ref[...].astype(f32), 0.0), axis=0, keepdims=True
        )
        cond = cond + jnp.where(spot == i, row, 0.0)
    mod = fine_dot(silu(cond), modw_ref[...])
    lane = lane_iota((1, 128))
    codes = jnp.zeros((1, 128), f32)
    for i in range(2):
        label = l_ref[first + i]
        codes = jnp.where(lane == i, (label >> 5).astype(f32), codes)
        codes = jnp.where(lane == 2 + i, (label & 31).astype(f32), codes)
        for k in range(6):
            mod_ref[i, k : k + 1] = mod[i : i + 1, k * 384 : k * 384 + 384]
        for b in range(2):
            extra_ref[1 + i * 2 + b : 2 + i * 2 + b] = emb[i : i + 1, b * 128 : b * 128 + 128]
        for b, p in enumerate(pairs()):
            extra_ref[5 + i * 3 + b : 6 + i * 3 + b] = cond[i : i + 1, p]
    extra_ref[0:1] = codes
    extra_ref[11:] = jnp.zeros((5, 128), f32)


def pairs(width=384):
    return [slice(j, j + 128) for j in range(0, width, 128)]


def forward_kernel(
    at_ref,
    kept_ref,
    got_ref,
    mod_ref,
    w_ref,
    qgain_ref,
    kgain_ref,
    row_ref,
    col_ref,
    table_ref,
    q_ref,
    k_ref,
    v_ref,
    att_ref,
):
    gains = [jnp.concatenate([r[...], r[...]], axis=1) for r in (qgain_ref, kgain_ref)]
    for i in range(2):
        x = both(at_ref, kept_ref, got_ref, i)
        h1 = (x * inv_rms(x) * (1.0 + mod_ref[i, 1:2]) + mod_ref[i, 0:1]).astype(bf16)
        z = dot(h1, w_ref[:, :768])
        v_ref[i] = dot(h1, w_ref[:, 768:]).astype(bf16)
        z = z * lax.rsqrt(head_mean(z * z) + EPS)
        cosine, sine = turns(at_ref, i, row_ref, col_ref, got_ref[i, 128:144], table_ref)
        for p in pairs():
            turned = []
            for part in range(2):
                n = z[:, part * 384 + p.start : part * 384 + p.stop] * gains[part]
                turned.append(n * cosine + partner(n) * sine)
            q = (turned[0].astype(bf16).astype(f32) * 0.125).astype(bf16)
            k = turned[1].astype(bf16)
            q_ref[i, :, p], k_ref[i, :, p] = q, k
            v = v_ref[i, :, p]
            e = jnp.exp(dot_nt(by_head(q), k))
            out = dot(e.astype(bf16), v) / jnp.sum(e, axis=-1, keepdims=True)
            out = jnp.where(lane_iota((1, 128)) < 64, out[:256], out[256:])
            att_ref[i * 256 : i * 256 + 256, p] = out.astype(bf16)


def mlp_kernel(
    at_ref,
    kept_ref,
    got_ref,
    dkept_ref,
    dgot_ref,
    att_ref,
    mod_ref,
    proj_ref,
    wgu_ref,
    wd_ref,
    keep_ref,
    send_ref,
    out_ref,
    outsend_ref,
    dmid_ref,
    sums_ref,
    branch_s,
    mid_s,
    h2_s,
    h2t_s,
    dmlp_s,
    mlp_s,
    dh2_s,
):
    images = range(2)

    def rows(i):
        return slice(i * 256, (i + 1) * 256)

    branch_s[...] = dot(att_ref[...], proj_ref[...])
    for i in images:
        mid = both(at_ref, kept_ref, got_ref, i) + mod_ref[i, 2:3] * branch_s[rows(i)]
        mid_s[rows(i)] = mid
        h2_s[rows(i)] = (mid * inv_rms(mid) * (1.0 + mod_ref[i, 4:5]) + mod_ref[i, 3:4]).astype(
            bf16
        )
        dmlp_s[rows(i)] = (mod_ref[i, 5:6] * both(at_ref, dkept_ref, dgot_ref, i)).astype(bf16)
    h2t_s[...] = h2_s[...].T
    h2 = h2_s[...]
    d_mlp = dmlp_s[...]
    first = True
    for ref, half in ((send_ref, 1 - at_ref[1]), (keep_ref, at_ref[1])):
        for n in range(2):
            base = half * 512 + n * CHUNK
            wg = wgu_ref[:, pl.ds(pl.multiple_of(base, CHUNK), CHUNK)]
            wu = wgu_ref[:, pl.ds(pl.multiple_of(base + 1024, CHUNK), CHUNK)]
            wd = wd_ref[pl.ds(pl.multiple_of(base, CHUNK), CHUNK), :]
            g = dot(h2, wg)
            u = dot(h2, wu)
            d_hid = dot_nt(d_mlp, wd)
            sig = 0.5 * jnp.tanh(0.5 * g) + 0.5
            act = g * sig
            hid = (act * u).astype(bf16)
            du = (d_hid * act).astype(bf16)
            dg = (d_hid * u * (sig + act * (1.0 - sig))).astype(bf16)
            mlp = dot(hid, wd)
            d_h2 = dot_nt(dg, wg) + dot_nt(du, wu)
            mlp_s[...] = mlp if first else mlp_s[...] + mlp
            dh2_s[...] = d_h2 if first else dh2_s[...] + d_h2
            first = False
            for m, d in ((0, dg), (4, du)):
                grad = dot(h2t_s[...], d).astype(bf16)
                for b in range(2):
                    ref[pl.ds((m + 2 * n + b) * 384, 384)] = grad[:, b * 128 : b * 128 + 128]
            down = dot_tn(hid, d_mlp).astype(bf16)
            for b in range(2):
                for c in range(3):
                    ref[pl.ds((8 + 2 * n + b) * 384 + c * 128, 128)] = down[
                        b * 128 : b * 128 + 128, c * 128 : c * 128 + 128
                    ]
    for i in images:
        mid, mlp, dh2 = mid_s[rows(i)], mlp_s[rows(i)], dh2_s[rows(i)]
        dy = both(at_ref, dkept_ref, dgot_ref, i)
        out = (mid + mod_ref[i, 5:6] * mlp).astype(bf16)
        out_ref[2 * at_ref[0] + i] = out[:128]
        outsend_ref[i] = out[128:]
        s = inv_rms(mid)
        n = mid * s
        e2 = dh2 * (1.0 + mod_ref[i, 4:5])
        d_mid = dy + s * (e2 - n * jnp.mean(e2 * n, axis=-1, keepdims=True))
        dmid_ref[rows(i)] = d_mid
        for k, v in enumerate((d_mid * branch_s[rows(i)], dh2, dh2 * n, dy * mlp)):
            total = jnp.sum(v, axis=0, keepdims=True)
            for b, p in enumerate(pairs()):
                sums_ref[pl.ds(i * 12 + k * 3 + b, 1)] = total[:, p]


def backward_kernel(
    at_ref,
    kept_ref,
    got_ref,
    mod_ref,
    w_ref,
    qgain_ref,
    kgain_ref,
    row_ref,
    col_ref,
    table_ref,
    q_ref,
    k_ref,
    v_ref,
    att_ref,
    dmid_ref,
    proj_ref,
    outsend_ref,
    keep_ref,
    send_ref,
    grad_ref,
    swap_ref,
    sums_ref,
    h1_s,
    dqkv_s,
    dbranch_s,
    units_s,
):
    gains = [jnp.concatenate([r[...], r[...]], axis=1) for r in (qgain_ref, kgain_ref)]
    gain_sums = [0.0, 0.0]
    for i in range(2):
        here = slice(i * 256, i * 256 + 256)
        x = both(at_ref, kept_ref, got_ref, i)
        s1 = inv_rms(x)
        n1 = x * s1
        h1 = (n1 * (1.0 + mod_ref[i, 1:2]) + mod_ref[i, 0:1]).astype(bf16)
        h1_s[here] = h1
        d_mid = dmid_ref[here]
        d_branch = (mod_ref[i, 2:3] * d_mid).astype(bf16)
        dbranch_s[here] = d_branch
        d_att = dot_nt(d_branch, proj_ref[...]).astype(bf16)
        z = dot(h1, w_ref[:, :768])
        r = lax.rsqrt(head_mean(z * z) + EPS)
        z = z * r
        cosine, sine = turns(at_ref, i, row_ref, col_ref, got_ref[i, 128:144], table_ref)
        turned = [[], []]
        for p in pairs():
            q, k, v, do = q_ref[i, :, p], k_ref[i, :, p], v_ref[i, :, p], d_att[:, p]
            q2, do2 = by_head(q), by_head(do)
            e = jnp.exp(dot_nt(k, q2))
            soft = e * (1.0 / jnp.sum(e, axis=0, keepdims=True))
            d_probs = dot_nt(v, do2)
            delta = jnp.sum(soft * d_probs, axis=0, keepdims=True)
            ds = (soft * (d_probs - delta)).astype(bf16)
            dq = dot_tn(ds, k)
            dq = jnp.where(lane_iota((1, 128)) < 64, dq[:256], dq[256:])
            dk = dot(ds, q2)
            dv = dot(soft.astype(bf16), do2)
            for part, d in enumerate((dq * 0.125, dk)):
                n = z[:, part * 384 + p.start : part * 384 + p.stop]
                dn = d * cosine - partner(d) * sine
                gain_sums[part] = gain_sums[part] + jnp.sum(dn * n, axis=0, keepdims=True)
                turned[part].append(dn * gains[part])
            dqkv_s[here, 768 + p.start : 768 + p.stop] = dv.astype(bf16)
        e = jnp.concatenate(turned[0] + turned[1], axis=1)
        dqkv_s[here, :768] = (r * (e - z * head_mean(e * z))).astype(bf16)
        d_h1 = dot_nt(dqkv_s[here], w_ref[...])
        e1 = d_h1 * (1.0 + mod_ref[i, 1:2])
        grad = d_mid + s1 * (e1 - n1 * jnp.mean(e1 * n1, axis=-1, keepdims=True))
        grad_ref[2 * at_ref[0] + i] = grad[:128]
        swap_ref[i, 0] = outsend_ref[i]
        swap_ref[i, 1] = grad[128:].astype(bf16)
        for k, v in enumerate((d_h1, d_h1 * n1)):
            total = jnp.sum(v, axis=0, keepdims=True)
            for b, p in enumerate(pairs()):
                sums_ref[pl.ds(i * 6 + k * 3 + b, 1)] = total[:, p]
    gain_sums = [g + pltpu.roll(g, 64, 1) for g in gain_sums]
    sums_ref[pl.ds(12, 1)] = jnp.where(lane_iota((1, 128)) < 64, gain_sums[0], gain_sums[1])
    sums_ref[pl.ds(13, 3)] = jnp.zeros((3, 128), f32)
    h1t = h1_s[...].T
    for part in range(3):
        w = dot(h1t, dqkv_s[:, part * 384 : part * 384 + 384]).astype(bf16)
        for b, p in enumerate(pairs()):
            n = part * 3 + b
            units_s[n // 6, pl.ds(n % 6 * 384, 384)] = w[:, p]
    w = dot_tn(att_ref[...], dbranch_s[...]).astype(bf16)
    for b, p in enumerate(pairs()):
        units_s[1, pl.ds((3 + b) * 384, 384)] = w[:, p]
    keep_ref[...] = units_s[at_ref[1]]
    send_ref[...] = units_s[1 - at_ref[1]]


def whole_spec(shape):
    return pl.BlockSpec(shape, lambda *_: (0,) * len(shape))


def params(mib):
    return pltpu.CompilerParams(vmem_limit_bytes=mib * MIB)


def shape_of(shape, dtype):
    return jax.ShapeDtypeStruct(shape, dtype)


SCALARS = pl.BlockSpec(memory_space=pltpu.SMEM)
RESIDENT = pl.BlockSpec(memory_space=pltpu.VMEM)
IN_HBM = pl.BlockSpec(memory_space=pltpu.HBM)


def cost(flops, nbytes):
    return pl.CostEstimate(flops=flops, bytes_accessed=nbytes, transcendentals=0)


def pack_call(latents, out_grad, pos_row, pos_col):
    theirs = pl.BlockSpec((2, 128, 384), lambda j: (1 - lax.axis_index("band"), 0, 0))
    shapes = [(2, 144, 384), (2, 128, 384)]
    return pl.pallas_call(
        pack_kernel,
        grid=(1,),
        in_specs=[theirs, theirs, whole_spec((4, 128)), whole_spec((4, 128))],
        out_specs=[RESIDENT] * 2,
        out_shape=[shape_of(s, bf16) for s in shapes],
        compiler_params=params(56),
        cost_estimate=cost(200_000, 800_000),
        name="pack_swaps",
    )(latents, out_grad, pos_row, pos_col)


def modulation_call(at, timesteps, labels, t_w1, t_w2, label_table, mod_w):
    def row_spec(i):
        return pl.BlockSpec((16, 384), lambda j, at, t, l: (l[2 * at[0] + i] >> 4, 0))

    shapes = [(2, 6, 384), (16, 128)]
    return pl.pallas_call(
        modulation_kernel,
        grid_spec=pltpu.PrefetchScalarGridSpec(
            num_scalar_prefetch=3,
            grid=(1,),
            in_specs=[
                whole_spec((256, 384)),
                whole_spec((384, 384)),
                row_spec(0),
                row_spec(1),
                whole_spec((384, 2304)),
            ],
            out_specs=[RESIDENT] * 2,
        ),
        out_shape=[shape_of(s, f32) for s in shapes],
        compiler_params=params(56),
        cost_estimate=cost(1_000_000_000, 3_000_000),
        name="modulation",
    )(at, timesteps, labels, t_w1, t_w2, label_table, label_table, mod_w)


def resident_call(kernel, name, outs, estimate, mib, scratch=(), loose=(), loose_out=()):
    def spec(is_loose, shape):
        return whole_spec(shape) if is_loose else RESIDENT

    def call(at, *arrays):
        return pl.pallas_call(
            kernel,
            grid=(1,),
            in_specs=[SCALARS] + [spec(n in loose, a.shape) for n, a in enumerate(arrays)],
            out_specs=[spec(n in loose_out, o[0]) for n, o in enumerate(outs)],
            out_shape=[shape_of(*o) for o in outs],
            scratch_shapes=[pltpu.VMEM(*o) for o in scratch],
            compiler_params=params(mib),
            cost_estimate=estimate,
            name=name,
        )(at, *arrays)

    return call


def relay_kernel(mod_ref, out_ref):
    out_ref[...] = mod_ref[...]


def relay_call(mod):
    return pl.pallas_call(
        relay_kernel,
        in_specs=[RESIDENT],
        out_specs=RESIDENT,
        out_shape=shape_of((2, 6, 384), f32),
        compiler_params=params(2),
        cost_estimate=cost(1_000, 40_000),
        name="relay_modulation",
    )(mod)


forward_call = resident_call(
    forward_kernel,
    "attention_forward",
    [((2, 256, 384), bf16)] * 3 + [((512, 384), bf16)],
    cost(3_000_000_000, 4_000_000),
    12,
    loose_out=range(4),
)
mlp_call = resident_call(
    mlp_kernel,
    "mlp_both_ways",
    [
        ((4608, 128), bf16),
        ((4608, 128), bf16),
        ((4, 128, 384), bf16),
        ((2, 128, 384), bf16),
        ((512, 384), f32),
        ((24, 128), f32),
    ],
    cost(6_000_000_000, 8_000_000),
    24,
    [
        ((512, 384), f32),
        ((512, 384), f32),
        ((512, 384), bf16),
        ((384, 512), bf16),
        ((512, 384), bf16),
        ((512, 384), f32),
        ((512, 384), f32),
    ],
    loose=(4,),
    loose_out=(2, 3, 4, 5),
)
backward_call = resident_call(
    backward_kernel,
    "attention_backward",
    [
        ((2304, 128), bf16),
        ((2304, 128), bf16),
        ((4, 128, 384), f32),
        ((2, 2, 128, 384), bf16),
        ((16, 128), f32),
    ],
    cost(5_000_000_000, 6_000_000),
    24,
    [((512, 384), bf16), ((512, 1152), bf16), ((512, 384), bf16), ((2, 2304, 128), bf16)],
    loose=range(9, 16),
    loose_out=(2, 3, 4),
)


def join_kernel(
    a_ref, a_got_ref, b_ref, b_got_ref, sums1_ref, sums2_ref, extra_ref, out_ref, lines
):
    lines[:24] = sums1_ref[...]
    lines[24:40] = sums2_ref[...]
    lines[37:48] = extra_ref[:11]
    out_ref[:, :288] = (a_ref[...].astype(f32) + a_got_ref[...].astype(f32)).astype(bf16)
    out_ref[:, 288:432] = (b_ref[...].astype(f32) + b_got_ref[...].astype(f32)).astype(bf16)
    out_ref[:, 432:] = jnp.broadcast_to(lines[...].astype(bf16)[None], (16, 48, 128))


def join_call(keep1, got1, keep2, got2, *lines):
    big, small = (16, 288, 128), (16, 144, 128)
    return pl.pallas_call(
        join_kernel,
        out_shape=shape_of((16, 480, 128), bf16),
        scratch_shapes=[pltpu.VMEM((48, 128), f32)],
        compiler_params=params(14),
        cost_estimate=cost(2_000_000, 6_000_000),
        name="join_messages",
    )(keep1.reshape(big), got1.reshape(big), keep2.reshape(small), got2.reshape(small), *lines)


def extra_kernel(a_ref, out_ref):
    out_ref[...] = a_ref[:, 432:]


def extra_call(a):
    return pl.pallas_call(
        extra_kernel,
        in_specs=[RESIDENT],
        out_specs=RESIDENT,
        out_shape=shape_of((16, 48, 128), bf16),
        compiler_params=params(4),
        cost_estimate=cost(1_000, 200_000),
        name="extra_rows",
    )(a)


def sum_kernel(at_ref, a_ref, keep_ref, send_ref, total_s):
    total = a_ref[0, :432].astype(f32)
    for n in range(1, 16):
        total = total + a_ref[n, :432].astype(f32)
    total = total.astype(bf16)
    total_s[0] = total[:224]
    total_s[1, :208] = total[224:]
    total_s[1, 208:] = jnp.zeros((16, 128), bf16)
    keep_ref[...] = total_s[at_ref[2]]
    send_ref[...] = total_s[1 - at_ref[2]]


def sum_call(at, a):
    return pl.pallas_call(
        sum_kernel,
        in_specs=[SCALARS, RESIDENT],
        out_specs=[RESIDENT] * 2,
        out_shape=[shape_of((224, 128), bf16)] * 2,
        scratch_shapes=[pltpu.VMEM((2, 224, 128), bf16)],
        compiler_params=params(14),
        cost_estimate=cost(2_000_000, 3_000_000),
        name="sum_layer",
    )(at, a)


def pick_lines(rows_ref, rows_s, here, dmod_ref, cond_ref, emb_ref, codes_ref, gains_ref):
    for n in range(8):
        rows_s[pl.ds(n * 768, 768)] = rows_ref[pl.ds(n * 768, 768)].astype(f32)

    def line(r):
        return rows_s[pl.ds(r, 128, stride=48), :]

    for i in range(2):
        spot = pl.ds(pl.multiple_of(here + i * 128, 128), 128)
        for k in range(6):
            for b in range(3):
                r = 24 + i * 6 + k * 3 + b if k < 2 else i * 12 + (k - 2) * 3 + b
                at = k * 384 + b * 128
                dmod_ref[spot, at : at + 128] = line(r).astype(bf16)
        for b in range(2):
            emb_ref[spot, b * 128 : b * 128 + 128] = line(38 + i * 2 + b).astype(bf16)
        for b in range(3):
            cond_ref[spot, b * 128 : b * 128 + 128] = line(42 + i * 3 + b)
        codes = line(37)
        label = codes[:, i : i + 1] * 32.0 + codes[:, i + 2 : i + 3]
        codes_ref[spot, :] = jnp.broadcast_to(label, (128, 128)).astype(jnp.int32)
    gains_ref[...] = jnp.sum(line(36), axis=0, keepdims=True)


def lines(rows):
    return [
        ((rows, 2304), bf16),
        ((rows, 384), f32),
        ((rows, 256), bf16),
        ((rows, 128), jnp.int32),
    ]


GAINS = ((1, 128), f32)


def line_kernel(rows_ref, modw_ref, *refs):
    outs, rows_s = refs[:5], refs[5]
    pick_lines(rows_ref, rows_s, 0, *outs)


def line_call(rows, mod_w):
    return pl.pallas_call(
        line_kernel,
        in_specs=[RESIDENT] * 2,
        out_shape=[shape_of(*o) for o in lines(256) + [GAINS]],
        scratch_shapes=[pltpu.VMEM((6144, 128), f32)],
        compiler_params=params(14),
        cost_estimate=cost(100_000, 100_000),
        name="image_lines",
    )(rows, mod_w)


CONDITIONS = [(256, 384), (384, 384), (1001, 384), (384, 2304), (1, 64), (1, 64)]


def condition_kernel(at_ref, *refs):
    own, got_ref, (tw1_ref, tw2_ref, modw_ref) = refs[:5], refs[5], refs[6:9]
    stages = refs[9:15]
    whole, gains_s, rows_s = refs[15:19], refs[19], refs[20]
    tw1g, tw2g, tableg, modwg, qgain, kgain = stages
    mine = pl.ds(pl.multiple_of(at_ref[1] * 256, 256), 256)
    for ref, own_ref in zip(whole, own):
        ref[mine, :] = own_ref[...]
    pick_lines(got_ref, rows_s, (1 - at_ref[1]) * 256, *whole, gains_s)
    dmod_s, cond_s, emb_s, label_s = whole
    gain_sums = own[4][...] + gains_s[...]
    qgain[...], kgain[...] = gain_sums[:, :64], gain_sums[:, 64:]
    cond = cond_s[...]
    sig = 1.0 / (1.0 + jnp.exp(-cond))
    act_t = (cond * sig).astype(bf16).T
    for k in range(6):
        cols = slice(k * 384, k * 384 + 384)
        modwg[:, cols] = dot(act_t, dmod_s[:, cols])
    d_cond = dot_nt(dmod_s[...], modw_ref[...]) * (sig + cond * sig * (1.0 - sig))
    dc = d_cond.astype(bf16)
    label = label_s[...]
    label = jnp.concatenate([label, label], axis=1)
    for n in range(4):
        hot = jnp.where(lane_iota((512, 256)) + n * 256 == label, 1.0, 0.0).astype(bf16)
        rows = dot_tn(hot, dc)
        top = min(256, 1001 - n * 256)
        tableg[n * 256 : n * 256 + top] = rows[:top]
    emb = emb_s[...]
    pre = dot(emb, tw1_ref[...])
    sig = 1.0 / (1.0 + jnp.exp(-pre))
    hid = pre * sig
    tw2g[...] = dot_tn(hid.astype(bf16), dc)
    d_pre = (dot_nt(dc, tw2_ref[...]) * (sig + hid * (1.0 - sig))).astype(bf16)
    tw1g[...] = dot_tn(emb, d_pre)


def condition_call(at, own, got, t_w1, t_w2, mod_w):
    return pl.pallas_call(
        condition_kernel,
        grid=(1,),
        in_specs=[SCALARS] + [RESIDENT] * 9,
        out_specs=[whole_spec(v) for v in CONDITIONS],
        out_shape=[shape_of(s, f32) for s in CONDITIONS],
        scratch_shapes=[pltpu.VMEM(*o) for o in lines(512) + [GAINS, ((6144, 128), f32)]],
        compiler_params=params(36),
        cost_estimate=cost(100_000_000, 100_000),
        name="condition_gradients",
    )(at, *own, got, t_w1, t_w2, mod_w)


def place_kernel(at_ref, swaps_ref, out_in, grad_in, out_ref, grad_ref):
    out_ref[...] = swaps_ref[:, 0]
    grad_ref[...] = swaps_ref[:, 1].astype(f32)


def place_call(at, swaps, block_out, latents_grad):
    anywhere = pl.BlockSpec(memory_space=pl.ANY)
    theirs = pl.BlockSpec((2, 128, 384), lambda j, at: (1 - at[0], 0, 0))
    return pl.pallas_call(
        place_kernel,
        grid_spec=pltpu.PrefetchScalarGridSpec(
            num_scalar_prefetch=1,
            grid=(1,),
            in_specs=[whole_spec((2, 2, 128, 384)), anywhere, anywhere],
            out_specs=[theirs, theirs],
        ),
        out_shape=[shape_of((4, 128, 384), bf16), shape_of((4, 128, 384), f32)],
        input_output_aliases={2: 0, 3: 1},
        compiler_params=params(8),
        cost_estimate=cost(200_000, 1_500_000),
        name="place_swaps",
    )(at, swaps, block_out, latents_grad)


def cuts(start, chunk):
    out, at = [], start
    while at < start + 384:
        n = at // chunk
        stop = min((n + 1) * chunk, start + 384)
        out.append((n, at - n * chunk, stop - n * chunk))
        at = stop
    return out


def unpack_kernel(own, at_ref, sums_ref, *refs):
    qkv_ref, proj_ref, gu_ref, down_ref, proj_s, sem = refs[-6:]
    t = pl.program_id(0)
    half = at_ref[1] if own else 1 - at_ref[1]

    def piece(n, a, b):
        low = [sums_ref[n, a : min(b, 224)]] if a < 224 else []
        return low + ([sums_ref[16 + n, max(a, 224) - 224 : b - 224]] if b > 224 else [])

    def first(u):
        rows = [v for n, a, b in cuts(u * 384, 288) for v in piece(n, a, b)]
        return jnp.concatenate(rows).astype(f32)

    def second(u):
        rows = [v for n, a, b in cuts(u * 384, 144) for v in piece(n, 288 + a, 288 + b)]
        return jnp.concatenate(rows).astype(f32)

    proj_copy = pltpu.make_async_copy(proj_s, proj_ref, sem)
    for n in range(2):

        @pl.when(t == n)
        def _():
            for b in range(4):
                gu_ref[:, b * 128 : b * 128 + 128] = first(4 * n + b)
            for m in range(2):
                rows = first(8 + 2 * n + m)
                for b, p in enumerate(pairs()):
                    down_ref[m * 128 : m * 128 + 128, p] = rows[b * 128 : b * 128 + 128]

    @pl.when((t == 0) & (half == 1))
    def _():
        for b, p in enumerate(pairs()):
            proj_s[:, p] = second(3 + b)
        proj_copy.start()

    @pl.when(t == 0)
    def _():
        for b, p in enumerate(pairs()):
            qkv_ref[:, p] = second(b)

    @pl.when((t == 1) & (half == 0))
    def _():
        for b, p in enumerate(pairs()):
            qkv_ref[:, p] = second(3 + b)

    @pl.when((t == 1) & (half == 1))
    def _():
        proj_copy.wait()


def unpack_call(own, at, sums, earlier=()):
    def half_of(at):
        return at[1] if own else 1 - at[1]

    shapes = [(384, 1152), (384, 384), (384, 2048), (1024, 384)]
    return pl.pallas_call(
        lambda *refs: unpack_kernel(own, *refs),
        grid_spec=pltpu.PrefetchScalarGridSpec(
            num_scalar_prefetch=1,
            grid=(2,),
            in_specs=[RESIDENT] + [pl.BlockSpec(memory_space=pl.ANY)] * len(earlier),
            out_specs=[
                pl.BlockSpec(
                    (384, 384), lambda t, at: (0, half_of(at) * 2 + (1 - half_of(at)) * t)
                ),
                IN_HBM,
                pl.BlockSpec((384, 512), lambda t, at: (0, 2 * t + half_of(at))),
                pl.BlockSpec((256, 384), lambda t, at: (2 * half_of(at) + t, 0)),
            ],
            scratch_shapes=[pltpu.VMEM((384, 384), f32), pltpu.SemaphoreType.DMA],
        ),
        out_shape=[shape_of(s, f32) for s in shapes],
        input_output_aliases={2 + n: n for n in range(len(earlier))},
        compiler_params=params(20),
        cost_estimate=cost(2_000_000, 6_000_000),
        name="unpack_own" if own else "unpack_other",
    )(at, sums, *earlier)


def flat(y, z, x, c):
    return ((((y * 8 + z) * 2 + x % 2) * 2 + c) * 2) + x // 2


PLACES = [(y, z, x, c) for z, y, x, c in itertools.product(range(8), range(4), range(4), range(2))]


def groups(key):
    found = {}
    for place in PLACES:
        found.setdefault(key(*place), []).append(flat(*place))
    return list(found.values())


PLANE = groups(lambda y, z, x, c: (z // 2, c))
LAYER = groups(lambda y, z, x, c: (z, c))
RING = groups(lambda y, z, x, c: (y, x, c))


def moves(to):
    return [(flat(*place), flat(*to(*place))) for place in PLACES]


def exchange(v, lists):
    return lax.all_to_all(v, AXES, 0, 0, tiled=True, axis_index_groups=lists)


def plus(a, b):
    return (a.astype(f32) + b.astype(f32)).astype(bf16)


def column_sum(keep, send):
    v = plus(keep, lax.ppermute(send, AXES, moves(lambda y, z, x, c: (y, z ^ 1, x, c))))
    for to in (
        lambda y, z, x, c: (y, z ^ 2, x, c),
        lambda y, z, x, c: (y, (6 - (z & 6)) + (z & 1), x, c),
    ):
        v = plus(v, lax.ppermute(v, AXES, moves(to)))
    return v


BAND_SWAP = [(n, n ^ 1) for n in range(256)]
CORE_SWAP = [(n, n ^ 2) for n in range(256)]


def swap(v):
    return lax.ppermute(v, AXES, BAND_SWAP)


def core_swap(v):
    return lax.ppermute(v, AXES, CORE_SWAP)


def body(
    latents,
    pos_row,
    pos_col,
    timesteps,
    labels,
    t_w1,
    t_w2,
    label_table,
    mod_w,
    qkv_w,
    q_gain,
    k_gain,
    proj_w,
    gate_up_w,
    down_w,
    out_grad,
):
    band, img = lax.axis_index("band"), lax.axis_index("img")
    at = jnp.stack([band, img % 2, img // 4 % 2]).astype(jnp.int32)
    send, dsend = pack_call(latents, out_grad, pos_row, pos_col)
    got, dgot = swap(send), swap(dsend)
    mod, extra = modulation_call(at, timesteps, labels, t_w1, t_w2, label_table, mod_w)
    mod = relay_call(mod)
    turn = (q_gain.reshape(1, 64), k_gain.reshape(1, 64), pos_row, pos_col, turn_table())
    q, k, v, att = forward_call(at, latents, got, mod, qkv_w, *turn)
    keep1, send1, block_out, out_send, d_mid, sums1 = mlp_call(
        at, latents, got, out_grad, dgot, att, mod, proj_w, gate_up_w, down_w
    )
    got1 = core_swap(send1)
    keep2, send2, latents_grad, swaps, sums2 = backward_call(
        at, latents, got, mod, qkv_w, *turn, q, k, v, att, d_mid, proj_w, out_send
    )
    joined = join_call(keep1, got1, keep2, core_swap(send2), sums1, sums2, extra)
    joined = exchange(joined, LAYER)
    joined, extra = lax.optimization_barrier((joined, extra_call(joined)))
    keep, send = sum_call(at, joined)
    extra = lax.all_gather(
        extra.reshape(768, 128), AXES, axis=0, tiled=True, axis_index_groups=RING
    )
    chunk = column_sum(keep, send)
    chunk, swaps = lax.optimization_barrier((chunk, swap(swaps)))
    wide = lax.optimization_barrier(jnp.broadcast_to(chunk[None], (32, 224, 128)))
    summed = exchange(wide, PLANE)
    block_out, latents_grad = place_call(at, swaps, block_out, latents_grad)
    extra, block_out, latents_grad, _ = lax.optimization_barrier(
        (extra, block_out, latents_grad, wide)
    )
    conditioned = condition_call(at, line_call(extra, mod_w), core_swap(extra), t_w1, t_w2, mod_w)
    summed, conditioned = lax.optimization_barrier((summed, conditioned))
    tw1_grad, tw2_grad, table_grad, modw_grad, q_sum, k_sum = conditioned
    sums = unpack_call(True, at, summed)
    qkv_sum, proj_sum, gu_sum, down_sum = unpack_call(False, at, core_swap(summed), sums)
    return (
        block_out,
        latents_grad,
        tw1_grad,
        tw2_grad,
        table_grad,
        modw_grad,
        qkv_sum,
        q_sum.reshape(64),
        k_sum.reshape(64),
        proj_sum,
        gu_sum,
        down_sum,
    )


def solution(mesh):
    split = P("img", "band", None)
    return jax.shard_map(
        body,
        mesh=mesh,
        in_specs=(split, P("img", "band"), P("img", "band"), P("img"), P("img"))
        + (P(),) * 10
        + (split,),
        out_specs=(split, split) + (P(),) * 10,
        check_vma=False,
    )
```
